128 devices in a mesh: dp: 32 (over x, y, core), mp: 4 (over z).
Axes of the slice: x: 4, y: 4, z: 4, core: 2. Of those that a mesh axis runs over, the one named last changes fastest.
Arguments:
- frames: bfloat16 [49152, 1536], P('dp'), may hold values from -6 to 6
- grad_out: bfloat16 [49152, 1536], P('dp'), may hold values from -6 to 6
- w_in: bfloat16 [1536, 2, 1536], P(None, None, 'mp'), may hold values from -0.15625 to 0.15625
- conv_kernel: float32 [31, 1536], P(None, 'mp'), may hold values from -1 to 1
- conv_bias: float32 [1536], P('mp'), may hold values from -3 to 3
- w_out: bfloat16 [1536, 1536], P('mp'), may hold values from -0.15625 to 0.15625
- seg_lengths: int32 [32, 32], P('dp'), may hold values from 24 to 72, as said below
- seg_owner: int32 [32, 32], P('dp'), may hold values from 0 to 31, as said below
- slot_device: int32 [32, 32], P('dp'), may hold values from 0 to 31, as said below
Outputs:
- dx_frames: bfloat16 [1024, 72, 1536], P('dp', None, 'mp')
- grad_w_in: float32 [1536, 2, 1536], P('dp', None, 'mp')
- grad_w_out: float32 [1536, 1536], P('mp', 'dp')
- grad_kernel: float32 [31, 1536], P(None, 'mp')
- grad_bias: float32 [1536], P('mp')
The draws below stay inside these ranges and needn't reach their ends.
Inputs may be any that keep to these rules, and one draw needn't show every extreme that they name: `seg_lengths`: each row sums to 1536, and every row holds at least one length 72. `seg_owner`: each row is a permutation: every pack holds exactly one utterance of each owner. `slot_device`: each row is a permutation: owner o's utterance u is packed on pack slot_device[o, u].
All inputs are finite; a program needn't handle non-finite values.
Results may differ from the reference program's by a relative error of at most 0.0049.
Values may be sent and summed in bfloat16 or wider, within the bound.
No kernel may reach another device: no remote copies, remote signals or barrier semaphores. Data moves between devices by JAX's collectives and lax.ppermute only.
A program may use at most 128 MiB of HBM per device.

```python
import math
import jax
import jax.numpy as jnp
from jax import lax

D = 1536
TAPS = 31
MEAN = 48
MAXLEN = 72
ROWS_DEV = 1536
ROWS = 49152
UTTS = 1024
N_DP = 32


def draw_seg_lengths(key, part):
    key = jax.random.fold_in(key, 11)
    first, second = jax.random.split(key)
    half = MEAN // 2
    spread = jax.random.randint(first, (N_DP, N_DP // 2), 0, half + 1)
    spread = spread.at[:, 0].set(half)
    paired = jnp.concatenate([MEAN + spread, MEAN - spread], axis=1)
    order = jax.vmap(lambda subkey: jax.random.permutation(subkey, N_DP))(jax.random.split(second, N_DP))
    return jnp.take_along_axis(paired, order, axis=1).astype(jnp.int32)


def draw_seg_owner(key, part):
    key = jax.random.fold_in(key, 23)
    return jax.vmap(lambda subkey: jax.random.permutation(subkey, N_DP))(jax.random.split(key, N_DP)).astype(jnp.int32)


def draw_slot_device(key, part):
    key = jax.random.fold_in(key, 37)
    return jax.vmap(lambda subkey: jax.random.permutation(subkey, N_DP))(jax.random.split(key, N_DP)).astype(jnp.int32)


def strengthened(values, stream_key, source, target, parts, factor):
    owner, partner = [(jnp.arange(values.shape[dim]) // (values.shape[dim] // parts)).reshape([-1 if axis == dim else 1 for axis in range(values.ndim)]) for dim in (source, target)]
    chosen = jax.random.permutation(stream_key, parts)[partner]
    strong = (owner == chosen) | (owner == (partner + parts // 2) % parts)
    return jnp.where(strong, factor * values, values)


def block_scale(key, shape, cuts, least, high):
    factor_of = 1.0
    for dim, shards_of in cuts:
        steps = jax.random.uniform(jax.random.fold_in(jax.random.fold_in(key, 6), dim), (shards_of,), jnp.float32, least / len(cuts), high / len(cuts))
        factor_of = factor_of * jnp.repeat(jnp.exp(steps), shape[dim] // shards_of).reshape((-1,) + (1,) * (len(shape) - 1 - dim))
    return factor_of


def noise(rng, dims, scale, most, pieces=(), kind=jnp.bfloat16):
    level = block_scale(rng, dims, pieces, -0.22, 0.18) if pieces else 1.0
    array = jax.random.normal(rng, dims, jnp.float32) * scale * level
    return jnp.minimum(jnp.maximum(array, -most), most).astype(kind)


def noise_with(own_key, shape, scale, bound, cuts, heavy, held_as=jnp.bfloat16):
    entries = scale * jax.random.normal(own_key, shape, jnp.float32)
    if cuts:
        entries = entries * block_scale(own_key, shape, cuts, -0.22, 0.18)
    return jnp.clip(strengthened(entries, jax.random.fold_in(own_key, 3), *heavy), -bound, bound).astype(held_as)


def setup_inputs(seed: int = 0) -> dict:
    arg_keys = jax.random.split(jax.random.key(seed), 10)
    return {
        "frames": noise_with(arg_keys[0], (ROWS, D), 1.0, 6.0, ((0, 32),), (0, 1, 32, 2.75)),
        "grad_out": noise_with(arg_keys[1], (ROWS, D), 1.0, 6.0, ((0, 32),), (0, 1, 32, 2.75)),
        "w_in": noise(arg_keys[2], (D, 2, D), D ** -0.5, 0.15625, ((2, 4),)),
        "conv_kernel": noise(arg_keys[3], (TAPS, D), TAPS ** -0.5, 1.0, ((1, 4),), jnp.float32),
        "conv_bias": noise(arg_keys[4], (D,), 0.5, 3.0, ((0, 4),), jnp.float32),
        "w_out": noise(arg_keys[5], (D, D), D ** -0.5, 0.15625, ((0, 4),)),
        "seg_lengths": draw_seg_lengths(jax.random.fold_in(arg_keys[9], 71), 0),
        "seg_owner": draw_seg_owner(jax.random.fold_in(arg_keys[9], 71), 0),
        "slot_device": draw_slot_device(jax.random.fold_in(arg_keys[9], 71), 0),
    }


def segment_ids(lengths, rows):
    seg_ends = jnp.cumsum(lengths).astype(jnp.int32)
    position = jnp.arange(rows, dtype=jnp.int32)
    return lax.optimization_barrier(jnp.sum((position[:, None] >= seg_ends[None, :]).astype(jnp.int32), axis=1))

def padded_pair(signal, segment):
    reach = (TAPS - 1) // 2
    padded = jnp.pad(signal, ((reach, reach), (0, 0)))
    padded_segment = jnp.pad(segment, (reach, reach), constant_values=-1)
    return (padded, padded_segment)

def shifted(padded, padded_segment, segment, offset):
    reach = (TAPS - 1) // 2
    rows = segment.shape[0]
    piece = padded[reach + offset:reach + offset + rows]
    keep = padded_segment[reach + offset:reach + offset + rows] == segment
    return jnp.where(keep[:, None], piece, jnp.zeros((), piece.dtype))

def depthwise(signal, segment, kernel, direction):
    reach = (TAPS - 1) // 2
    padded, padded_segment = padded_pair(signal, segment)
    total = jnp.zeros_like(signal)
    for tap_index in range(TAPS):
        total = total + kernel[tap_index] * shifted(padded, padded_segment, segment, direction * (tap_index - reach))
    return total

def kernel_terms(grad_conv, gated, segment):
    reach = (TAPS - 1) // 2
    padded, padded_segment = padded_pair(gated, segment)
    terms = []
    for tap_index in range(TAPS):
        terms.append(lax.optimization_barrier(jnp.sum(grad_conv * shifted(padded, padded_segment, segment, tap_index - reach), axis=0)))
    return jnp.stack(terms)

def pack_backward(frame_block, grad_block, lengths, w_flat, conv_kernel, conv_bias, w_out):
    width = w_out.shape[0]
    segment = segment_ids(lengths, frame_block.shape[0])
    projected = jnp.dot(frame_block, w_flat, preferred_element_type=jnp.float32)
    value = projected[:, :width]
    gate = projected[:, width:]
    gate_sig = jax.nn.sigmoid(gate)
    gated = value * gate_sig
    conv_out = depthwise(gated, segment, conv_kernel, 1) + conv_bias
    conv_sig = jax.nn.sigmoid(conv_out)
    activated = (conv_out * conv_sig).astype(jnp.bfloat16)
    grad_swish = jnp.dot(grad_block, w_out.T, preferred_element_type=jnp.float32)
    grad_conv = grad_swish * conv_sig * (1.0 + conv_out * (1.0 - conv_sig))
    grad_glu = depthwise(grad_conv, segment, conv_kernel, -1)
    grad_proj = jnp.concatenate([grad_glu * gate_sig, grad_glu * value * gate_sig * (1.0 - gate_sig)], axis=1).astype(jnp.bfloat16)
    grad_rows = jnp.dot(grad_proj, w_flat.T, preferred_element_type=jnp.float32).astype(jnp.bfloat16)
    w_in_term = jnp.dot(frame_block.T, grad_proj, preferred_element_type=jnp.float32)
    w_out_term = jnp.dot(activated.T, grad_block, preferred_element_type=jnp.float32)
    kernel_term = kernel_terms(grad_conv, gated, segment)
    bias_term = lax.optimization_barrier(jnp.sum(grad_conv, axis=0))
    return (grad_rows, (w_in_term, w_out_term, kernel_term, bias_term))

def reference(frames, grad_out, w_in, conv_kernel, conv_bias, w_out, seg_lengths, seg_owner, slot_device):
    w_flat = w_in.reshape(D, 2 * D)

    def step(totals, inputs):
        frame_block, grad_block, lengths = inputs
        grad_rows, terms = pack_backward(frame_block, grad_block, lengths, w_flat, conv_kernel, conv_bias, w_out)
        totals = tuple((left + right for left, right in zip(totals, terms)))
        return (totals, grad_rows)
    start_totals = (jnp.zeros((D, 2 * D), jnp.float32), jnp.zeros((D, D), jnp.float32), jnp.zeros((TAPS, D), jnp.float32), jnp.zeros((D,), jnp.float32))
    totals, grad_rows = lax.scan(step, start_totals, (frames.reshape(N_DP, ROWS_DEV, D), grad_out.reshape(N_DP, ROWS_DEV, D), seg_lengths))
    scale = 1.0 / math.sqrt(ROWS)
    grad_w_in = (totals[0] * scale).reshape(D, 2, D)
    grad_w_out = totals[1] * scale
    grad_kernel = totals[2] * scale
    grad_bias = totals[3] * scale
    owners = jnp.arange(N_DP, dtype=jnp.int32)
    starts = jnp.cumsum(seg_lengths, axis=1).astype(jnp.int32) - seg_lengths
    match = (seg_owner[:, :, None] == owners[None, None, :]).astype(jnp.int32)
    owner_start = lax.optimization_barrier(jnp.sum(match * starts[:, :, None], axis=1))
    owner_length = lax.optimization_barrier(jnp.sum(match * seg_lengths[:, :, None], axis=1))
    start_slot = owner_start[slot_device, owners[:, None]]
    length_slot = owner_length[slot_device, owners[:, None]]
    offsets = jnp.arange(MAXLEN, dtype=jnp.int32)
    row_index = slot_device[:, :, None] * ROWS_DEV + start_slot[:, :, None] + offsets[None, None, :]
    valid = offsets[None, None, :] < length_slot[:, :, None]
    flat = grad_rows.reshape(ROWS, D)
    picked = jnp.take(flat, jnp.where(valid, row_index, 0).reshape(-1).astype(jnp.int32), axis=0).reshape(UTTS, MAXLEN, D)
    dx_frames = jnp.where(valid.reshape(UTTS, MAXLEN, 1), picked, jnp.zeros((), picked.dtype))
    return (dx_frames, grad_w_in, grad_w_out, grad_kernel, grad_bias)
```

```python
import math
import numpy as np
import jax, jax.numpy as jnp
from jax import lax
from jax.sharding import PartitionSpec as P
from jax.experimental import pallas as pl
from jax.experimental.pallas import tpu as pltpu

TAPS = 31
MAXLEN = 72
REACH = 15
WIN = 80
POINTS = 95
HALF = 48
FREQ = 2 * HALF
SEGS = 32
BLOCK = 256


def tables():
    f = np.arange(HALF)[:, None].astype(np.float64)
    w = np.where(f == 0, 1.0 / POINTS, 2.0 / POINTS)
    r = np.arange(WIN)[None, :]
    ang = 2 * np.pi * ((f * r) % POINTS) / POINTS
    fwd = np.concatenate([np.cos(ang), np.sin(ang)], 0)
    inv = np.concatenate([w * np.cos(ang), w * np.sin(ang)], 0).T
    t = np.arange(TAPS + 1)[None, :] - REACH
    tang = 2 * np.pi * ((f * t) % POINTS) / POINTS
    taps = np.concatenate([np.cos(tang), np.sin(tang)], 0)
    back = np.concatenate([w * np.cos(tang), -w * np.sin(tang)], 0).T
    taps[:, TAPS:] = 0
    back[TAPS:] = 0
    def split(table):
        high = table.astype(jnp.bfloat16).astype(np.float32)
        low = (table - high).astype(jnp.bfloat16).astype(np.float32)
        return np.concatenate([high, low, high], 1)

    return (
        jnp.asarray(split(fwd), jnp.float32),
        jnp.asarray(split(inv), jnp.bfloat16),
        jnp.asarray(taps, jnp.float32),
        jnp.asarray(back, jnp.float32),
    )


def pack_kernel(
    len_ref, frames_hbm, gout_hbm, w_ref, wout_ref, taps_ref, bias_ref,
    fwd_ref, inv_ref, tap_table_ref, back_table_ref,
    gp_ref, act_ref, kb_ref,
    fr, go, gsig, gated, gsw, conv, gc, spec, kf, acc, f_sem, g_sem,
):
    rows = frames_hbm.shape[0]
    ch = wout_ref.shape[0]
    blocks = rows // BLOCK

    def copy(hbm, vmem, sem, i):
        at = pl.ds(pl.multiple_of(i * BLOCK, BLOCK), BLOCK)
        return pltpu.make_async_copy(hbm.at[at], vmem.at[at], sem.at[i])

    for i in range(blocks):
        copy(frames_hbm, fr, f_sem, i).start()
        copy(gout_hbm, go, g_sem, i).start()

    tail = pl.ds(rows, WIN)
    gated[tail, :] = jnp.zeros((WIN, ch), jnp.float32)
    gc[tail, :] = jnp.zeros((WIN, ch), jnp.float32)
    kf[...] = jnp.dot(
        tap_table_ref[...], taps_ref[...],
        precision=lax.Precision.HIGHEST, preferred_element_type=jnp.float32,
    )
    acc[...] = jnp.zeros_like(acc)

    def project(i, carry):
        at = pl.ds(pl.multiple_of(i * BLOCK, BLOCK), BLOCK)
        copy(frames_hbm, fr, f_sem, i).wait()
        both = jnp.dot(fr[at, :], w_ref[...], preferred_element_type=jnp.float32)
        sig = jax.nn.sigmoid(both[:, ch:])
        g = both[:, :ch] * sig
        gsig[at, :] = sig
        gated[at, :] = g
        copy(gout_hbm, go, g_sem, i).wait()
        gsw[at, :] = lax.dot_general(
            go[at, :], wout_ref[...], (((1,), (1,)), ((), ())), preferred_element_type=jnp.float32
        )
        return carry

    lax.fori_loop(0, blocks, project, 0)

    lane = lax.rem(lax.broadcasted_iota(jnp.int32, (FREQ, 3 * WIN), 1), WIN)
    row16 = lax.broadcasted_iota(jnp.int32, (8, ch), 0)
    bias = bias_ref[...]

    def pieces(x):
        high = x.astype(jnp.bfloat16)
        low = (x - high.astype(jnp.float32)).astype(jnp.bfloat16)
        return jnp.concatenate([high, high, low], 0)

    def place(start):
        base = pl.multiple_of(lax.div(start, 8) * 8, 8)
        return base, start - base

    def spectrum(src, base, off, length):
        masked = jnp.where((lane >= off) & (lane < off + length), fwd_ref[...], 0.0)
        return jnp.dot(
            masked.astype(jnp.bfloat16), pieces(src[pl.ds(base, WIN), :]),
            preferred_element_type=jnp.float32,
        )

    def put(real, imag, base, off, shift):
        out = jnp.dot(
            inv_ref[...],
            pieces(jnp.concatenate([real, imag], 0)),
            preferred_element_type=jnp.float32,
        )
        if shift is not None:
            out = out + shift
        head = pl.ds(base, 8)
        conv[head, :] = jnp.where(row16 >= off, out[:8], conv[head, :])
        conv[pl.ds(base + 8, WIN - 8), :] = out[8:]

    def forward(k, start):
        length = len_ref[0, k]
        base, off = place(start)
        s = spectrum(gated, base, off, length)
        spec[k] = s
        gr, gi = s[:HALF], s[HALF:]
        kc, ks = kf[:HALF], kf[HALF:]
        put(kc * gr + ks * gi, kc * gi - ks * gr, base, off, bias)
        return start + length

    lax.fori_loop(0, SEGS, forward, 0)

    def swish(i, total):
        at = pl.ds(pl.multiple_of(i * BLOCK, BLOCK), BLOCK)
        c = conv[at, :]
        sig = jax.nn.sigmoid(c)
        act_ref[at, :] = (c * sig).astype(jnp.bfloat16)
        g = gsw[at, :] * sig * (1.0 + c * (1.0 - sig))
        gc[at, :] = g
        return total + jnp.sum(g.reshape(BLOCK // 8, 8, ch), axis=0)

    bias_sum = lax.fori_loop(0, blocks, swish, jnp.zeros((8, ch), jnp.float32))

    def backward(k, start):
        length = len_ref[0, k]
        base, off = place(start)
        s = spectrum(gc, base, off, length)
        cr, ci = s[:HALF], s[HALF:]
        g = spec[k]
        gr, gi = g[:HALF], g[HALF:]
        kc, ks = kf[:HALF], kf[HALF:]
        put(kc * cr - ks * ci, kc * ci + ks * cr, base, off, None)
        acc[:HALF, :] += gr * cr + gi * ci
        acc[HALF:, :] += gr * ci - gi * cr
        return start + length

    lax.fori_loop(0, SEGS, backward, 0)

    def project_back(i, carry):
        at = pl.ds(pl.multiple_of(i * BLOCK, BLOCK), BLOCK)
        g = conv[at, :]
        sig = gsig[at, :]
        gp_ref[at, :ch] = (g * sig).astype(jnp.bfloat16)
        gp_ref[at, ch:] = (g * gated[at, :] * (1.0 - sig)).astype(jnp.bfloat16)
        return carry

    lax.fori_loop(0, blocks, project_back, 0)

    taps_grad = jnp.dot(
        back_table_ref[...], acc[...],
        precision=lax.Precision.HIGHEST, preferred_element_type=jnp.float32,
    )
    which = lax.broadcasted_iota(jnp.int32, (TAPS + 1, ch), 0)
    kb_ref[...] = jnp.where(which < TAPS, taps_grad, jnp.sum(bias_sum, axis=0, keepdims=True))


def pack_call(lengths, frames, grad_out, w_flat, w_out, conv_kernel, conv_bias):
    rows, width = frames.shape
    ch = w_out.shape[0]
    fwd, inv, tap_table, back_table = tables()
    taps = jnp.concatenate([conv_kernel, jnp.zeros((1, ch), jnp.float32)], 0)
    vm = pl.BlockSpec(memory_space=pltpu.VMEM)
    blocks = rows // BLOCK
    f32, bf = jnp.float32, jnp.bfloat16
    return pl.pallas_call(
        pack_kernel,
        out_shape=(
            jax.ShapeDtypeStruct((rows, 2 * ch), bf),
            jax.ShapeDtypeStruct((rows, ch), bf),
            jax.ShapeDtypeStruct((TAPS + 1, ch), f32),
        ),
        in_specs=[
            pl.BlockSpec(memory_space=pltpu.SMEM),
            pl.BlockSpec(memory_space=pl.ANY),
            pl.BlockSpec(memory_space=pl.ANY),
        ] + [vm] * 8,
        out_specs=(vm, vm, vm),
        scratch_shapes=[
            pltpu.VMEM((rows, width), bf),
            pltpu.VMEM((rows, width), bf),
            pltpu.VMEM((rows, ch), f32),
            pltpu.VMEM((rows + WIN, ch), f32),
            pltpu.VMEM((rows, ch), f32),
            pltpu.VMEM((rows + WIN, ch), f32),
            pltpu.VMEM((rows + WIN, ch), f32),
            pltpu.VMEM((SEGS, FREQ, ch), f32),
            pltpu.VMEM((FREQ, ch), f32),
            pltpu.VMEM((FREQ, ch), f32),
            pltpu.SemaphoreType.DMA((blocks,)),
            pltpu.SemaphoreType.DMA((blocks,)),
        ],
        compiler_params=pltpu.CompilerParams(vmem_limit_bytes=56 * 1024 * 1024),
        cost_estimate=pl.CostEstimate(flops=8 * 10**9, bytes_accessed=18 * 10**6, transcendentals=0),
    )(lengths, frames, grad_out, w_flat, w_out, taps, conv_bias.reshape(1, ch), fwd, inv, tap_table, back_table)


def pick_kernel(len_ref, owner_ref, keep_a, keep_b, first_a, first_b, last_a, last_b, out_ref, held):
    half, ch = last_a.shape
    rows = 2 * half
    for at, keep, first, last in ((0, keep_a, first_a, last_a), (half, keep_b, first_b, last_b)):
        total = keep[:, :ch] + first[:, :ch].astype(jnp.float32) + last[...].astype(jnp.float32)
        held[pl.ds(at, half), :] = total.astype(jnp.bfloat16).astype(jnp.float32)
    held[pl.ds(rows, WIN), :] = jnp.zeros((WIN, ch), jnp.float32)
    row = lax.broadcasted_iota(jnp.int32, (MAXLEN, WIN), 0)
    lane = lax.broadcasted_iota(jnp.int32, (MAXLEN, WIN), 1)

    def pick(k, start):
        length = len_ref[0, k]
        base = pl.multiple_of(lax.div(start, 8) * 8, 8)
        hot = ((lane == row + (start - base)) & (row < length)).astype(jnp.float32)
        out_ref[owner_ref[0, k]] = jnp.dot(
            hot.astype(jnp.bfloat16), held[pl.ds(base, WIN), :].astype(jnp.bfloat16),
            preferred_element_type=jnp.float32,
        ).astype(jnp.bfloat16)
        return start + length

    lax.fori_loop(0, SEGS, pick, 0)


def pick_call(lengths, owners, *parts):
    half, ch = parts[-1].shape
    vm = pl.BlockSpec(memory_space=pltpu.VMEM)
    sm = pl.BlockSpec(memory_space=pltpu.SMEM)
    return pl.pallas_call(
        pick_kernel,
        out_shape=jax.ShapeDtypeStruct((SEGS, MAXLEN, ch), jnp.bfloat16),
        in_specs=[sm, sm] + [vm] * 6,
        out_specs=vm,
        scratch_shapes=[pltpu.VMEM((2 * half + WIN, ch), jnp.float32)],
        compiler_params=pltpu.CompilerParams(vmem_limit_bytes=40 * 1024 * 1024),
        cost_estimate=pl.CostEstimate(flops=10**9, bytes_accessed=10**7, transcendentals=0),
    )(lengths, owners, *parts)


def order_kernel(slot_ref, src, dst, sem):
    def copy(u):
        return pltpu.make_async_copy(src.at[slot_ref[0, u]], dst.at[u], sem.at[u])

    for u in range(SEGS):
        copy(u).start()
    for u in range(SEGS):
        copy(u).wait()


def order_call(slots, received):
    return pl.pallas_call(
        order_kernel,
        out_shape=jax.ShapeDtypeStruct(received.shape, received.dtype),
        in_specs=[pl.BlockSpec(memory_space=pltpu.SMEM), pl.BlockSpec(memory_space=pl.ANY)],
        out_specs=pl.BlockSpec(memory_space=pl.ANY),
        scratch_shapes=[pltpu.SemaphoreType.DMA((SEGS,))],
        cost_estimate=pl.CostEstimate(flops=0, bytes_accessed=4 * 10**6, transcendentals=0),
    )(slots, received)


def on_device(
    frames, grad_out, w_in, conv_kernel, conv_bias, w_out, seg_lengths, seg_owner, slot_device
):
    f32, bf = jnp.float32, jnp.bfloat16
    count_dev = lax.axis_size("dp")
    rows, width = frames.shape
    ch = w_out.shape[0]
    half = rows // 2
    scale = 1.0 / math.sqrt(rows * count_dev)
    w_flat = w_in.reshape(width, 2 * ch)
    grad_proj, activated, small = pack_call(
        seg_lengths, frames, grad_out, w_flat, w_out, conv_kernel, conv_bias
    )
    small_all = lax.all_gather(small, "dp", axis=0)

    mine = lax.axis_index("mp")
    near, far = mine ^ 1, 3 - mine
    other = 3 - near
    blocks = w_flat.reshape(4, ch, 2 * ch)

    def weights(a, b):
        return jnp.concatenate(
            [lax.dynamic_index_in_dim(blocks, a, 0, False), lax.dynamic_index_in_dim(blocks, b, 0, False)], 0
        )

    def part(rows_of, w):
        return lax.dot_general(rows_of, w, (((1,), (1,)), ((), ())), preferred_element_type=f32)

    pair = [(i, i ^ 1) for i in range(4)]
    cross = [(i, 3 - i) for i in range(4)]
    top, low = grad_proj[:half], grad_proj[half:]
    w_send = weights(near, other)
    first_a = lax.ppermute(part(top, w_send).astype(bf), "mp", pair)
    first_b = lax.ppermute(part(low, weights(far, other)).astype(bf), "mp", cross)
    keep_a = part(top, weights(mine, far))
    keep_b = part(low, weights(mine, near))
    last_a = lax.ppermute((keep_a[:, ch:] + first_a[:, ch:].astype(f32)).astype(bf), "mp", cross)
    last_b = lax.ppermute((keep_b[:, ch:] + first_b[:, ch:].astype(f32)).astype(bf), "mp", pair)
    outgoing = pick_call(seg_lengths, seg_owner, keep_a, keep_b, first_a, first_b, last_a, last_b)
    received = lax.all_to_all(outgoing, "dp", split_axis=0, concat_axis=0, tiled=True)
    dx_frames = order_call(slot_device, received)

    tn = (((0,), (0,)), ((), ()))
    term = lax.dot_general(frames, grad_proj, tn, preferred_element_type=f32).astype(bf)
    out_term = lax.dot_general(grad_out, activated, tn, preferred_element_type=f32).astype(bf)
    deep = width // count_dev
    terms = jnp.concatenate([term, out_term], 1).reshape(count_dev, deep, 3 * ch)
    terms = lax.all_to_all(terms, "dp", split_axis=0, concat_axis=0, tiled=True)
    sums = jnp.sum(terms.astype(f32), axis=0) * scale
    small_sum = jnp.sum(small_all, axis=0) * scale
    return (
        dx_frames,
        sums[:, : 2 * ch].reshape(deep, 2, ch),
        sums[:, 2 * ch :].T,
        small_sum[:TAPS],
        small_sum[TAPS],
    )

def solution(mesh):
    return jax.shard_map(
        on_device,
        mesh=mesh,
        in_specs=(
            P("dp", None),
            P("dp", None),
            P(None, None, "mp"),
            P(None, "mp"),
            P("mp"),
            P("mp", None),
            P("dp", None),
            P("dp", None),
            P("dp", None),
        ),
        out_specs=(P("dp", None, "mp"), P("dp", None, "mp"), P("mp", "dp"), P(None, "mp"), P("mp")),
        check_vma=False,
    )
```

```python
import math

import jax
import jax.numpy as jnp
import numpy as np
from jax import lax
from jax.experimental import pallas as pl
from jax.experimental.pallas import tpu as pltpu
from jax.sharding import PartitionSpec as P

TAPS = 31
MAXLEN = 72
REACH = 15
WIN = 80
POINTS = 95
HALF = 48
FREQ = 2 * HALF
MARGIN = 96
SEGS = 32
GROUP = 4
MIB = 1024 * 1024
F32, BF16 = jnp.float32, jnp.bfloat16
NT = (((1,), (1,)), ((), ()))
TN = (((0,), (0,)), ((), ()))


def tables():
    f = np.arange(HALF)[:, None].astype(np.float64)
    w = np.where(f == 0, 1.0 / POINTS, 2.0 / POINTS)
    ang = 2 * np.pi * ((f * np.arange(WIN)[None, :]) % POINTS) / POINTS
    fwd = np.concatenate([np.cos(ang), np.sin(ang)], 0)
    inv = np.concatenate([w * np.cos(ang), w * np.sin(ang)], 0).T
    tang = 2 * np.pi * ((f * (np.arange(TAPS)[None, :] - REACH)) % POINTS) / POINTS
    taps = np.concatenate([np.cos(tang), np.sin(tang)], 0)
    back = np.concatenate([w * np.cos(tang), -w * np.sin(tang)], 0).T

    def split(table):
        high = table.astype(BF16).astype(np.float32)
        low = (table - high).astype(BF16).astype(np.float32)
        return np.concatenate([high, low, high], 1)

    return (
        jnp.asarray(split(fwd), F32),
        jnp.asarray(split(inv), BF16),
        jnp.asarray(taps, F32),
        jnp.asarray(back, F32),
    )


def aligned(start, rows):
    base = pl.multiple_of(lax.div(start, rows) * rows, rows)
    return base, start - base


def pieces(x):
    high = x.astype(BF16)
    low = (x - high.astype(F32)).astype(BF16)
    return jnp.concatenate([high, high, low], 0)


def chunk_kernel(first, rows, load, last, halves, *refs):
    (len_ref, frames_hbm, gout_hbm, w_ref, wout_ref, taps_ref, bias_ref,
     fwd_ref, inv_ref, tap_table_ref, back_table_ref) = refs[:11]
    refs = refs[11:]
    if first:
        gp_prev, act_prev, sum_prev = refs[:3]
        refs = refs[3:]
    gp_ref, act_ref, sum_ref = refs[:3]
    outs = refs[3 : 3 + len(halves)]
    fr, go, gsig, gated, gsw, conv, gc, spec, kf, acc, f_sem, g_sem = refs[3 + len(halves) :]
    ch = wout_ref.shape[0]
    blocks = 3
    block = load // blocks

    def copy(hbm, vmem, sem, i):
        src = pl.ds(pl.multiple_of(first + i * block, 16), block)
        dst = pl.ds(pl.multiple_of(i * block, 16), block)
        return pltpu.make_async_copy(hbm.at[src], vmem.at[dst], sem.at[i])

    for i in range(blocks):
        copy(frames_hbm, fr, f_sem, i).start()
        copy(gout_hbm, go, g_sem, i).start()

    tail = pl.ds(load, WIN)
    gated[tail, :] = jnp.zeros((WIN, ch), F32)
    gc[tail, :] = jnp.zeros((WIN, ch), F32)
    conv[...] = jnp.zeros_like(conv)
    kf[...] = jnp.dot(
        tap_table_ref[...], taps_ref[...],
        precision=lax.Precision.HIGHEST, preferred_element_type=F32,
    )
    acc[...] = sum_prev[...] if first else jnp.zeros_like(acc)

    def before(state):
        return state[1] < first

    def skip(state):
        return state[0] + 1, state[1] + len_ref[0, state[0]]

    k0, s0 = lax.while_loop(before, skip, (jnp.int32(0), jnp.int32(0)))
    s0 = s0 - first

    def project(i, carry):
        at = pl.ds(pl.multiple_of(i * block, 16), block)
        copy(frames_hbm, fr, f_sem, i).wait()
        both = jnp.dot(fr[at, :], w_ref[...], preferred_element_type=F32)
        sig = jax.nn.sigmoid(both[:, ch:])
        gsig[at, :] = sig
        gated[at, :] = both[:, :ch] * sig
        copy(gout_hbm, go, g_sem, i).wait()
        gsw[at, :] = lax.dot_general(go[at, :], wout_ref[...], NT, preferred_element_type=F32)
        return carry

    lax.fori_loop(0, blocks, project, 0)

    lane = lax.rem(lax.broadcasted_iota(jnp.int32, (FREQ, 3 * WIN), 1), WIN)
    row8 = lax.broadcasted_iota(jnp.int32, (8, ch), 0)

    def spectrum(src, base, off, length):
        masked = jnp.where((lane >= off) & (lane < off + length), fwd_ref[...], 0.0)
        return jnp.dot(
            masked.astype(BF16), pieces(src[pl.ds(base, WIN), :]), preferred_element_type=F32
        )

    def inverse(real, imag):
        return jnp.dot(
            inv_ref[...], pieces(jnp.concatenate([real, imag], 0)), preferred_element_type=F32
        )

    def put(out, base, off):
        head = pl.ds(base, 8)
        conv[head, :] = jnp.where(row8 >= off, out[:8], conv[head, :])
        conv[pl.ds(base + 8, WIN - 8), :] = out[8:]

    def group_of(start, k):
        places = []
        for j in range(GROUP):
            live = (start < rows) & (k + j < SEGS)
            length = jnp.where(live, len_ref[0, jnp.minimum(k + j, SEGS - 1)], 0)
            base, off = aligned(jnp.where(live, start, load), 8)
            places.append((base, off, length))
            start = start + length
        return places, start

    def more(state):
        return (state[1] < rows) & (state[0] < SEGS)

    def forward(state):
        k, start = state
        places, start = group_of(start, k)
        results = []
        kc, ks = kf[:HALF], kf[HALF:]
        for j, (base, off, length) in enumerate(places):
            s = spectrum(gated, base, off, length)
            spec[k - k0 + j] = s
            gr, gi = s[:HALF], s[HALF:]
            results.append(inverse(kc * gr + ks * gi, kc * gi - ks * gr))
        for (base, off, length), out in zip(places, results):
            put(out, base, off)
        return k + GROUP, start

    lax.while_loop(more, forward, (k0, s0))

    bias = bias_ref[...]

    def swish(i, carry):
        at = pl.ds(pl.multiple_of(i * block, 16), block)
        c = conv[at, :] + bias
        sig = jax.nn.sigmoid(c)
        act_ref[at, :] = (c * sig).astype(BF16)
        gc[at, :] = gsw[at, :] * sig * (1.0 + c * (1.0 - sig))
        return carry

    lax.fori_loop(0, blocks, swish, 0)

    def backward(state):
        k, start = state
        places, start = group_of(start, k)
        results = []
        kc, ks = kf[:HALF], kf[HALF:]
        real = jnp.zeros((HALF, ch), F32)
        imag = jnp.zeros((HALF, ch), F32)
        plain = jnp.zeros((8, ch), F32)
        for j, (base, off, length) in enumerate(places):
            s = spectrum(gc, base, off, length)
            cr, ci = s[:HALF], s[HALF:]
            g = spec[k - k0 + j]
            gr, gi = g[:HALF], g[HALF:]
            results.append(inverse(kc * cr - ks * ci, kc * ci + ks * cr))
            real += gr * cr + gi * ci
            imag += gr * ci - gi * cr
            plain += s[:8]
        acc[:HALF, :] += real
        acc[HALF:FREQ, :] += imag
        acc[FREQ:, :] += plain
        for (base, off, length), out in zip(places, results):
            put(out, base, off)
        return k + GROUP, start

    lax.while_loop(more, backward, (k0, s0))

    def project_back(i, carry):
        at = pl.ds(pl.multiple_of(i * block, 16), block)
        g = conv[at, :]
        sig = gsig[at, :]
        gp_ref[at, :ch] = (g * sig).astype(BF16)
        gp_ref[at, ch:] = (g * gated[at, :] * (1.0 - sig)).astype(BF16)
        return carry

    lax.fori_loop(0, blocks, project_back, 0)

    if first:
        head = pl.ds(0, MARGIN)
        from_prev = lax.broadcasted_iota(jnp.int32, (MARGIN, 1), 0) < s0
        gp_ref[head, :] = jnp.where(
            from_prev, gp_prev[...].astype(F32), gp_ref[head, :].astype(F32)
        ).astype(BF16)
        act_ref[head, :] = jnp.where(
            from_prev, act_prev[...].astype(F32), act_ref[head, :].astype(F32)
        ).astype(BF16)

    mine = lax.axis_index("mp")
    for out, (start, size, picks) in zip(outs, halves):
        for j, pick in enumerate(picks):
            at = pl.ds(pl.multiple_of(pick(mine) * ch, ch), ch)
            out[:, j * ch : (j + 1) * ch] = lax.dot_general(
                gp_ref[start : start + size, :], w_ref[at, :], NT, preferred_element_type=F32
            ).astype(out.dtype)

    if last:
        taps_grad = jnp.dot(
            back_table_ref[...], acc[:FREQ, :],
            precision=lax.Precision.HIGHEST, preferred_element_type=F32,
        )
        sum_ref[:TAPS, :] = taps_grad
        sum_ref[TAPS:, :] = acc[FREQ : FREQ + 1, :]
    else:
        sum_ref[...] = acc[...]


def chunk_call(first, rows, halves, prev, lengths, frames, grad_out, w_flat, w_out, taps, bias, consts):
    total, width = frames.shape
    ch = w_out.shape[0]
    last = first + rows == total
    load = rows if last else rows + MARGIN
    vm = pl.BlockSpec(memory_space=pltpu.VMEM)
    hbm = pl.BlockSpec(memory_space=pl.ANY)
    sm = pl.BlockSpec(memory_space=pltpu.SMEM)
    operands = [lengths, frames, grad_out, w_flat, w_out, taps, bias, *consts]
    specs = [sm, hbm, hbm] + [vm] * 8
    if first:
        gp_prev, act_prev, sum_prev = prev
        at = gp_prev.shape[0] - MARGIN
        operands += [gp_prev[at:], act_prev[at:], sum_prev]
        specs += [vm] * 3

    def body(*refs):
        chunk_kernel(first, rows, load, last, [h[:3] for h in halves], *refs)

    out_shape = [
        jax.ShapeDtypeStruct((load, 2 * ch), BF16),
        jax.ShapeDtypeStruct((load, ch), BF16),
        jax.ShapeDtypeStruct((TAPS + 1 if last else FREQ + 8, ch), F32),
    ] + [jax.ShapeDtypeStruct((size, len(picks) * ch), dtype) for _, size, picks, dtype in halves]
    return pl.pallas_call(
        body,
        out_shape=out_shape,
        in_specs=specs,
        out_specs=[vm] * len(out_shape),
        scratch_shapes=[
            pltpu.VMEM((load, width), BF16),
            pltpu.VMEM((load, width), BF16),
            pltpu.VMEM((load, ch), F32),
            pltpu.VMEM((load + WIN, ch), F32),
            pltpu.VMEM((load, ch), F32),
            pltpu.VMEM((load + WIN, ch), F32),
            pltpu.VMEM((load + WIN, ch), F32),
            pltpu.VMEM((SEGS + GROUP, FREQ, ch), F32),
            pltpu.VMEM((FREQ, ch), F32),
            pltpu.VMEM((FREQ + 8, ch), F32),
            pltpu.SemaphoreType.DMA((3,)),
            pltpu.SemaphoreType.DMA((3,)),
        ],
        compiler_params=pltpu.CompilerParams(vmem_limit_bytes=48 * MIB),
        cost_estimate=pl.CostEstimate(flops=2 * 10**10, bytes_accessed=2 * 10**7, transcendentals=0),
        name="chunk%d" % first,
    )(*operands)


def pick_kernel(
    len_ref, owner_ref, keep0, near0, far0, back0, keep_a, keep_b, first_a, first_b, last_a, last_b,
    out_ref, held,
):
    rows0, ch = keep0.shape
    half = last_a.shape[0]
    rows = rows0 + 2 * half
    held[pl.ds(0, rows0), :] = (
        keep0[...] + near0[...].astype(F32) + far0[...].astype(F32) + back0[...].astype(F32)
    ).astype(BF16)
    for at, keep, one, two in ((rows0, keep_a, first_a, last_a), (rows0 + half, keep_b, first_b, last_b)):
        held[pl.ds(at, half), :] = (
            keep[:, :ch] + one[:, :ch].astype(F32) + two[...].astype(F32)
        ).astype(BF16)
    held[pl.ds(rows, MARGIN), :] = jnp.zeros((MARGIN, ch), BF16)
    row = lax.broadcasted_iota(jnp.int32, (MAXLEN, MARGIN), 0)
    lane = lax.broadcasted_iota(jnp.int32, (MAXLEN, MARGIN), 1)

    def pick(i, start):
        for j in range(GROUP):
            k = i * GROUP + j
            length = len_ref[0, k]
            base, off = aligned(start, 16)
            hot = jnp.where((lane == row + off) & (row < length), 1.0, 0.0).astype(BF16)
            out_ref[owner_ref[0, k]] = jnp.dot(
                hot, held[pl.ds(base, MARGIN), :], preferred_element_type=F32
            ).astype(BF16)
            start = start + length
        return start

    lax.fori_loop(0, SEGS // GROUP, pick, jnp.int32(0))


def pick_call(lengths, owners, rows, *parts):
    ch = parts[-1].shape[1]
    vm = pl.BlockSpec(memory_space=pltpu.VMEM)
    sm = pl.BlockSpec(memory_space=pltpu.SMEM)
    return pl.pallas_call(
        pick_kernel,
        out_shape=jax.ShapeDtypeStruct((SEGS, MAXLEN, ch), BF16),
        in_specs=[sm, sm] + [vm] * len(parts),
        out_specs=vm,
        scratch_shapes=[pltpu.VMEM((rows + MARGIN, ch), BF16)],
        compiler_params=pltpu.CompilerParams(vmem_limit_bytes=40 * MIB),
        cost_estimate=pl.CostEstimate(flops=10**9, bytes_accessed=10**7, transcendentals=0),
        name="pick",
    )(lengths, owners, *parts)


def order_kernel(slot_ref, src, dst, sem):
    def copy(u):
        return pltpu.make_async_copy(src.at[slot_ref[0, u]], dst.at[u], sem.at[u])

    for u in range(SEGS):
        copy(u).start()
    for u in range(SEGS):
        copy(u).wait()


def order_call(slots, received):
    return pl.pallas_call(
        order_kernel,
        out_shape=jax.ShapeDtypeStruct(received.shape, received.dtype),
        in_specs=[pl.BlockSpec(memory_space=pltpu.SMEM), pl.BlockSpec(memory_space=pltpu.VMEM)],
        out_specs=pl.BlockSpec(memory_space=pl.ANY),
        scratch_shapes=[pltpu.SemaphoreType.DMA((SEGS,))],
        compiler_params=pltpu.CompilerParams(vmem_limit_bytes=16 * MIB),
        cost_estimate=pl.CostEstimate(flops=0, bytes_accessed=4 * 10**6, transcendentals=0),
        name="order",
    )(slots, received)


def weight_kernel(deep, frames_ref, gout_ref, gp0, gp1, act0, act1, keep_ref, send_ref, held):
    core = lax.rem(lax.axis_index("dp"), 2)
    total, cols = frames_ref.shape
    rows1 = gp1.shape[0]
    rows0 = total - rows1
    wide = gp0.shape[1]

    def both(left, right0, right1):
        one = lax.dot_general(left[:rows0, :], right0[:rows0, :], TN, preferred_element_type=F32)
        return one + lax.dot_general(left[rows0:, :], right1[...], TN, preferred_element_type=F32)

    held[:, :wide] = both(frames_ref, gp0, gp1)
    held[:, wide:] = both(gout_ref, act0, act1)
    for j in range(cols // (2 * deep)):
        own = pl.ds(pl.multiple_of((2 * j + core) * deep, 16), deep)
        other = pl.ds(pl.multiple_of((2 * j + 1 - core) * deep, 16), deep)
        keep_ref[j] = held[own, :]
        send_ref[j] = held[other, :].astype(BF16)


def weight_call(deep, frames, grad_out, gp0, gp1, act0, act1):
    total, width = frames.shape
    wide = gp0.shape[1] + act0.shape[1]
    cols = width // 4
    pairs = width // (2 * deep)
    vm = pl.BlockSpec(memory_space=pltpu.VMEM)
    tall = pl.BlockSpec((total, cols), lambda i: (0, i))
    out = pl.BlockSpec((pairs // 4, deep, wide), lambda i: (i, 0, 0))
    return pl.pallas_call(
        lambda *refs: weight_kernel(deep, *refs),
        grid=(4,),
        out_shape=(
            jax.ShapeDtypeStruct((pairs, deep, wide), F32),
            jax.ShapeDtypeStruct((pairs, deep, wide), BF16),
        ),
        in_specs=[tall, tall, vm, vm, vm, vm],
        out_specs=(out, out),
        scratch_shapes=[pltpu.VMEM((cols, wide), F32)],
        compiler_params=pltpu.CompilerParams(vmem_limit_bytes=48 * MIB),
        cost_estimate=pl.CostEstimate(flops=11 * 10**9, bytes_accessed=2 * 10**7, transcendentals=0),
        name="weight",
    )(frames, grad_out, gp0, gp1, act0, act1)


def on_device(
    frames, grad_out, w_in, conv_kernel, conv_bias, w_out, seg_lengths, seg_owner, slot_device
):
    count_dev = lax.axis_size("dp")
    rows, width = frames.shape
    ch = w_out.shape[0]
    scale = 1.0 / math.sqrt(rows * count_dev)
    deep = width // count_dev
    w_flat = w_in.reshape(width, 2 * ch)
    consts = tables()
    shared = (seg_lengths, frames, grad_out, w_flat, w_out, conv_kernel, conv_bias.reshape(1, ch), consts)
    half = rows // 2
    quarter = half // 2

    def turn(d):
        return lambda m: lax.rem(m + d, 4)

    def mine(m):
        return m

    def near(m):
        return m ^ 1

    def far(m):
        return 3 - m

    def other(m):
        return 3 - (m ^ 1)

    gp0, act0, sum0, keep0, near0, far0, back0 = chunk_call(
        0, half,
        [(0, half, [turn(d)], F32 if d == 0 else BF16) for d in range(4)],
        None, *shared,
    )

    def ring(d):
        return [(i, (i + d) % 4) for i in range(4)]

    far0 = lax.ppermute(far0, "mp", ring(2))
    near0 = lax.ppermute(near0, "mp", ring(1))
    back0 = lax.ppermute(back0, "mp", ring(3))

    gp1, act1, small, send_a, send_b, keep_a, keep_b = chunk_call(
        half, half,
        [
            (0, quarter, [near, other], BF16),
            (quarter, quarter, [far, other], BF16),
            (0, quarter, [mine, far], F32),
            (quarter, quarter, [mine, near], F32),
        ],
        (gp0, act0, sum0), *shared,
    )
    pair = [(i, i ^ 1) for i in range(4)]
    cross = [(i, 3 - i) for i in range(4)]
    first_a = lax.ppermute(send_a, "mp", pair)
    first_b = lax.ppermute(send_b, "mp", cross)
    small_all = lax.all_gather(small, "dp", axis=0)
    last_a = lax.ppermute((keep_a[:, ch:] + first_a[:, ch:].astype(F32)).astype(BF16), "mp", cross)
    last_b = lax.ppermute((keep_b[:, ch:] + first_b[:, ch:].astype(F32)).astype(BF16), "mp", pair)
    outgoing = pick_call(
        seg_lengths, seg_owner, rows,
        keep0, near0, far0, back0, keep_a, keep_b, first_a, first_b, last_a, last_b,
    )
    received = lax.all_to_all(outgoing, "dp", split_axis=0, concat_axis=0, tiled=True)
    dx_frames = order_call(slot_device, received)

    keep, send = weight_call(deep, frames, grad_out, gp0, gp1, act0, act1)
    got = lax.ppermute(send, "dp", [(i, i ^ 1) for i in range(count_dev)])
    terms = (keep + got.astype(F32)).astype(BF16)
    cores = [[2 * i + c for i in range(count_dev // 2)] for c in range(2)]
    terms = lax.all_to_all(
        terms, "dp", split_axis=0, concat_axis=0, axis_index_groups=cores, tiled=True
    )
    sums = jnp.sum(terms.astype(F32), axis=0) * scale
    small_sum = jnp.sum(small_all, axis=0) * scale
    return (
        dx_frames,
        sums[:, : 2 * ch].reshape(deep, 2, ch),
        sums[:, 2 * ch :].T,
        small_sum[:TAPS],
        small_sum[TAPS],
    )


def solution(mesh):
    return jax.shard_map(
        on_device,
        mesh=mesh,
        in_specs=(
            P("dp", None),
            P("dp", None),
            P(None, None, "mp"),
            P(None, "mp"),
            P("mp"),
            P("mp", None),
            P("dp", None),
            P("dp", None),
            P("dp", None),
        ),
        out_specs=(P("dp", None, "mp"), P("dp", None, "mp"), P("mp", "dp"), P(None, "mp"), P("mp")),
        check_vma=False,
    )
```

```python
import math

import jax
import jax.numpy as jnp
import numpy as np
from jax import lax
from jax.experimental import pallas as pl
from jax.experimental.pallas import tpu as pltpu
from jax.sharding import PartitionSpec as P

TAPS = 31
MAXLEN = 72
REACH = 15
WIN = 80
POINTS = 95
HALF = 48
FREQ = 2 * HALF
MARGIN = 96
SEGS = 32
GROUP = 4
MIB = 1024 * 1024
TINY = pl.CostEstimate(flops=10**6, bytes_accessed=10**5, transcendentals=0)
LONG = pl.CostEstimate(flops=10**6, bytes_accessed=6 * 10**7, transcendentals=0)
F32, BF16 = jnp.float32, jnp.bfloat16
NT = (((1,), (1,)), ((), ()))
TN = (((0,), (0,)), ((), ()))


def tables():
    f = np.arange(HALF)[:, None].astype(np.float64)
    w = np.where(f == 0, 1.0 / POINTS, 2.0 / POINTS)
    ang = 2 * np.pi * ((f * np.arange(WIN)[None, :]) % POINTS) / POINTS
    fwd = np.concatenate([np.cos(ang), np.sin(ang)], 0)
    inv = np.concatenate([w * np.cos(ang), w * np.sin(ang)], 0).T
    tang = 2 * np.pi * ((f * (np.arange(TAPS)[None, :] - REACH)) % POINTS) / POINTS
    taps = np.concatenate([np.cos(tang), np.sin(tang)], 0)
    back = np.concatenate([w * np.cos(tang), -w * np.sin(tang)], 0).T

    def split(table):
        high = table.astype(BF16).astype(np.float32)
        low = (table - high).astype(BF16).astype(np.float32)
        return np.concatenate([high, low, high], 1)

    return (
        jnp.asarray(split(fwd), F32),
        jnp.asarray(split(inv), BF16),
        jnp.asarray(taps, F32),
        jnp.asarray(back, F32),
    )


def aligned(start, rows):
    base = pl.multiple_of(lax.div(start, rows) * rows, rows)
    return base, start - base


def pieces(x):
    high = x.astype(BF16)
    low = (x - high.astype(F32)).astype(BF16)
    return jnp.concatenate([high, high, low], 0)


def chunk_kernel(first, rows, load, last, halves, *refs):
    (len_ref, frames_hbm, gout_hbm, w_ref, wout_ref, taps_ref, bias_ref,
     fwd_ref, inv_ref, tap_table_ref, back_table_ref) = refs[:11]
    refs = refs[11:]
    if first:
        gp_prev, act_prev, sum_prev = refs[:3]
        refs = refs[3:]
    gp_ref, act_ref, sum_ref = refs[:3]
    outs = refs[3 : 3 + len(halves)]
    fr, go, gsig, gated, gsw, conv, gc, spec, kf, acc, f_sem, g_sem = refs[3 + len(halves) :]
    ch = wout_ref.shape[0]
    blocks = 3
    block = load // blocks

    def copy(hbm, vmem, sem, i):
        src = pl.ds(pl.multiple_of(first + i * block, 16), block)
        dst = pl.ds(pl.multiple_of(i * block, 16), block)
        return pltpu.make_async_copy(hbm.at[src], vmem.at[dst], sem.at[i])

    for i in range(blocks):
        copy(frames_hbm, fr, f_sem, i).start()
        copy(gout_hbm, go, g_sem, i).start()

    tail = pl.ds(load, WIN)
    gated[tail, :] = jnp.zeros((WIN, ch), F32)
    gc[tail, :] = jnp.zeros((WIN, ch), F32)
    conv[...] = jnp.zeros_like(conv)
    kf[...] = jnp.dot(
        tap_table_ref[...], taps_ref[...],
        precision=lax.Precision.HIGHEST, preferred_element_type=F32,
    )
    acc[...] = sum_prev[...] if first else jnp.zeros_like(acc)

    def before(state):
        return state[1] < first

    def skip(state):
        return state[0] + 1, state[1] + len_ref[0, state[0]]

    k0, s0 = lax.while_loop(before, skip, (jnp.int32(0), jnp.int32(0)))
    s0 = s0 - first

    def project(i, carry):
        at = pl.ds(pl.multiple_of(i * block, 16), block)
        copy(frames_hbm, fr, f_sem, i).wait()
        both = jnp.dot(fr[at, :], w_ref[...], preferred_element_type=F32)
        sig = jax.nn.sigmoid(both[:, ch:])
        gsig[at, :] = sig
        gated[at, :] = both[:, :ch] * sig
        copy(gout_hbm, go, g_sem, i).wait()
        gsw[at, :] = lax.dot_general(go[at, :], wout_ref[...], NT, preferred_element_type=F32)
        return carry

    lax.fori_loop(0, blocks, project, 0)

    lane = lax.rem(lax.broadcasted_iota(jnp.int32, (FREQ, 3 * WIN), 1), WIN)
    row8 = lax.broadcasted_iota(jnp.int32, (8, ch), 0)

    def spectrum(src, base, off, length):
        masked = jnp.where((lane >= off) & (lane < off + length), fwd_ref[...], 0.0)
        return jnp.dot(
            masked.astype(BF16), pieces(src[pl.ds(base, WIN), :]), preferred_element_type=F32
        )

    def inverse(real, imag):
        return jnp.dot(
            inv_ref[...], pieces(jnp.concatenate([real, imag], 0)), preferred_element_type=F32
        )

    def put(out, base, off):
        head = pl.ds(base, 8)
        conv[head, :] = jnp.where(row8 >= off, out[:8], conv[head, :])
        conv[pl.ds(base + 8, WIN - 8), :] = out[8:]

    def group_of(start, k):
        places = []
        for j in range(GROUP):
            live = (start < rows) & (k + j < SEGS)
            length = jnp.where(live, len_ref[0, jnp.minimum(k + j, SEGS - 1)], 0)
            base, off = aligned(jnp.where(live, start, load), 8)
            places.append((base, off, length))
            start = start + length
        return places, start

    def more(state):
        return (state[1] < rows) & (state[0] < SEGS)

    def forward(state):
        k, start = state
        places, start = group_of(start, k)
        results = []
        kc, ks = kf[:HALF], kf[HALF:]
        for j, (base, off, length) in enumerate(places):
            s = spectrum(gated, base, off, length)
            spec[k - k0 + j] = s
            gr, gi = s[:HALF], s[HALF:]
            results.append(inverse(kc * gr + ks * gi, kc * gi - ks * gr))
        for (base, off, length), out in zip(places, results):
            put(out, base, off)
        return k + GROUP, start

    lax.while_loop(more, forward, (k0, s0))

    bias = bias_ref[...]

    def swish(i, carry):
        at = pl.ds(pl.multiple_of(i * block, 16), block)
        c = conv[at, :] + bias
        sig = jax.nn.sigmoid(c)
        act_ref[at, :] = (c * sig).astype(BF16)
        gc[at, :] = gsw[at, :] * sig * (1.0 + c * (1.0 - sig))
        return carry

    lax.fori_loop(0, blocks, swish, 0)

    def backward(state):
        k, start = state
        places, start = group_of(start, k)
        results = []
        kc, ks = kf[:HALF], kf[HALF:]
        real = jnp.zeros((HALF, ch), F32)
        imag = jnp.zeros((HALF, ch), F32)
        plain = jnp.zeros((8, ch), F32)
        for j, (base, off, length) in enumerate(places):
            s = spectrum(gc, base, off, length)
            cr, ci = s[:HALF], s[HALF:]
            g = spec[k - k0 + j]
            gr, gi = g[:HALF], g[HALF:]
            results.append(inverse(kc * cr - ks * ci, kc * ci + ks * cr))
            real += gr * cr + gi * ci
            imag += gr * ci - gi * cr
            plain += s[:8]
        acc[:HALF, :] += real
        acc[HALF:FREQ, :] += imag
        acc[FREQ:, :] += plain
        for (base, off, length), out in zip(places, results):
            put(out, base, off)
        return k + GROUP, start

    lax.while_loop(more, backward, (k0, s0))

    def project_back(i, carry):
        at = pl.ds(pl.multiple_of(i * block, 16), block)
        g = conv[at, :]
        sig = gsig[at, :]
        gp_ref[at, :ch] = (g * sig).astype(BF16)
        gp_ref[at, ch:] = (g * gated[at, :] * (1.0 - sig)).astype(BF16)
        return carry

    lax.fori_loop(0, blocks, project_back, 0)

    if first:
        head = pl.ds(0, MARGIN)
        from_prev = lax.broadcasted_iota(jnp.int32, (MARGIN, 1), 0) < s0
        gp_ref[head, :] = jnp.where(
            from_prev, gp_prev[...].astype(F32), gp_ref[head, :].astype(F32)
        ).astype(BF16)
        act_ref[head, :] = jnp.where(
            from_prev, act_prev[...].astype(F32), act_ref[head, :].astype(F32)
        ).astype(BF16)

    mine = lax.axis_index("mp")
    for out, (start, size, picks) in zip(outs, halves):
        for j, pick in enumerate(picks):
            at = pl.ds(pl.multiple_of(pick(mine) * ch, ch), ch)
            out[:, j * ch : (j + 1) * ch] = lax.dot_general(
                gp_ref[start : start + size, :], w_ref[at, :], NT, preferred_element_type=F32
            ).astype(out.dtype)

    if last:
        taps_grad = jnp.dot(
            back_table_ref[...], acc[:FREQ, :],
            precision=lax.Precision.HIGHEST, preferred_element_type=F32,
        )
        sum_ref[:TAPS, :] = taps_grad
        sum_ref[TAPS:, :] = acc[FREQ : FREQ + 1, :]
    else:
        sum_ref[...] = acc[...]


def chunk_call(first, rows, halves, prev, lengths, frames, grad_out, w_flat, w_out, taps, bias, consts):
    total, width = frames.shape
    ch = w_out.shape[0]
    last = first + rows == total
    load = rows if last else rows + MARGIN
    vm = pl.BlockSpec(memory_space=pltpu.VMEM)
    hbm = pl.BlockSpec(memory_space=pl.ANY)
    sm = pl.BlockSpec(memory_space=pltpu.SMEM)
    operands = [lengths, frames, grad_out, w_flat, w_out, taps, bias, *consts]
    specs = [sm, hbm, hbm] + [vm] * 8
    if first:
        gp_prev, act_prev, sum_prev = prev
        at = gp_prev.shape[0] - MARGIN
        operands += [gp_prev[at:], act_prev[at:], sum_prev]
        specs += [vm] * 3

    def body(*refs):
        chunk_kernel(first, rows, load, last, [h[:3] for h in halves], *refs)

    out_shape = [
        jax.ShapeDtypeStruct((load, 2 * ch), BF16),
        jax.ShapeDtypeStruct((load, ch), BF16),
        jax.ShapeDtypeStruct((TAPS + 1 if last else FREQ + 8, ch), F32),
    ] + [jax.ShapeDtypeStruct((size, len(picks) * ch), dtype) for _, size, picks, dtype in halves]
    return pl.pallas_call(
        body,
        out_shape=out_shape,
        in_specs=specs,
        out_specs=[vm] * len(out_shape),
        scratch_shapes=[
            pltpu.VMEM((load, width), BF16),
            pltpu.VMEM((load, width), BF16),
            pltpu.VMEM((load, ch), F32),
            pltpu.VMEM((load + WIN, ch), F32),
            pltpu.VMEM((load, ch), F32),
            pltpu.VMEM((load + WIN, ch), F32),
            pltpu.VMEM((load + WIN, ch), F32),
            pltpu.VMEM((SEGS + GROUP, FREQ, ch), F32),
            pltpu.VMEM((FREQ, ch), F32),
            pltpu.VMEM((FREQ + 8, ch), F32),
            pltpu.SemaphoreType.DMA((3,)),
            pltpu.SemaphoreType.DMA((3,)),
        ],
        compiler_params=pltpu.CompilerParams(vmem_limit_bytes=48 * MIB),
        cost_estimate=pl.CostEstimate(flops=2 * 10**10, bytes_accessed=2 * 10**7, transcendentals=0),
        name="chunk%d" % first,
    )(*operands)


def fold_kernel(keep0, near0, far0, back0, keep_a, keep_b, first_a, first_b, held_ref, part_ref, out_a, out_b):
    half, ch = out_a.shape
    held_ref[...] = (
        keep0[...] + near0[...].astype(F32) + far0[...].astype(F32) + back0[...].astype(F32)
    ).astype(BF16)
    for at, keep, one, out in ((0, keep_a, first_a, out_a), (half, keep_b, first_b, out_b)):
        out[...] = (keep[:, ch:] + one[:, ch:].astype(F32)).astype(BF16)
        part_ref[at : at + half, :] = keep[:, :ch] + one[:, :ch].astype(F32)


def pick_kernel(len_ref, owner_ref, held0, part, last_a, last_b, out_ref, held):
    rows0, ch = held0.shape
    half = last_a.shape[0]
    rows = rows0 + 2 * half
    held[pl.ds(0, rows0), :] = held0[...]
    for at, two in ((0, last_a), (half, last_b)):
        held[pl.ds(rows0 + at, half), :] = (part[at : at + half, :] + two[...].astype(F32)).astype(BF16)
    held[pl.ds(rows, MARGIN), :] = jnp.zeros((MARGIN, ch), BF16)
    row = lax.broadcasted_iota(jnp.int32, (MAXLEN, MARGIN), 0)
    lane = lax.broadcasted_iota(jnp.int32, (MAXLEN, MARGIN), 1)

    def pick(i, start):
        for j in range(GROUP):
            k = i * GROUP + j
            length = len_ref[0, k]
            base, off = aligned(start, 16)
            hot = jnp.where((lane == row + off) & (row < length), 1.0, 0.0).astype(BF16)
            out_ref[owner_ref[0, k]] = jnp.dot(
                hot, held[pl.ds(base, MARGIN), :], preferred_element_type=F32
            ).astype(BF16)
            start = start + length
        return start

    lax.fori_loop(0, SEGS // GROUP, pick, jnp.int32(0))


def pick_call(lengths, owners, rows, *parts):
    ch = parts[-1].shape[1]
    vm = pl.BlockSpec(memory_space=pltpu.VMEM)
    sm = pl.BlockSpec(memory_space=pltpu.SMEM)
    return pl.pallas_call(
        pick_kernel,
        out_shape=jax.ShapeDtypeStruct((SEGS, MAXLEN, ch), BF16),
        in_specs=[sm, sm] + [vm] * len(parts),
        out_specs=vm,
        scratch_shapes=[pltpu.VMEM((rows + MARGIN, ch), BF16)],
        compiler_params=pltpu.CompilerParams(vmem_limit_bytes=40 * MIB),
        cost_estimate=TINY,
        name="pick",
    )(lengths, owners, *parts)


def order_kernel(slot_ref, src, dst, sem):
    def copy(u):
        return pltpu.make_async_copy(src.at[slot_ref[0, u]], dst.at[u], sem.at[u])

    for u in range(SEGS):
        copy(u).start()
    for u in range(SEGS):
        copy(u).wait()


def order_call(slots, received):
    return pl.pallas_call(
        order_kernel,
        out_shape=jax.ShapeDtypeStruct(received.shape, received.dtype),
        in_specs=[pl.BlockSpec(memory_space=pltpu.SMEM), pl.BlockSpec(memory_space=pltpu.VMEM)],
        out_specs=pl.BlockSpec(memory_space=pl.ANY),
        scratch_shapes=[pltpu.SemaphoreType.DMA((SEGS,))],
        compiler_params=pltpu.CompilerParams(vmem_limit_bytes=16 * MIB),
        cost_estimate=TINY,
        name="order",
    )(slots, received)


def weight_kernel(deep, frames_ref, gout_ref, gp0, gp1, act0, act1, keep_ref, send_ref, held):
    step = pl.program_id(0) * 4
    core = lax.rem(lax.axis_index("dp"), 2)
    total, cols = frames_ref.shape
    rows1 = gp1.shape[0]
    rows0 = total - rows1
    wide = gp0.shape[1]

    def both(left, right0, right1):
        one = lax.dot_general(left[:rows0, :], right0[:rows0, :], TN, preferred_element_type=F32)
        return one + lax.dot_general(left[rows0:, :], right1[...], TN, preferred_element_type=F32)

    held[:, :wide] = both(frames_ref, gp0, gp1)
    held[:, wide:] = both(gout_ref, act0, act1)
    for j in range(cols // (2 * deep)):
        own = pl.ds(pl.multiple_of((2 * j + core) * deep, 16), deep)
        other = pl.ds(pl.multiple_of((2 * j + 1 - core) * deep, 16), deep)
        keep_ref[step + j] = held[own, :]
        send_ref[step + j] = held[other, :].astype(BF16)


def weight_call(deep, frames, grad_out, gp0, gp1, act0, act1):
    total, width = frames.shape
    wide = gp0.shape[1] + act0.shape[1]
    cols = width // 4
    pairs = width // (2 * deep)
    vm = pl.BlockSpec(memory_space=pltpu.VMEM)
    tall = pl.BlockSpec((total, cols), lambda i: (0, i))
    return pl.pallas_call(
        lambda *refs: weight_kernel(deep, *refs),
        grid=(4,),
        out_shape=(
            jax.ShapeDtypeStruct((pairs, deep, wide), F32),
            jax.ShapeDtypeStruct((pairs, deep, wide), BF16),
        ),
        in_specs=[tall, tall, vm, vm, vm, vm],
        out_specs=(vm, vm),
        scratch_shapes=[pltpu.VMEM((cols, wide), F32)],
        compiler_params=pltpu.CompilerParams(vmem_limit_bytes=48 * MIB),
        cost_estimate=pl.CostEstimate(flops=11 * 10**9, bytes_accessed=2 * 10**7, transcendentals=0),
        name="weight",
    )(frames, grad_out, gp0, gp1, act0, act1)


CUT = 640


def put_small(out, at, x):
    taps, ch = x.shape
    high = x.astype(BF16)
    for j, part in enumerate((high, (x - high.astype(F32)).astype(BF16))):
        out[at + j] = jnp.zeros(out.shape[1:], out.dtype)
        out[at + j, :taps, :ch] = part


def get_small(ref, at, shape):
    taps, ch = shape
    return ref[at, :taps, :ch].astype(F32) + ref[at + 1, :taps, :ch].astype(F32)


def places():
    dp = lax.axis_index("dp")
    return lax.div(dp, 8), lax.rem(lax.div(dp, 2), 4)


def near(v):
    return v ^ 1


def far(v):
    return 3 - v


def both_ways():
    dp = lax.axis_index("dp")
    x, y = lax.div(dp, 8), lax.rem(lax.div(dp, 2), 4)
    return (slice(0, CUT), x, y, True), (slice(CUT, None), y, x, False)


def core_sum_kernel(keep, got, small, small_got, *outs):
    small_total = small[...] + small_got[...]
    outs[4][...] = small_total
    for i, (cols, a, b, x_first) in enumerate(both_ways()):
        for j in range(4):
            for where, out, slot in ((a, outs[i], 0), (far(a), outs[i], 4), (near(a), outs[2 + i], 0), (far(near(a)), outs[2 + i], 4)):
                at = where * 4 + j if x_first else j * 4 + where
                total = keep[at, :, cols] + got[at, :, cols].astype(F32)
                out[slot + j] = total.astype(out.dtype)
    put_small(outs[3], 8, small_total)


def half_sum_kernel(own_x, own_y, small, got_x, got_y, *outs):
    small_total = small[...] + get_small(got_y, 8, small.shape)
    outs[4][...] = small_total
    for i, ((cols, a, b, x_first), own, got) in enumerate(zip(both_ways(), (own_x, own_y), (got_x, got_y))):
        for s in range(2):
            for j, where in enumerate((b, far(b))):
                at = 4 * s + where
                outs[i][2 * s + j] = own[at] + got[at].astype(F32)
            for j, where in enumerate((near(b), far(near(b)))):
                at = 4 * s + where
                outs[2 + i][2 * s + j] = (own[at] + got[at].astype(F32)).astype(BF16)
    put_small(outs[3], 4, small_total)


def square_sum_kernel(own_x, own_y, small, got_x, got_y, own_ref, small_out, *outs):
    taps, ch = small.shape
    small_total = small[...] + get_small(got_y, 4, small.shape)
    small_out[...] = small_total
    high = small_total.astype(BF16)
    low = (small_total - high.astype(F32)).astype(BF16)
    for out, at_x, at_y in ((own_ref, 0, 0), (outs[0], 2, 1), (outs[1], 1, 2), (outs[2], 3, 3)):
        out[:, :CUT] = (own_x[at_x] + got_x[at_x].astype(F32)).astype(out.dtype)
        out[:, CUT : 3 * ch] = (own_y[at_y] + got_y[at_y].astype(F32)).astype(out.dtype)
    for out in outs:
        out[:, 3 * ch :] = jnp.zeros((out.shape[0], 2 * ch), BF16)
        out[:taps, 3 * ch : 4 * ch] = high
        out[:taps, 4 * ch :] = low


def last_sum_kernel(scale, own, small, r1, r2, r3, w_out, small_out):
    taps, ch = small.shape
    total, small_total = own[...], small[...]
    for r in (r1, r2, r3):
        total = total + r[:, : 3 * ch].astype(F32)
        small_total = small_total + r[:taps, 3 * ch : 4 * ch].astype(F32) + r[:taps, 4 * ch :].astype(F32)
    w_out[...] = total * scale
    small_out[...] = small_total * scale


def sum_call(kernel, name, cost, out_shape, *operands):
    vm = pl.BlockSpec(memory_space=pltpu.VMEM)
    return pl.pallas_call(
        kernel,
        out_shape=out_shape,
        in_specs=[vm] * len(operands),
        out_specs=[vm] * len(out_shape),
        compiler_params=pltpu.CompilerParams(vmem_limit_bytes=32 * MIB),
        cost_estimate=cost,
        name=name,
    )(*operands)


def halves(n, deep, wide, small):
    return [
        jax.ShapeDtypeStruct((n, deep, CUT), F32),
        jax.ShapeDtypeStruct((n, deep, wide - CUT), F32),
        jax.ShapeDtypeStruct((n, deep, CUT), BF16),
        jax.ShapeDtypeStruct((n + 2, deep, wide - CUT), BF16),
        jax.ShapeDtypeStruct(small.shape, F32),
    ]


def move(array, fx=None, fy=None):
    def to(i):
        x, y, c = i // 8, i // 2 % 4, i % 2
        if fx is None and fy is None:
            c ^= 1
        return ((fx(x) if fx else x) * 4 + (fy(y) if fy else y)) * 2 + c

    return lax.ppermute(array, "dp", [(i, to(i)) for i in range(lax.axis_size("dp"))])


def together(live, stage, *operands):
    shapes = jax.eval_shape(stage, *operands)

    def never(*_):
        return jax.tree.map(lambda s: jnp.zeros(s.shape, s.dtype), shapes)

    return lax.cond(live, stage, never, *operands)


def on_device(
    frames, grad_out, w_in, conv_kernel, conv_bias, w_out, seg_lengths, seg_owner, slot_device
):
    count_dev = lax.axis_size("dp")
    rows, width = frames.shape
    ch = w_out.shape[0]
    scale = 1.0 / math.sqrt(rows * count_dev)
    deep = width // count_dev
    w_flat = w_in.reshape(width, 2 * ch)
    consts = tables()
    shared = (seg_lengths, frames, grad_out, w_flat, w_out, conv_kernel, conv_bias.reshape(1, ch), consts)
    half = rows // 2
    quarter = half // 2

    def turn(d):
        return lambda m: (m + d) % 4

    def mine(m):
        return m

    def other(m):
        return far(near(m))

    gp0, act0, sum0, keep0, near0, far0, back0 = chunk_call(
        0, half,
        [(0, half, [turn(d)], F32 if d == 0 else BF16) for d in range(4)],
        None, *shared,
    )

    def ring(d):
        return [(i, (i + d) % 4) for i in range(4)]

    live = seg_lengths[0, 0] > 0

    def zeroth_stage(near0, far0, back0, gp0, act0, sum0, *shared):
        shared = shared[:7] + (shared[7:],)
        return (
            lax.ppermute(near0, "mp", ring(1)),
            lax.ppermute(far0, "mp", ring(2)),
            lax.ppermute(back0, "mp", ring(3)),
            *chunk_call(
                half, half,
                [
                    (0, quarter, [near, other], BF16),
                    (quarter, quarter, [far, other], BF16),
                    (0, quarter, [mine, far], F32),
                    (quarter, quarter, [mine, near], F32),
                ],
                (gp0, act0, sum0), *shared,
            ),
        )

    near0, far0, back0, gp1, act1, small, send_a, send_b, keep_a, keep_b = together(
        live, zeroth_stage, near0, far0, back0, gp0, act0, sum0, *shared[:7], *consts
    )
    pair = [(i, i ^ 1) for i in range(4)]
    cross = [(i, 3 - i) for i in range(4)]
    first_a = lax.ppermute(send_a, "mp", pair)
    first_b = lax.ppermute(send_b, "mp", cross)
    def first_stage(frames, grad_out, gp0, gp1, act0, act1, small, send_a, send_b):
        first_a = lax.ppermute(send_a, "mp", pair)
        first_b = lax.ppermute(send_b, "mp", cross)
        small_got = move(small)
        return first_a, first_b, small_got, *weight_call(deep, frames, grad_out, gp0, gp1, act0, act1)

    def second_stage(send_a, send_b, send_x, send_y):
        return (
            lax.ppermute(send_a, "mp", cross),
            lax.ppermute(send_b, "mp", pair),
            move(send_x, fx=near),
            move(send_y, fy=near),
        )

    def third_stage(lengths, owners, held0, part, last_a, last_b, send_x, send_y):
        return (
            move(send_x, fy=near),
            move(send_y, fx=near),
            pick_call(lengths, owners, rows, held0, part, last_a, last_b),
        )

    first_a, first_b, small_got, keep, send = together(
        live, first_stage, frames, grad_out, gp0, gp1, act0, act1, small, send_a, send_b
    )
    got = move(send)
    held0, part, send_a, send_b = sum_call(
        fold_kernel, "fold", LONG,
        [
            jax.ShapeDtypeStruct((half, ch), BF16),
            jax.ShapeDtypeStruct((half, ch), F32),
            jax.ShapeDtypeStruct((quarter, ch), BF16),
            jax.ShapeDtypeStruct((quarter, ch), BF16),
        ],
        keep0, near0, far0, back0, keep_a, keep_b, first_a, first_b,
    )
    own_x, own_y, send_x, send_y, small = sum_call(
        core_sum_kernel, "core_sum", TINY, halves(8, deep, 3 * ch, small), keep, got, small, small_got
    )
    last_a, last_b, got_x, got_y = together(live, second_stage, send_a, send_b, send_x, send_y)
    own_x, own_y, send_x, send_y, small = sum_call(
        half_sum_kernel, "half_sum", TINY, halves(4, deep, 3 * ch, small), own_x, own_y, small, got_x, got_y
    )
    got_x, got_y, outgoing = together(
        live, third_stage, seg_lengths, seg_owner, held0, part, last_a, last_b, send_x, send_y
    )
    received = lax.all_to_all(outgoing, "dp", split_axis=0, concat_axis=0, tiled=True)
    dx_frames = order_call(slot_device, received)
    wide = 3 * ch
    own, small, *sends = sum_call(
        square_sum_kernel, "square_sum", TINY,
        [jax.ShapeDtypeStruct((deep, wide), F32), jax.ShapeDtypeStruct(small.shape, F32)]
        + [jax.ShapeDtypeStruct((deep, wide + 2 * ch), BF16)] * 3,
        own_x, own_y, small, got_x, got_y,
    )
    sums, small_sum = sum_call(
        lambda *refs: last_sum_kernel(scale, *refs), "last_sum", TINY,
        [jax.ShapeDtypeStruct((deep, wide), F32), jax.ShapeDtypeStruct(small.shape, F32)],
        own, small, move(sends[0], fx=far), move(sends[1], fy=far), move(sends[2], fx=far, fy=far),
    )
    return (
        dx_frames,
        sums[:, : 2 * ch].reshape(deep, 2, ch),
        sums[:, 2 * ch :].T,
        small_sum[:TAPS],
        small_sum[TAPS],
    )


def solution(mesh):
    return jax.shard_map(
        on_device,
        mesh=mesh,
        in_specs=(
            P("dp", None),
            P("dp", None),
            P(None, None, "mp"),
            P(None, "mp"),
            P("mp"),
            P("mp", None),
            P("dp", None),
            P("dp", None),
            P("dp", None),
        ),
        out_specs=(P("dp", None, "mp"), P("dp", None, "mp"), P("mp", "dp"), P(None, "mp"), P("mp")),
        check_vma=False,
    )
```

```python
import math

import jax
import jax.numpy as jnp
import numpy as np
from jax import lax
from jax.experimental import pallas as pl
from jax.experimental.pallas import tpu as pltpu
from jax.sharding import PartitionSpec as P

TAPS = 31
MAXLEN = 72
REACH = 15
WIN = 80
POINTS = 87
MAIN = 40
EDGE = 4
FREQ = 2 * (MAIN + EDGE)
MARGIN = 96
ROWS0 = 640
SEGS = 32
GROUP = 4
MIB = 1024 * 1024
TINY = pl.CostEstimate(flops=10**6, bytes_accessed=10**5, transcendentals=0)
LONG = pl.CostEstimate(flops=10**6, bytes_accessed=6 * 10**7, transcendentals=0)
F32, BF16 = jnp.float32, jnp.bfloat16
NT = (((1,), (1,)), ((), ()))
TN = (((0,), (0,)), ((), ()))


def tables():
    f = np.arange(MAIN + EDGE)[:, None]
    scale = np.where(f == 0, 1.0 / POINTS, 2.0 / POINTS)

    def waves(at, edge_sign):
        ang = 2 * np.pi * ((f * at[None, :]) % POINTS) / POINTS
        cos, sin = np.cos(ang), np.sin(ang)
        return cos[:MAIN], sin[:MAIN], cos[MAIN:], edge_sign * sin[MAIN:]

    rows = np.arange(WIN)
    shift = np.arange(TAPS) - REACH
    fwd = np.concatenate(waves(rows, 1), 0)
    weight = np.concatenate([scale[:MAIN]] * 2 + [scale[MAIN:]] * 2, 0)
    inv = (weight * fwd).T
    c, s, c4, s4 = waves(shift, 1)
    taps = np.concatenate([c, s, c4, c4, s4, -s4], 0)
    main, edge = scale[:MAIN], scale[MAIN:]
    back = np.concatenate([main * c, -main * s, edge * c4, edge * c4, -edge * s4, edge * s4], 0).T

    def split(table):
        high = table.astype(BF16).astype(np.float32)
        low = (table - high).astype(BF16).astype(np.float32)
        return np.concatenate([high, low, high], 1)

    return (
        jnp.asarray(split(fwd), BF16),
        jnp.asarray(split(inv)[:, : 2 * FREQ + 2 * MAIN], BF16),
        jnp.asarray(taps, F32),
        jnp.asarray(back, F32),
    )


def aligned(start, rows):
    base = pl.multiple_of(lax.div(start, rows) * rows, rows)
    return base, start - base


def pieces(x, rows):
    high = x.astype(BF16).astype(F32)
    return jnp.concatenate([high, high, (x - high)[:rows]], 0).astype(BF16)


def turned(x):
    return jnp.concatenate([x[EDGE:], x[:EDGE]], 0)


def chunk_kernel(first, rows, load, blocks, last, halves, *refs):
    (len_ref, frames_hbm, gout_hbm, w_ref, wout_ref, taps_ref, bias_ref,
     fwd_ref, inv_ref, tap_table_ref, back_table_ref) = refs[:11]
    refs = refs[11:]
    if first:
        gp_prev_hbm, act_prev_hbm, sum_prev = refs[:3]
        refs = refs[3:]
        gp_prev, act_prev, tail_sem = refs[-3:]
        refs = refs[:-3]
    gp_ref, act_ref, sum_ref = refs[:3]
    outs = refs[3 : 3 + len(halves)]
    fr, go, gsig, gated, gsw, conv, gc, spec, kf, acc, f_sem, g_sem = refs[3 + len(halves) :]
    ch = wout_ref.shape[0]
    block = load // blocks

    def copy(hbm, vmem, sem, i):
        src = pl.ds(pl.multiple_of(first + i * block, 16), block)
        dst = pl.ds(pl.multiple_of(i * block, 16), block)
        return pltpu.make_async_copy(hbm.at[src], vmem.at[dst], sem.at[i])

    if first:
        at = pl.ds(gp_prev_hbm.shape[0] - MARGIN, MARGIN)
        tails = [
            pltpu.make_async_copy(gp_prev_hbm.at[at], gp_prev, tail_sem.at[0]),
            pltpu.make_async_copy(act_prev_hbm.at[at], act_prev, tail_sem.at[1]),
        ]
        for tail in tails:
            tail.start()
    for i in range(blocks):
        copy(frames_hbm, fr, f_sem, i).start()
        copy(gout_hbm, go, g_sem, i).start()

    beyond = pl.ds(load, WIN)
    gated[beyond, :] = jnp.zeros((WIN, ch), F32)
    gc[beyond, :] = jnp.zeros((WIN, ch), F32)
    conv[...] = jnp.zeros_like(conv)
    kf[...] = jnp.dot(
        tap_table_ref[...], taps_ref[...],
        precision=lax.Precision.HIGHEST, preferred_element_type=F32,
    )
    acc[...] = sum_prev[...] if first else jnp.zeros_like(acc)

    def before(state):
        return state[1] < first

    def skip(state):
        return state[0] + 1, state[1] + len_ref[0, state[0]]

    k0, s0 = lax.while_loop(before, skip, (jnp.int32(0), jnp.int32(0)))
    s0 = s0 - first

    def project(i, carry):
        at = pl.ds(pl.multiple_of(i * block, 16), block)
        copy(frames_hbm, fr, f_sem, i).wait()
        both = jnp.dot(fr[at, :], w_ref[...], preferred_element_type=F32)
        sig = jax.nn.sigmoid(both[:, ch:])
        gsig[at, :] = sig
        gated[at, :] = both[:, :ch] * sig
        copy(gout_hbm, go, g_sem, i).wait()
        gsw[at, :] = lax.dot_general(go[at, :], wout_ref[...], NT, preferred_element_type=F32)
        return carry

    lax.fori_loop(0, blocks, project, 0)

    row = lax.broadcasted_iota(jnp.int32, (WIN, ch), 0)
    row8 = row[:8]

    def spectra(src, places):
        parts = []
        for base, off, length in places:
            x = src[pl.ds(base, WIN), :]
            parts.append(pieces(jnp.where((row >= off) & (row < off + length), x, 0.0), WIN))
        both = jnp.dot(fwd_ref[...], jnp.concatenate(parts, 1), preferred_element_type=F32)
        return [both[:, j * ch : (j + 1) * ch] for j in range(len(places))]

    def inverses(specs):
        parts = [pieces(jnp.concatenate(p, 0), 2 * MAIN) for p in specs]
        both = jnp.dot(inv_ref[...], jnp.concatenate(parts, 1), preferred_element_type=F32)
        return [both[:, j * ch : (j + 1) * ch] for j in range(len(specs))]

    main, sine, edge = slice(0, MAIN), slice(MAIN, 2 * MAIN), slice(2 * MAIN, FREQ)

    def put(out, base, off):
        head = pl.ds(base, 8)
        conv[head, :] = jnp.where(row8 >= off, out[:8], conv[head, :])
        conv[pl.ds(base + 8, WIN - 8), :] = out[8:]

    def group_of(start, k):
        places = []
        for j in range(GROUP):
            live = (start < rows) & (k + j < SEGS)
            length = jnp.where(live, len_ref[0, jnp.minimum(k + j, SEGS - 1)], 0)
            base, off = aligned(jnp.where(live, start, load), 8)
            places.append((base, off, length))
            start = start + length
        return places, start

    def more(state):
        return (state[1] < rows) & (state[0] < SEGS)

    def forward(state):
        k, start = state
        places, start = group_of(start, k)
        results = []
        kc, ks, ke, kt = kf[main], kf[sine], kf[edge], kf[FREQ:]
        for j in range(0, GROUP, 2):
            specs = []
            for i, s in enumerate(spectra(gated, places[j : j + 2])):
                spec[k - k0 + j + i] = s
                gr, gi, ge = s[main], s[sine], s[edge]
                specs.append((kc * gr + ks * gi, kc * gi - ks * gr, ke * ge + kt * turned(ge)))
            results += inverses(specs)
        for (base, off, length), out in zip(places, results):
            put(out, base, off)
        return k + GROUP, start

    lax.while_loop(more, forward, (k0, s0))

    bias = bias_ref[...].reshape(1, ch)

    def swish(i, carry):
        at = pl.ds(pl.multiple_of(i * block, 16), block)
        c = conv[at, :] + bias
        sig = jax.nn.sigmoid(c)
        act_ref[at, :] = (c * sig).astype(BF16)
        gc[at, :] = gsw[at, :] * sig * (1.0 + c * (1.0 - sig))
        return carry

    lax.fori_loop(0, blocks, swish, 0)

    def backward(state):
        k, start = state
        places, start = group_of(start, k)
        results = []
        kc, ks, ke, kt = kf[main], kf[sine], kf[edge], kf[FREQ:]
        sums = [jnp.zeros((n, ch), F32) for n in (MAIN, MAIN, 8, 8, 8)]
        for j in range(0, GROUP, 2):
            specs = []
            for i, s in enumerate(spectra(gc, places[j : j + 2])):
                cr, ci, ce = s[main], s[sine], s[edge]
                g = spec[k - k0 + j + i]
                gr, gi, ge = g[main], g[sine], g[edge]
                swapped = turned(ce)
                specs.append((kc * cr - ks * ci, kc * ci + ks * cr, ke * ce - kt * swapped))
                terms = (gr * cr + gi * ci, gr * ci - gi * cr, ge * ce, ge * swapped, s[:8])
                sums = [total + term for total, term in zip(sums, terms)]
            results += inverses(specs)
        at = 0
        for total in sums:
            acc[at : at + total.shape[0], :] += total
            at += total.shape[0]
        for (base, off, length), out in zip(places, results):
            put(out, base, off)
        return k + GROUP, start

    lax.while_loop(more, backward, (k0, s0))

    def project_back(i, carry):
        at = pl.ds(pl.multiple_of(i * block, 16), block)
        g = conv[at, :]
        sig = gsig[at, :]
        gp_ref[at, :ch] = (g * sig).astype(BF16)
        gp_ref[at, ch:] = (g * gated[at, :] * (1.0 - sig)).astype(BF16)
        return carry

    lax.fori_loop(0, blocks, project_back, 0)

    if first:
        for tail in tails:
            tail.wait()
        head = pl.ds(0, MARGIN)
        from_prev = lax.broadcasted_iota(jnp.int32, (MARGIN, 1), 0) < s0
        gp_ref[head, :] = jnp.where(
            from_prev, gp_prev[...].astype(F32), gp_ref[head, :].astype(F32)
        ).astype(BF16)
        act_ref[head, :] = jnp.where(
            from_prev, act_prev[...].astype(F32), act_ref[head, :].astype(F32)
        ).astype(BF16)

    mine = lax.axis_index("mp")
    for out, (start, size, picks) in zip(outs, halves):
        for j, pick in enumerate(picks):
            at = pl.ds(pl.multiple_of(pick(mine) * ch, ch), ch)
            out[:, j * ch : (j + 1) * ch] = lax.dot_general(
                gp_ref[start : start + size, :], w_ref[at, :], NT, preferred_element_type=F32
            ).astype(out.dtype)

    if last:
        taps_grad = jnp.dot(
            back_table_ref[...], acc[: FREQ + 8, :],
            precision=lax.Precision.HIGHEST, preferred_element_type=F32,
        )
        sum_ref[:TAPS, :] = taps_grad
        sum_ref[TAPS:, :] = acc[FREQ + 8 : FREQ + 9, :]
    else:
        sum_ref[...] = acc[...]


def chunk_call(first, rows, halves, prev, lengths, frames, grad_out, w_flat, w_out, taps, bias, consts):
    total, width = frames.shape
    ch = w_out.shape[0]
    last = first + rows == total
    load = rows if last else rows + MARGIN
    blocks = next(n for n in range(-(-load // 384), load) if load % (16 * n) == 0)
    vm = pl.BlockSpec(memory_space=pltpu.VMEM)
    hbm = pl.BlockSpec(memory_space=pl.ANY)
    sm = pl.BlockSpec(memory_space=pltpu.SMEM)
    operands = [lengths, frames, grad_out, w_flat, w_out, taps, bias, *consts]
    specs = [sm, hbm, hbm] + [vm] * 8
    if first:
        operands += prev
        specs += [hbm, hbm, vm]

    def body(*refs):
        chunk_kernel(first, rows, load, blocks, last, [h[:3] for h in halves], *refs)

    out_shape = [
        jax.ShapeDtypeStruct((load, 2 * ch), BF16),
        jax.ShapeDtypeStruct((load, ch), BF16),
        jax.ShapeDtypeStruct((TAPS + 1 if last else FREQ + 16, ch), F32),
    ] + [jax.ShapeDtypeStruct((size, len(picks) * ch), dtype) for _, size, picks, dtype in halves]
    return pl.pallas_call(
        body,
        out_shape=out_shape,
        in_specs=specs,
        out_specs=[vm] * len(out_shape),
        scratch_shapes=[
            pltpu.VMEM((load, width), BF16),
            pltpu.VMEM((load, width), BF16),
            pltpu.VMEM((load, ch), F32),
            pltpu.VMEM((load + WIN, ch), F32),
            pltpu.VMEM((load, ch), F32),
            pltpu.VMEM((load + WIN, ch), F32),
            pltpu.VMEM((load + WIN, ch), F32),
            pltpu.VMEM((SEGS + GROUP, FREQ, ch), F32),
            pltpu.VMEM((FREQ + 8, ch), F32),
            pltpu.VMEM((FREQ + 16, ch), F32),
            pltpu.SemaphoreType.DMA((blocks,)),
            pltpu.SemaphoreType.DMA((blocks,)),
        ] + ([
            pltpu.VMEM((MARGIN, 2 * ch), BF16),
            pltpu.VMEM((MARGIN, ch), BF16),
            pltpu.SemaphoreType.DMA((2,)),
        ] if first else []),
        compiler_params=pltpu.CompilerParams(vmem_limit_bytes=40 * MIB),
        cost_estimate=pl.CostEstimate(flops=2 * 10**10, bytes_accessed=2 * 10**7, transcendentals=0),
        name="chunk%d" % first,
    )(*operands)


def zero_sum_kernel(keep0, near0, far0, back0, after, held_ref):
    held_ref[...] = (
        keep0[...] + near0[...].astype(F32) + far0[...].astype(F32) + back0[...].astype(F32)
    ).astype(BF16)


def pass_kernel(keep_a, keep_b, first_a, first_b, out_a, out_b):
    out_a[...] = (keep_a[...] + first_a[...].astype(F32)).astype(BF16)
    out_b[...] = (keep_b[...] + first_b[...].astype(F32)).astype(BF16)


def pass_call(keep_a, keep_b, first_a, first_b):
    half, ch = keep_a.shape[0], keep_a.shape[1] // 2
    out = jax.ShapeDtypeStruct((half, ch), BF16)
    return pl.pallas_call(
        pass_kernel,
        grid=(1,),
        out_shape=(out, out),
        in_specs=[pl.BlockSpec((half, ch), lambda i: (0, 1))] * 4,
        out_specs=[pl.BlockSpec((half, ch), lambda i: (0, 0))] * 2,
        compiler_params=pltpu.CompilerParams(vmem_limit_bytes=16 * MIB),
        cost_estimate=TINY,
        name="pass",
    )(keep_a, keep_b, first_a, first_b)


def pick_kernel(
    len_ref, owner_ref, held0, keep_a, keep_b, first_a, first_b, last_a, last_b, out_ref, held
):
    rows0, ch = held0.shape
    half = last_a.shape[0]
    rows = rows0 + 2 * half
    held[pl.ds(0, rows0), :] = held0[...]
    for at, keep, one, two in ((rows0, keep_a, first_a, last_a), (rows0 + half, keep_b, first_b, last_b)):
        held[pl.ds(at, half), :] = (keep[...] + one[...].astype(F32) + two[...].astype(F32)).astype(BF16)
    held[pl.ds(rows, MARGIN), :] = jnp.zeros((MARGIN, ch), BF16)
    row = lax.broadcasted_iota(jnp.int32, (MAXLEN, MARGIN), 0)
    lane = lax.broadcasted_iota(jnp.int32, (MAXLEN, MARGIN), 1)

    def pick(i, start):
        for j in range(GROUP):
            k = i * GROUP + j
            length = len_ref[0, k]
            base, off = aligned(start, 16)
            hot = jnp.where((lane == row + off) & (row < length), 1.0, 0.0).astype(BF16)
            out_ref[owner_ref[0, k]] = jnp.dot(
                hot, held[pl.ds(base, MARGIN), :], preferred_element_type=F32
            ).astype(BF16)
            start = start + length
        return start

    lax.fori_loop(0, SEGS // GROUP, pick, jnp.int32(0))


def pick_call(lengths, owners, held0, keep_a, keep_b, first_a, first_b, last_a, last_b):
    rows0, ch = held0.shape
    half = last_a.shape[0]
    sm = pl.BlockSpec(memory_space=pltpu.SMEM)
    part = pl.BlockSpec((half, ch), lambda i: (0, 0))
    return pl.pallas_call(
        pick_kernel,
        grid=(1,),
        out_shape=jax.ShapeDtypeStruct((SEGS, MAXLEN, ch), BF16),
        in_specs=[sm, sm, pl.BlockSpec((rows0, ch), lambda i: (0, 0))] + [part] * 6,
        out_specs=pl.BlockSpec((SEGS, MAXLEN, ch), lambda i: (0, 0, 0)),
        scratch_shapes=[pltpu.VMEM((rows0 + 2 * half + MARGIN, ch), BF16)],
        compiler_params=pltpu.CompilerParams(vmem_limit_bytes=24 * MIB),
        cost_estimate=TINY,
        name="pick",
    )(lengths, owners, held0, keep_a, keep_b, first_a, first_b, last_a, last_b)


def order_kernel(slot_ref, src, dst, sem):
    def copy(u):
        return pltpu.make_async_copy(src.at[slot_ref[0, u]], dst.at[u], sem.at[u])

    for u in range(SEGS):
        copy(u).start()
    for u in range(SEGS):
        copy(u).wait()


def order_call(slots, received):
    return pl.pallas_call(
        order_kernel,
        out_shape=jax.ShapeDtypeStruct(received.shape, received.dtype),
        in_specs=[pl.BlockSpec(memory_space=pltpu.SMEM), pl.BlockSpec(memory_space=pltpu.VMEM)],
        out_specs=pl.BlockSpec(memory_space=pl.ANY),
        scratch_shapes=[pltpu.SemaphoreType.DMA((SEGS,))],
        compiler_params=pltpu.CompilerParams(vmem_limit_bytes=16 * MIB),
        cost_estimate=TINY,
        name="order",
    )(slots, received)


COLS = 4
PARTS = 4


def weight_kernel(
    deep, frames_hbm, gout_hbm, gp0_hbm, gp1_hbm, act0_hbm, act1_hbm, keep_ref, send_ref,
    fr, go, gp, act, held, f_sem, g_sem, p_sem,
):
    core = lax.rem(lax.axis_index("dp"), 2)
    total, width = frames_hbm.shape
    cols = width // COLS
    rows1 = gp1_hbm.shape[0]
    rows0 = total - rows1
    wide = gp.shape[1]

    def read(hbm, vmem, sem):
        step = total // PARTS
        return [
            pltpu.make_async_copy(hbm.at[pl.ds(i * step, step)], vmem.at[pl.ds(i * step, step)], sem.at[i])
            for i in range(PARTS)
        ]

    def pair(one, two, out, at):
        return [
            pltpu.make_async_copy(one.at[pl.ds(0, rows0)], out.at[pl.ds(0, rows0)], p_sem.at[at]),
            pltpu.make_async_copy(two, out.at[pl.ds(rows0, rows1)], p_sem.at[at + 1]),
        ]

    first = pair(act0_hbm, act1_hbm, act, 0) + read(gout_hbm, go, g_sem)
    second = pair(gp0_hbm, gp1_hbm, gp, 2) + read(frames_hbm, fr, f_sem)
    for copy in first + second:
        copy.start()
    pairs = cols // (2 * deep)
    for copies, left, right, at in ((first, go, act, slice(wide, None)), (second, fr, gp, slice(0, wide))):
        for copy in copies:
            copy.wait()
        for j in range(COLS):
            held[j % 2, :, at] = lax.dot_general(
                left[:, j * cols : (j + 1) * cols], right[...], TN, preferred_element_type=F32
            )
            for i in range(pairs):
                own = pl.ds(pl.multiple_of((2 * i + core) * deep, 16), deep)
                other = pl.ds(pl.multiple_of((2 * i + 1 - core) * deep, 16), deep)
                keep_ref[j * pairs + i, :, at] = held[j % 2, own, at]
                send_ref[j * pairs + i, :, at] = held[j % 2, other, at].astype(BF16)


def weight_call(deep, frames, grad_out, gp0, gp1, act0, act1):
    total, width = frames.shape
    ch = act0.shape[1]
    pairs = width // (2 * deep)
    vm = pl.BlockSpec(memory_space=pltpu.VMEM)
    return pl.pallas_call(
        lambda *refs: weight_kernel(deep, *refs),
        out_shape=(
            jax.ShapeDtypeStruct((pairs, deep, 3 * ch), F32),
            jax.ShapeDtypeStruct((pairs, deep, 3 * ch), BF16),
        ),
        in_specs=[pl.BlockSpec(memory_space=pl.ANY)] * 6,
        out_specs=(vm, vm),
        scratch_shapes=[
            pltpu.VMEM((total, width), BF16),
            pltpu.VMEM((total, width), BF16),
            pltpu.VMEM((total, 2 * ch), BF16),
            pltpu.VMEM((total, ch), BF16),
            pltpu.VMEM((2, width // COLS, 3 * ch), F32),
            pltpu.SemaphoreType.DMA((PARTS,)),
            pltpu.SemaphoreType.DMA((PARTS,)),
            pltpu.SemaphoreType.DMA((4,)),
        ],
        compiler_params=pltpu.CompilerParams(vmem_limit_bytes=40 * MIB),
        cost_estimate=pl.CostEstimate(flops=11 * 10**9, bytes_accessed=2 * 10**7, transcendentals=0),
        name="weight",
    )(frames, grad_out, gp0, gp1, act0, act1)


CUT = 640


def put_small(out, at, x):
    taps, ch = x.shape
    high = x.astype(BF16)
    for j, part in enumerate((high, (x - high.astype(F32)).astype(BF16))):
        out[at + j] = jnp.zeros(out.shape[1:], out.dtype)
        out[at + j, :taps, :ch] = part


def get_small(ref, at, shape):
    taps, ch = shape
    return ref[at, :taps, :ch].astype(F32) + ref[at + 1, :taps, :ch].astype(F32)


def places():
    dp = lax.axis_index("dp")
    return lax.div(dp, 8), lax.rem(lax.div(dp, 2), 4)


def near(v):
    return v ^ 1


def far(v):
    return 3 - v


def both_ways():
    dp = lax.axis_index("dp")
    x, y = lax.div(dp, 8), lax.rem(lax.div(dp, 2), 4)
    return (slice(0, CUT), x, y, True), (slice(CUT, None), y, x, False)


def core_sum_kernel(keep, got, small, small_got, *outs):
    small_total = small[...] + small_got[...]
    outs[4][...] = small_total
    for i, (cols, a, b, x_first) in enumerate(both_ways()):
        for j in range(4):
            for where, out, slot in ((a, outs[i], 0), (far(a), outs[i], 4), (near(a), outs[2 + i], 0), (far(near(a)), outs[2 + i], 4)):
                at = where * 4 + j if x_first else j * 4 + where
                total = keep[at, :, cols] + got[at, :, cols].astype(F32)
                out[slot + j] = total.astype(out.dtype)
    put_small(outs[3], 8, small_total)


def half_sum_kernel(own_x, own_y, small, got_x, got_y, *outs):
    small_total = small[...] + get_small(got_y, 8, small.shape)
    outs[4][...] = small_total
    for i, ((cols, a, b, x_first), own, got) in enumerate(zip(both_ways(), (own_x, own_y), (got_x, got_y))):
        for s in range(2):
            for j, where in enumerate((b, far(b))):
                at = 4 * s + where
                outs[i][2 * s + j] = own[at] + got[at].astype(F32)
            for j, where in enumerate((near(b), far(near(b)))):
                at = 4 * s + where
                outs[2 + i][2 * s + j] = (own[at] + got[at].astype(F32)).astype(BF16)
    put_small(outs[3], 4, small_total)


def square_sum_kernel(own_x, own_y, small, got_x, got_y, own_ref, small_out, *outs):
    taps, ch = small.shape
    small_total = small[...] + get_small(got_y, 4, small.shape)
    small_out[...] = small_total
    high = small_total.astype(BF16)
    low = (small_total - high.astype(F32)).astype(BF16)
    for out, at_x, at_y in ((own_ref, 0, 0), (outs[0], 2, 1), (outs[1], 1, 2), (outs[2], 3, 3)):
        out[:, :CUT] = (own_x[at_x] + got_x[at_x].astype(F32)).astype(out.dtype)
        out[:, CUT : 3 * ch] = (own_y[at_y] + got_y[at_y].astype(F32)).astype(out.dtype)
    for out in outs:
        out[:, 3 * ch :] = jnp.zeros((out.shape[0], 2 * ch), BF16)
        out[:taps, 3 * ch : 4 * ch] = high
        out[:taps, 4 * ch :] = low


def last_sum_kernel(scale, own, small, r1, r2, r3, after, w_in_out, w_out_out, kernel_out, bias_out):
    taps, ch = small.shape
    total, small_total = own[...], small[...]
    for r in (r1, r2, r3):
        total = total + r[:, : 3 * ch].astype(F32)
        small_total = small_total + r[:taps, 3 * ch : 4 * ch].astype(F32) + r[:taps, 4 * ch :].astype(F32)
    total, small_total = total * scale, small_total * scale
    w_in_out[:, 0, :] = total[:, :ch]
    w_in_out[:, 1, :] = total[:, ch : 2 * ch]
    w_out_out[...] = total[:, 2 * ch :]
    kernel_out[...] = small_total[:TAPS]
    bias_out[...] = small_total[TAPS:].reshape(ch)


def sum_call(kernel, name, cost, out_shape, *operands, after=()):
    vm = pl.BlockSpec(memory_space=pltpu.VMEM)
    return pl.pallas_call(
        kernel,
        out_shape=out_shape,
        in_specs=[vm] * len(operands) + [pl.BlockSpec(memory_space=pl.ANY)] * len(after),
        out_specs=[vm] * len(out_shape),
        compiler_params=pltpu.CompilerParams(vmem_limit_bytes=24 * MIB),
        cost_estimate=cost,
        name=name,
    )(*operands, *after)


def halves(n, deep, wide, small):
    return [
        jax.ShapeDtypeStruct((n, deep, CUT), F32),
        jax.ShapeDtypeStruct((n, deep, wide - CUT), F32),
        jax.ShapeDtypeStruct((n, deep, CUT), BF16),
        jax.ShapeDtypeStruct((n + 2, deep, wide - CUT), BF16),
        jax.ShapeDtypeStruct(small.shape, F32),
    ]


def move(array, fx=None, fy=None):
    def to(i):
        x, y, c = i // 8, i // 2 % 4, i % 2
        if fx is None and fy is None:
            c ^= 1
        return ((fx(x) if fx else x) * 4 + (fy(y) if fy else y)) * 2 + c

    return lax.ppermute(array, "dp", [(i, to(i)) for i in range(lax.axis_size("dp"))])


def together(live, stage, *operands):
    shapes = jax.eval_shape(stage, *operands)

    def never(*_):
        return jax.tree.map(lambda s: jnp.zeros(s.shape, s.dtype), shapes)

    return lax.cond(live, stage, never, *operands)


def on_device(
    frames, grad_out, w_in, conv_kernel, conv_bias, w_out, seg_lengths, seg_owner, slot_device
):
    count_dev = lax.axis_size("dp")
    rows, width = frames.shape
    ch = w_out.shape[0]
    scale = 1.0 / math.sqrt(rows * count_dev)
    deep = width // count_dev
    w_flat = w_in.reshape(width, 2 * ch)
    consts = tables()
    shared = (seg_lengths, frames, grad_out, w_flat, w_out, conv_kernel, conv_bias, consts)
    quarter = (rows - ROWS0) // 2

    def turn(d):
        return lambda m: (m + d) % 4

    def mine(m):
        return m

    def other(m):
        return far(near(m))

    gp0, act0, sum0, keep0, near0, far0, back0 = chunk_call(
        0, ROWS0,
        [(0, ROWS0, [turn(d)], F32 if d == 0 else BF16) for d in range(4)],
        None, *shared,
    )

    def ring(d):
        return [(i, (i + d) % 4) for i in range(4)]

    live = seg_lengths[0, 0] > 0

    def zeroth_stage(near0, far0, back0, gp0, act0, sum0, *shared):
        shared = shared[:7] + (shared[7:],)
        return (
            lax.ppermute(near0, "mp", ring(1)),
            lax.ppermute(far0, "mp", ring(2)),
            lax.ppermute(back0, "mp", ring(3)),
            *chunk_call(
                ROWS0, rows - ROWS0,
                [
                    (0, quarter, [near, other], BF16),
                    (quarter, quarter, [far, other], BF16),
                    (0, quarter, [mine, far], F32),
                    (quarter, quarter, [mine, near], F32),
                ],
                (gp0, act0, sum0), *shared,
            ),
        )

    near0, far0, back0, gp1, act1, small, send_a, send_b, keep_a, keep_b = together(
        live, zeroth_stage, near0, far0, back0, gp0, act0, sum0, *shared[:7], *consts
    )
    pair = [(i, i ^ 1) for i in range(4)]
    cross = [(i, 3 - i) for i in range(4)]
    first_a = lax.ppermute(send_a, "mp", pair)
    first_b = lax.ppermute(send_b, "mp", cross)
    wide = 3 * ch

    def weight_stage(frames, grad_out, gp0, gp1, act0, act1, small, keep0, near0, far0, back0):
        small_got = move(small)
        keep, send = weight_call(deep, frames, grad_out, gp0, gp1, act0, act1)
        got = move(send)
        (held0,) = sum_call(
            zero_sum_kernel, "zero_sum", TINY, [jax.ShapeDtypeStruct(keep0.shape, BF16)],
            keep0, near0, far0, back0, after=(keep,),
        )
        sums = sum_call(
            core_sum_kernel, "core_sum", TINY, halves(8, deep, wide, small), keep, got, small, small_got
        )
        return held0, *sums

    def first_stage(send_a, send_b, *operands):
        first_a = lax.ppermute(send_a, "mp", pair)
        first_b = lax.ppermute(send_b, "mp", cross)
        return first_a, first_b, *together(live, weight_stage, *operands)

    def last_stage(send_a, send_b):
        return lax.ppermute(send_a, "mp", cross), lax.ppermute(send_b, "mp", pair)

    def second_stage(send_x, send_y, *operands):
        got_x, got_y = move(send_x, fx=near), move(send_y, fy=near)
        return got_x, got_y, *together(live, last_stage, *operands)

    def third_stage(send_x, send_y, *operands):
        got_x, got_y = move(send_x, fy=near), move(send_y, fx=near)
        return got_x, got_y, pick_call(*operands)

    first_a, first_b, held0, own_x, own_y, send_x, send_y, small = together(
        live, first_stage, send_a, send_b,
        frames, grad_out, gp0, gp1, act0, act1, small, keep0, near0, far0, back0,
    )
    send_a, send_b = pass_call(keep_a, keep_b, first_a, first_b)
    got_x, got_y, last_a, last_b = together(live, second_stage, send_x, send_y, send_a, send_b)
    own_x, own_y, send_x, send_y, small = sum_call(
        half_sum_kernel, "half_sum", TINY, halves(4, deep, wide, small), own_x, own_y, small, got_x, got_y
    )
    got_x, got_y, outgoing = together(
        live, third_stage, send_x, send_y,
        seg_lengths, seg_owner, held0, keep_a, keep_b, first_a, first_b, last_a, last_b,
    )
    received = lax.all_to_all(outgoing, "dp", split_axis=0, concat_axis=0, tiled=True)
    dx_frames = order_call(slot_device, received)
    own, small, *sends = sum_call(
        square_sum_kernel, "square_sum", TINY,
        [jax.ShapeDtypeStruct((deep, wide), F32), jax.ShapeDtypeStruct(small.shape, F32)]
        + [jax.ShapeDtypeStruct((deep, wide + 2 * ch), BF16)] * 3,
        own_x, own_y, small, got_x, got_y,
    )
    grad_w_in, grad_w_out, grad_kernel, grad_bias = sum_call(
        lambda *refs: last_sum_kernel(scale, *refs), "last_sum", TINY,
        [
            jax.ShapeDtypeStruct((deep, 2, ch), F32),
            jax.ShapeDtypeStruct((deep, ch), F32),
            jax.ShapeDtypeStruct((TAPS, ch), F32),
            jax.ShapeDtypeStruct((ch,), F32),
        ],
        own, small, move(sends[2], fx=far, fy=far), move(sends[0], fx=far), move(sends[1], fy=far),
        after=(dx_frames,),
    )
    return dx_frames, grad_w_in, grad_w_out.T, grad_kernel, grad_bias


def solution(mesh):
    return jax.shard_map(
        on_device,
        mesh=mesh,
        in_specs=(
            P("dp", None),
            P("dp", None),
            P(None, None, "mp"),
            P(None, "mp"),
            P("mp"),
            P("mp", None),
            P("dp", None),
            P("dp", None),
            P("dp", None),
        ),
        out_specs=(P("dp", None, "mp"), P("dp", None, "mp"), P("mp", "dp"), P(None, "mp"), P("mp")),
        check_vma=False,
    )
```

```python
import math

import jax
import jax.numpy as jnp
import numpy as np
from jax import lax
from jax.experimental import pallas as pl
from jax.experimental.pallas import tpu as pltpu
from jax.sharding import PartitionSpec as P

TAPS = 31
MAXLEN = 72
REACH = 15
WIN = 80
POINTS = 87
MAIN = 40
EDGE = 4
FREQ = 2 * (MAIN + EDGE)
MARGIN = 96
ROWS0 = 576
SEGS = 32
GROUP = 5
PICKS = 8
MIB = 1024 * 1024
TINY = pl.CostEstimate(flops=10**6, bytes_accessed=10**5, transcendentals=0)
LONG = pl.CostEstimate(flops=10**6, bytes_accessed=6 * 10**7, transcendentals=0)
F32, BF16 = jnp.float32, jnp.bfloat16
NT = (((1,), (1,)), ((), ()))
TN = (((0,), (0,)), ((), ()))


def tables():
    f = np.arange(MAIN + EDGE)[:, None]
    scale = np.where(f == 0, 1.0 / POINTS, 2.0 / POINTS)

    def waves(at, edge_sign):
        ang = 2 * np.pi * ((f * at[None, :]) % POINTS) / POINTS
        cos, sin = np.cos(ang), np.sin(ang)
        return cos[:MAIN], sin[:MAIN], cos[MAIN:], edge_sign * sin[MAIN:]

    rows = np.arange(WIN)
    shift = np.arange(TAPS) - REACH
    fwd = np.concatenate(waves(rows, 1), 0)
    weight = np.concatenate([scale[:MAIN]] * 2 + [scale[MAIN:]] * 2, 0)
    inv = (weight * fwd).T
    c, s, c4, s4 = waves(shift, 1)
    taps = np.concatenate([c, s, c4, c4, s4, -s4], 0)
    main, edge = scale[:MAIN], scale[MAIN:]
    back = np.concatenate([main * c, -main * s, edge * c4, edge * c4, -edge * s4, edge * s4], 0).T

    def split(table):
        high = table.astype(BF16).astype(np.float32)
        low = (table - high).astype(BF16).astype(np.float32)
        return np.concatenate([high, low, high], 1)

    return (
        jnp.asarray(split(fwd), BF16),
        jnp.asarray(split(inv)[:, : 2 * FREQ + 2 * MAIN], BF16),
        jnp.asarray(taps, F32),
        jnp.asarray(back, F32),
    )


def aligned(start, rows):
    base = pl.multiple_of(lax.div(start, rows) * rows, rows)
    return base, start - base


def pieces(x):
    high = x.astype(BF16)
    return jnp.concatenate([high, high, (x - high.astype(F32)).astype(BF16)], 0)


def uneven_pieces(x, rows):
    high = x.astype(BF16).astype(F32)
    return jnp.concatenate(
        [jnp.concatenate([high, high], 0).astype(BF16), (x - high)[:rows].astype(BF16)], 0
    )


def turned(x):
    return jnp.concatenate([x[EDGE:], x[:EDGE]], 0)


def chunk_kernel(first, rows, load, blocks, last, halves, *refs):
    (len_ref, frames_hbm, gout_hbm, w_ref, wout_ref, taps_ref, bias_ref,
     fwd_ref, inv_ref, tap_table_ref, back_table_ref) = refs[:11]
    refs = refs[11:]
    if first:
        gp_prev_hbm, act_prev_hbm, sum_prev = refs[:3]
        refs = refs[3:]
        gp_prev, act_prev, tail_sem = refs[-3:]
        refs = refs[:-3]
    gp_ref, act_ref, sum_ref = refs[:3]
    outs = refs[3 : 3 + len(halves)]
    fr, go, gsig, gated, gsw, conv, gc, spec, kf, acc, f_sem, g_sem = refs[3 + len(halves) :]
    ch = wout_ref.shape[0]
    block = load // blocks

    def copy(hbm, vmem, sem, i):
        src = pl.ds(pl.multiple_of(first + i * block, 16), block)
        dst = pl.ds(pl.multiple_of(i * block, 16), block)
        return pltpu.make_async_copy(hbm.at[src], vmem.at[dst], sem.at[i])

    if first:
        at = pl.ds(gp_prev_hbm.shape[0] - MARGIN, MARGIN)
        tails = [
            pltpu.make_async_copy(gp_prev_hbm.at[at], gp_prev, tail_sem.at[0]),
            pltpu.make_async_copy(act_prev_hbm.at[at], act_prev, tail_sem.at[1]),
        ]
        for tail in tails:
            tail.start()
    for i in range(blocks):
        copy(frames_hbm, fr, f_sem, i).start()
        copy(gout_hbm, go, g_sem, i).start()

    beyond = pl.ds(load, WIN)
    gated[beyond, :] = jnp.zeros((WIN, ch), F32)
    gc[beyond, :] = jnp.zeros((WIN, ch), F32)
    conv[...] = jnp.zeros_like(conv)
    kf[...] = jnp.dot(
        tap_table_ref[...], taps_ref[...],
        precision=lax.Precision.HIGHEST, preferred_element_type=F32,
    )
    acc[...] = sum_prev[...] if first else jnp.zeros_like(acc)

    def before(state):
        return state[1] < first

    def skip(state):
        return state[0] + 1, state[1] + len_ref[0, state[0]]

    k0, s0 = lax.while_loop(before, skip, (jnp.int32(0), jnp.int32(0)))
    s0 = s0 - first

    def project(i, carry):
        at = pl.ds(pl.multiple_of(i * block, 16), block)
        copy(frames_hbm, fr, f_sem, i).wait()
        both = jnp.dot(fr[at, :], w_ref[...], preferred_element_type=F32)
        sig = jax.nn.sigmoid(both[:, ch:])
        gsig[at, :] = sig
        gated[at, :] = both[:, :ch] * sig
        copy(gout_hbm, go, g_sem, i).wait()
        gsw[at, :] = lax.dot_general(go[at, :], wout_ref[...], NT, preferred_element_type=F32)
        return carry

    lax.fori_loop(0, blocks, project, 0)

    row = lax.broadcasted_iota(jnp.int32, (WIN, 128), 0)
    row8 = lax.broadcasted_iota(jnp.int32, (8, ch), 0)

    def spectra(src, places):
        parts = []
        for base, off, length in places:
            keep = (row >= off) & (row < off + length)
            for lane in range(0, ch, 128):
                x = src[pl.ds(base, WIN), lane : lane + 128]
                parts.append(pieces(jnp.where(keep, x, 0.0)))
        both = jnp.dot(fwd_ref[...], jnp.concatenate(parts, 1), preferred_element_type=F32)
        return [both[:, j * ch : (j + 1) * ch] for j in range(len(places))]

    def inverses(specs):
        parts = [uneven_pieces(jnp.concatenate(p, 0), 2 * MAIN) for p in specs]
        both = jnp.dot(inv_ref[...], jnp.concatenate(parts, 1), preferred_element_type=F32)
        return [both[:, j * ch : (j + 1) * ch] for j in range(len(specs))]

    main, sine, edge = slice(0, MAIN), slice(MAIN, 2 * MAIN), slice(2 * MAIN, FREQ)

    def put(out, base, off):
        head = pl.ds(base, 8)
        conv[head, :] = jnp.where(row8 >= off, out[:8], conv[head, :])
        conv[pl.ds(base + 8, WIN - 8), :] = out[8:]

    def group_of(start, k):
        places = []
        for j in range(GROUP):
            live = (start < rows) & (k + j < SEGS)
            length = jnp.where(live, len_ref[0, jnp.minimum(k + j, SEGS - 1)], 0)
            base, off = aligned(jnp.where(live, start, load), 8)
            places.append((base, off, length))
            start = start + length
        return places, start

    def more(state):
        return (state[1] < rows) & (state[0] < SEGS)

    def forward(state):
        k, start = state
        places, start = group_of(start, k)
        kc, ks, ke, kt = kf[main], kf[sine], kf[edge], kf[FREQ:]
        specs = []
        for i, s in enumerate(spectra(gated, places)):
            spec[k - k0 + i] = s
            gr, gi, ge = s[main], s[sine], s[edge]
            specs.append((kc * gr + ks * gi, kc * gi - ks * gr, ke * ge + kt * turned(ge)))
        results = inverses(specs)
        for (base, off, length), out in zip(places, results):
            put(out, base, off)
        return k + GROUP, start

    lax.while_loop(more, forward, (k0, s0))

    bias = bias_ref[...].reshape(1, ch)

    def swish(i, carry):
        at = pl.ds(pl.multiple_of(i * block, 16), block)
        c = conv[at, :] + bias
        sig = jax.nn.sigmoid(c)
        act_ref[at, :] = (c * sig).astype(BF16)
        gc[at, :] = gsw[at, :] * sig * (1.0 + c * (1.0 - sig))
        return carry

    lax.fori_loop(0, blocks, swish, 0)

    def backward(state):
        k, start = state
        places, start = group_of(start, k)
        kc, ks, ke, kt = kf[main], kf[sine], kf[edge], kf[FREQ:]
        sums = [jnp.zeros((n, ch), F32) for n in (MAIN, MAIN, 8, 8, 8)]
        specs = []
        for i, s in enumerate(spectra(gc, places)):
            cr, ci, ce = s[main], s[sine], s[edge]
            g = spec[k - k0 + i]
            gr, gi, ge = g[main], g[sine], g[edge]
            swapped = turned(ce)
            specs.append((kc * cr - ks * ci, kc * ci + ks * cr, ke * ce - kt * swapped))
            terms = (gr * cr + gi * ci, gr * ci - gi * cr, ge * ce, ge * swapped, s[:8])
            sums = [total + term for total, term in zip(sums, terms)]
        results = inverses(specs)
        at = 0
        for total in sums:
            acc[at : at + total.shape[0], :] += total
            at += total.shape[0]
        for (base, off, length), out in zip(places, results):
            put(out, base, off)
        return k + GROUP, start

    lax.while_loop(more, backward, (k0, s0))

    def project_back(i, carry):
        at = pl.ds(pl.multiple_of(i * block, 16), block)
        g = conv[at, :]
        sig = gsig[at, :]
        gp_ref[at, :ch] = (g * sig).astype(BF16)
        gp_ref[at, ch:] = (g * gated[at, :] * (1.0 - sig)).astype(BF16)
        return carry

    lax.fori_loop(0, blocks, project_back, 0)

    if first:
        for tail in tails:
            tail.wait()
        head = pl.ds(0, MARGIN)
        from_prev = lax.broadcasted_iota(jnp.int32, (MARGIN, 1), 0) < s0
        gp_ref[head, :] = jnp.where(
            from_prev, gp_prev[...].astype(F32), gp_ref[head, :].astype(F32)
        ).astype(BF16)
        act_ref[head, :] = jnp.where(
            from_prev, act_prev[...].astype(F32), act_ref[head, :].astype(F32)
        ).astype(BF16)

    mine = lax.axis_index("mp")
    for out, (start, size, picks) in zip(outs, halves):
        for j, pick in enumerate(picks):
            at = pl.ds(pl.multiple_of(pick(mine) * ch, ch), ch)
            out[:, j * ch : (j + 1) * ch] = lax.dot_general(
                gp_ref[start : start + size, :], w_ref[at, :], NT, preferred_element_type=F32
            ).astype(out.dtype)

    if last:
        taps_grad = jnp.dot(
            back_table_ref[...], acc[: FREQ + 8, :],
            precision=lax.Precision.HIGHEST, preferred_element_type=F32,
        )
        sum_ref[:TAPS, :] = taps_grad
        sum_ref[TAPS:, :] = acc[FREQ + 8 : FREQ + 9, :]
    else:
        sum_ref[...] = acc[...]


def chunk_call(first, rows, halves, prev, lengths, frames, grad_out, w_flat, w_out, taps, bias, consts):
    total, width = frames.shape
    ch = w_out.shape[0]
    last = first + rows == total
    load = rows if last else rows + MARGIN
    blocks = next(n for n in range(-(-load // 480), load) if load % (16 * n) == 0)
    vm = pl.BlockSpec(memory_space=pltpu.VMEM)
    hbm = pl.BlockSpec(memory_space=pl.ANY)
    sm = pl.BlockSpec(memory_space=pltpu.SMEM)
    operands = [lengths, frames, grad_out, w_flat, w_out, taps, bias, *consts]
    specs = [sm, hbm, hbm] + [vm] * 8
    if first:
        operands += prev
        specs += [hbm, hbm, vm]

    def body(*refs):
        chunk_kernel(first, rows, load, blocks, last, [h[:3] for h in halves], *refs)

    out_shape = [
        jax.ShapeDtypeStruct((load, 2 * ch), BF16),
        jax.ShapeDtypeStruct((load, ch), BF16),
        jax.ShapeDtypeStruct((TAPS + 1 if last else FREQ + 16, ch), F32),
    ] + [jax.ShapeDtypeStruct((size, len(picks) * ch), dtype) for _, size, picks, dtype in halves]
    return pl.pallas_call(
        body,
        out_shape=out_shape,
        in_specs=specs,
        out_specs=[vm] * len(out_shape),
        scratch_shapes=[
            pltpu.VMEM((load, width), BF16),
            pltpu.VMEM((load, width), BF16),
            pltpu.VMEM((load, ch), F32),
            pltpu.VMEM((load + WIN, ch), F32),
            pltpu.VMEM((load, ch), F32),
            pltpu.VMEM((load + WIN, ch), F32),
            pltpu.VMEM((load + WIN, ch), F32),
            pltpu.VMEM((SEGS + GROUP, FREQ, ch), F32),
            pltpu.VMEM((FREQ + 8, ch), F32),
            pltpu.VMEM((FREQ + 16, ch), F32),
            pltpu.SemaphoreType.DMA((blocks,)),
            pltpu.SemaphoreType.DMA((blocks,)),
        ] + ([
            pltpu.VMEM((MARGIN, 2 * ch), BF16),
            pltpu.VMEM((MARGIN, ch), BF16),
            pltpu.SemaphoreType.DMA((2,)),
        ] if first else []),
        compiler_params=pltpu.CompilerParams(vmem_limit_bytes=40 * MIB),
        cost_estimate=pl.CostEstimate(flops=2 * 10**10, bytes_accessed=2 * 10**7, transcendentals=0),
        name="chunk%d" % first,
    )(*operands)


def zero_sum_kernel(keep0, near0, far0, back0, after, held_ref):
    held_ref[...] = (
        keep0[...] + near0[...].astype(F32) + far0[...].astype(F32) + back0[...].astype(F32)
    ).astype(BF16)


def pass_kernel(keep_a, keep_b, first_a, first_b, out_a, out_b):
    out_a[...] = (keep_a[...] + first_a[...].astype(F32)).astype(BF16)
    out_b[...] = (keep_b[...] + first_b[...].astype(F32)).astype(BF16)


def pass_call(keep_a, keep_b, first_a, first_b):
    half, ch = keep_a.shape[0], keep_a.shape[1] // 2
    out = jax.ShapeDtypeStruct((half, ch), BF16)
    return pl.pallas_call(
        pass_kernel,
        grid=(1,),
        out_shape=(out, out),
        in_specs=[pl.BlockSpec((half, ch), lambda i: (0, 1))] * 4,
        out_specs=[pl.BlockSpec((half, ch), lambda i: (0, 0))] * 2,
        compiler_params=pltpu.CompilerParams(vmem_limit_bytes=16 * MIB),
        cost_estimate=TINY,
        name="pass",
    )(keep_a, keep_b, first_a, first_b)


def pick_kernel(
    len_ref, owner_ref, held0, keep_a, keep_b, first_a, first_b, last_a, last_b, out_ref, held
):
    rows0, ch = held0.shape
    half = last_a.shape[0]
    rows = rows0 + 2 * half
    held[pl.ds(0, rows0), :] = held0[...]
    for at, keep, one, two in ((rows0, keep_a, first_a, last_a), (rows0 + half, keep_b, first_b, last_b)):
        held[pl.ds(at, half), :] = (keep[...] + one[...].astype(F32) + two[...].astype(F32)).astype(BF16)
    held[pl.ds(rows, MARGIN), :] = jnp.zeros((MARGIN, ch), BF16)
    row = lax.broadcasted_iota(jnp.int32, (MAXLEN, MARGIN), 0)
    lane = lax.broadcasted_iota(jnp.int32, (MAXLEN, MARGIN), 1)

    def pick(i, start):
        for j in range(PICKS):
            k = i * PICKS + j
            length = len_ref[0, k]
            base, off = aligned(start, 16)
            hot = jnp.where((lane == row + off) & (row < length), 1.0, 0.0).astype(BF16)
            out_ref[owner_ref[0, k]] = jnp.dot(
                hot, held[pl.ds(base, MARGIN), :], preferred_element_type=F32
            ).astype(BF16)
            start = start + length
        return start

    lax.fori_loop(0, SEGS // PICKS, pick, jnp.int32(0))


def pick_call(lengths, owners, held0, keep_a, keep_b, first_a, first_b, last_a, last_b):
    rows0, ch = held0.shape
    half = last_a.shape[0]
    sm = pl.BlockSpec(memory_space=pltpu.SMEM)
    part = pl.BlockSpec((half, ch), lambda i: (0, 0))
    return pl.pallas_call(
        pick_kernel,
        grid=(1,),
        out_shape=jax.ShapeDtypeStruct((SEGS, MAXLEN, ch), BF16),
        in_specs=[sm, sm, pl.BlockSpec((rows0, ch), lambda i: (0, 0))] + [part] * 6,
        out_specs=pl.BlockSpec((SEGS, MAXLEN, ch), lambda i: (0, 0, 0)),
        scratch_shapes=[pltpu.VMEM((rows0 + 2 * half + MARGIN, ch), BF16)],
        compiler_params=pltpu.CompilerParams(vmem_limit_bytes=24 * MIB),
        cost_estimate=TINY,
        name="pick",
    )(lengths, owners, held0, keep_a, keep_b, first_a, first_b, last_a, last_b)


def order_kernel(slot_ref, src, dst, done_ref, sem):
    def copy(u):
        return pltpu.make_async_copy(src.at[slot_ref[0, u]], dst.at[u], sem.at[u])

    for u in range(SEGS):
        copy(u).start()
    for u in range(SEGS):
        copy(u).wait()
    done_ref[...] = jnp.zeros_like(done_ref)


def order_call(slots, received):
    return pl.pallas_call(
        order_kernel,
        out_shape=(
            jax.ShapeDtypeStruct(received.shape, received.dtype),
            jax.ShapeDtypeStruct((8, 128), F32),
        ),
        in_specs=[pl.BlockSpec(memory_space=pltpu.SMEM), pl.BlockSpec(memory_space=pltpu.VMEM)],
        out_specs=(pl.BlockSpec(memory_space=pl.ANY), pl.BlockSpec(memory_space=pltpu.VMEM)),
        scratch_shapes=[pltpu.SemaphoreType.DMA((SEGS,))],
        compiler_params=pltpu.CompilerParams(vmem_limit_bytes=16 * MIB),
        cost_estimate=TINY,
        name="order",
    )(slots, received)


COLS = 4
PARTS = 4


def weight_kernel(
    deep, frames_hbm, gout_hbm, gp0_hbm, gp1_hbm, act0_hbm, act1_hbm, keep_ref, send_ref,
    fr, go, gp, act, held, f_sem, g_sem, p_sem,
):
    core = lax.rem(lax.axis_index("dp"), 2)
    total, width = frames_hbm.shape
    cols = width // COLS
    rows1 = gp1_hbm.shape[0]
    rows0 = total - rows1
    wide = gp.shape[1]

    def read(hbm, vmem, sem):
        step = total // PARTS
        return [
            pltpu.make_async_copy(hbm.at[pl.ds(i * step, step)], vmem.at[pl.ds(i * step, step)], sem.at[i])
            for i in range(PARTS)
        ]

    def pair(one, two, out, at):
        return [
            pltpu.make_async_copy(one.at[pl.ds(0, rows0)], out.at[pl.ds(0, rows0)], p_sem.at[at]),
            pltpu.make_async_copy(two, out.at[pl.ds(rows0, rows1)], p_sem.at[at + 1]),
        ]

    first = pair(act0_hbm, act1_hbm, act, 0) + read(gout_hbm, go, g_sem)
    second = pair(gp0_hbm, gp1_hbm, gp, 2) + read(frames_hbm, fr, f_sem)
    for copy in first + second:
        copy.start()
    pairs = cols // (2 * deep)
    for copies, left, right, at in ((first, go, act, slice(wide, None)), (second, fr, gp, slice(0, wide))):
        for copy in copies:
            copy.wait()
        for j in range(COLS):
            held[j % 2, :, at] = lax.dot_general(
                left[:, j * cols : (j + 1) * cols], right[...], TN, preferred_element_type=F32
            )
            for i in range(pairs):
                own = pl.ds(pl.multiple_of((2 * i + core) * deep, 16), deep)
                other = pl.ds(pl.multiple_of((2 * i + 1 - core) * deep, 16), deep)
                keep_ref[j * pairs + i, :, at] = held[j % 2, own, at]
                send_ref[j * pairs + i, :, at] = held[j % 2, other, at].astype(BF16)


def weight_call(deep, frames, grad_out, gp0, gp1, act0, act1):
    total, width = frames.shape
    ch = act0.shape[1]
    pairs = width // (2 * deep)
    vm = pl.BlockSpec(memory_space=pltpu.VMEM)
    return pl.pallas_call(
        lambda *refs: weight_kernel(deep, *refs),
        out_shape=(
            jax.ShapeDtypeStruct((pairs, deep, 3 * ch), F32),
            jax.ShapeDtypeStruct((pairs, deep, 3 * ch), BF16),
        ),
        in_specs=[pl.BlockSpec(memory_space=pl.ANY)] * 6,
        out_specs=(vm, vm),
        scratch_shapes=[
            pltpu.VMEM((total, width), BF16),
            pltpu.VMEM((total, width), BF16),
            pltpu.VMEM((total, 2 * ch), BF16),
            pltpu.VMEM((total, ch), BF16),
            pltpu.VMEM((2, width // COLS, 3 * ch), F32),
            pltpu.SemaphoreType.DMA((PARTS,)),
            pltpu.SemaphoreType.DMA((PARTS,)),
            pltpu.SemaphoreType.DMA((4,)),
        ],
        compiler_params=pltpu.CompilerParams(vmem_limit_bytes=40 * MIB),
        cost_estimate=pl.CostEstimate(flops=11 * 10**9, bytes_accessed=2 * 10**7, transcendentals=0),
        name="weight",
    )(frames, grad_out, gp0, gp1, act0, act1)


CUT = 640


def put_small(out, at, x):
    taps, ch = x.shape
    high = x.astype(BF16)
    for j, part in enumerate((high, (x - high.astype(F32)).astype(BF16))):
        out[at + j] = jnp.zeros(out.shape[1:], out.dtype)
        out[at + j, :taps, :ch] = part


def get_small(ref, at, shape):
    taps, ch = shape
    return ref[at, :taps, :ch].astype(F32) + ref[at + 1, :taps, :ch].astype(F32)


def places():
    dp = lax.axis_index("dp")
    return lax.div(dp, 8), lax.rem(lax.div(dp, 2), 4)


def near(v):
    return v ^ 1


def far(v):
    return 3 - v


def both_ways():
    dp = lax.axis_index("dp")
    x, y = lax.div(dp, 8), lax.rem(lax.div(dp, 2), 4)
    return (slice(0, CUT), x, y, True), (slice(CUT, None), y, x, False)


def core_sum_kernel(keep, got, small, small_got, *outs):
    small_total = small[...] + small_got[...]
    outs[4][...] = small_total
    for i, (cols, a, b, x_first) in enumerate(both_ways()):
        for j in range(4):
            for where, out, slot in ((a, outs[i], 0), (far(a), outs[i], 4), (near(a), outs[2 + i], 0), (far(near(a)), outs[2 + i], 4)):
                at = where * 4 + j if x_first else j * 4 + where
                total = keep[at, :, cols] + got[at, :, cols].astype(F32)
                out[slot + j] = total.astype(out.dtype)
    put_small(outs[3], 8, small_total)


def half_sum_kernel(own_x, own_y, small, got_x, got_y, *outs):
    small_total = small[...] + get_small(got_y, 8, small.shape)
    outs[4][...] = small_total
    for i, ((cols, a, b, x_first), own, got) in enumerate(zip(both_ways(), (own_x, own_y), (got_x, got_y))):
        for s in range(2):
            for j, where in enumerate((b, far(b))):
                at = 4 * s + where
                outs[i][2 * s + j] = own[at] + got[at].astype(F32)
            for j, where in enumerate((near(b), far(near(b)))):
                at = 4 * s + where
                outs[2 + i][2 * s + j] = (own[at] + got[at].astype(F32)).astype(BF16)
    put_small(outs[3], 4, small_total)


def square_sum_kernel(own_x, own_y, small, got_x, got_y, own_ref, small_out, *outs):
    taps, ch = small.shape
    small_total = small[...] + get_small(got_y, 4, small.shape)
    small_out[...] = small_total
    high = small_total.astype(BF16)
    low = (small_total - high.astype(F32)).astype(BF16)
    for out, at_x, at_y in ((own_ref, 0, 0), (outs[0], 2, 1), (outs[1], 1, 2), (outs[2], 3, 3)):
        out[:, :CUT] = (own_x[at_x] + got_x[at_x].astype(F32)).astype(out.dtype)
        out[:, CUT : 3 * ch] = (own_y[at_y] + got_y[at_y].astype(F32)).astype(out.dtype)
    for out in outs:
        out[:, 3 * ch :] = jnp.zeros((out.shape[0], 2 * ch), BF16)
        out[:taps, 3 * ch : 4 * ch] = high
        out[:taps, 4 * ch :] = low


def last_sum_kernel(scale, own, small, r1, r2, r3, after, w_in_out, w_out_out, kernel_out, bias_out):
    taps, ch = small.shape
    total, small_total = own[...], small[...]
    for r in (r1, r2, r3):
        total = total + r[:, : 3 * ch].astype(F32)
        small_total = small_total + r[:taps, 3 * ch : 4 * ch].astype(F32) + r[:taps, 4 * ch :].astype(F32)
    total, small_total = total * scale, small_total * scale
    w_in_out[:, 0, :] = total[:, :ch]
    w_in_out[:, 1, :] = total[:, ch : 2 * ch]
    w_out_out[...] = total[:, 2 * ch :]
    kernel_out[...] = small_total[:TAPS]
    bias_out[...] = small_total[TAPS:].reshape(ch)


def sum_call(kernel, name, cost, out_shape, *operands, after=()):
    vm = pl.BlockSpec(memory_space=pltpu.VMEM)
    return pl.pallas_call(
        kernel,
        out_shape=out_shape,
        in_specs=[vm] * len(operands) + [pl.BlockSpec(memory_space=pl.ANY)] * len(after),
        out_specs=[vm] * len(out_shape),
        compiler_params=pltpu.CompilerParams(vmem_limit_bytes=24 * MIB),
        cost_estimate=cost,
        name=name,
    )(*operands, *after)


def halves(n, deep, wide, small):
    return [
        jax.ShapeDtypeStruct((n, deep, CUT), F32),
        jax.ShapeDtypeStruct((n, deep, wide - CUT), F32),
        jax.ShapeDtypeStruct((n, deep, CUT), BF16),
        jax.ShapeDtypeStruct((n + 2, deep, wide - CUT), BF16),
        jax.ShapeDtypeStruct(small.shape, F32),
    ]


def move(array, fx=None, fy=None):
    def to(i):
        x, y, c = i // 8, i // 2 % 4, i % 2
        if fx is None and fy is None:
            c ^= 1
        return ((fx(x) if fx else x) * 4 + (fy(y) if fy else y)) * 2 + c

    return lax.ppermute(array, "dp", [(i, to(i)) for i in range(lax.axis_size("dp"))])


def together(live, stage, *operands):
    shapes = jax.eval_shape(stage, *operands)

    def never(*_):
        return jax.tree.map(lambda s: jnp.zeros(s.shape, s.dtype), shapes)

    return lax.cond(live, stage, never, *operands)


def on_device(
    frames, grad_out, w_in, conv_kernel, conv_bias, w_out, seg_lengths, seg_owner, slot_device
):
    count_dev = lax.axis_size("dp")
    rows, width = frames.shape
    ch = w_out.shape[0]
    scale = 1.0 / math.sqrt(rows * count_dev)
    deep = width // count_dev
    w_flat = w_in.reshape(width, 2 * ch)
    consts = tables()
    shared = (seg_lengths, frames, grad_out, w_flat, w_out, conv_kernel, conv_bias, consts)
    quarter = (rows - ROWS0) // 2

    def turn(d):
        return lambda m: (m + d) % 4

    def mine(m):
        return m

    def other(m):
        return far(near(m))

    gp0, act0, sum0, keep0, near0, far0, back0 = chunk_call(
        0, ROWS0,
        [(0, ROWS0, [turn(d)], F32 if d == 0 else BF16) for d in range(4)],
        None, *shared,
    )

    def ring(d):
        return [(i, (i + d) % 4) for i in range(4)]

    live = seg_lengths[0, 0] > 0

    def zeroth_stage(near0, far0, back0, gp0, act0, sum0, *shared):
        shared = shared[:7] + (shared[7:],)
        return (
            lax.ppermute(near0, "mp", ring(1)),
            lax.ppermute(far0, "mp", ring(2)),
            lax.ppermute(back0, "mp", ring(3)),
            *chunk_call(
                ROWS0, rows - ROWS0,
                [
                    (0, quarter, [near, other], BF16),
                    (quarter, quarter, [far, other], BF16),
                    (0, quarter, [mine, far], F32),
                    (quarter, quarter, [mine, near], F32),
                ],
                (gp0, act0, sum0), *shared,
            ),
        )

    near0, far0, back0, gp1, act1, small, send_a, send_b, keep_a, keep_b = together(
        live, zeroth_stage, near0, far0, back0, gp0, act0, sum0, *shared[:7], *consts
    )
    pair = [(i, i ^ 1) for i in range(4)]
    cross = [(i, 3 - i) for i in range(4)]
    first_a = lax.ppermute(send_a, "mp", pair)
    first_b = lax.ppermute(send_b, "mp", cross)
    wide = 3 * ch

    def weight_stage(frames, grad_out, gp0, gp1, act0, act1, small, keep0, near0, far0, back0):
        small_got = move(small)
        keep, send = weight_call(deep, frames, grad_out, gp0, gp1, act0, act1)
        got = move(send)
        (held0,) = sum_call(
            zero_sum_kernel, "zero_sum", TINY, [jax.ShapeDtypeStruct(keep0.shape, BF16)],
            keep0, near0, far0, back0, after=(keep,),
        )
        sums = sum_call(
            core_sum_kernel, "core_sum", TINY, halves(8, deep, wide, small), keep, got, small, small_got
        )
        return held0, *sums

    def first_stage(send_a, send_b, *operands):
        first_a = lax.ppermute(send_a, "mp", pair)
        first_b = lax.ppermute(send_b, "mp", cross)
        return first_a, first_b, *together(live, weight_stage, *operands)

    def last_stage(send_a, send_b):
        return lax.ppermute(send_a, "mp", cross), lax.ppermute(send_b, "mp", pair)

    def second_stage(send_x, send_y, *operands):
        got_x, got_y = move(send_x, fx=near), move(send_y, fy=near)
        return got_x, got_y, *together(live, last_stage, *operands)

    def third_stage(send_x, send_y, *operands):
        got_x, got_y = move(send_x, fy=near), move(send_y, fx=near)
        return got_x, got_y, pick_call(*operands)

    first_a, first_b, held0, own_x, own_y, send_x, send_y, small = together(
        live, first_stage, send_a, send_b,
        frames, grad_out, gp0, gp1, act0, act1, small, keep0, near0, far0, back0,
    )
    send_a, send_b = pass_call(keep_a, keep_b, first_a, first_b)
    got_x, got_y, last_a, last_b = together(live, second_stage, send_x, send_y, send_a, send_b)
    own_x, own_y, send_x, send_y, small = sum_call(
        half_sum_kernel, "half_sum", TINY, halves(4, deep, wide, small), own_x, own_y, small, got_x, got_y
    )
    got_x, got_y, outgoing = together(
        live, third_stage, send_x, send_y,
        seg_lengths, seg_owner, held0, keep_a, keep_b, first_a, first_b, last_a, last_b,
    )
    received = lax.all_to_all(outgoing, "dp", split_axis=0, concat_axis=0, tiled=True)
    dx_frames, done = order_call(slot_device, received)
    own, small, *sends = sum_call(
        square_sum_kernel, "square_sum", TINY,
        [jax.ShapeDtypeStruct((deep, wide), F32), jax.ShapeDtypeStruct(small.shape, F32)]
        + [jax.ShapeDtypeStruct((deep, wide + 2 * ch), BF16)] * 3,
        own_x, own_y, small, got_x, got_y,
    )
    grad_w_in, grad_w_out, grad_kernel, grad_bias = sum_call(
        lambda *refs: last_sum_kernel(scale, *refs), "last_sum", TINY,
        [
            jax.ShapeDtypeStruct((deep, 2, ch), F32),
            jax.ShapeDtypeStruct((deep, ch), F32),
            jax.ShapeDtypeStruct((TAPS, ch), F32),
            jax.ShapeDtypeStruct((ch,), F32),
        ],
        own, small, move(sends[2], fx=far, fy=far), move(sends[0], fx=far), move(sends[1], fy=far),
        after=(done,),
    )
    return dx_frames, grad_w_in, grad_w_out.T, grad_kernel, grad_bias


def solution(mesh):
    return jax.shard_map(
        on_device,
        mesh=mesh,
        in_specs=(
            P("dp", None),
            P("dp", None),
            P(None, None, "mp"),
            P(None, "mp"),
            P("mp"),
            P("mp", None),
            P("dp", None),
            P("dp", None),
            P("dp", None),
        ),
        out_specs=(P("dp", None, "mp"), P("dp", None, "mp"), P("mp", "dp"), P(None, "mp"), P("mp")),
        check_vma=False,
    )
```

```python
import math

import jax
import jax.numpy as jnp
import numpy as np
from jax import lax
from jax.experimental import pallas as pl
from jax.experimental.pallas import tpu as pltpu
from jax.sharding import PartitionSpec as P

TAPS = 31
MAXLEN = 72
REACH = 15
WIN = 80
POINTS = 87
MAIN = 40
EDGE = 4
FREQ = 2 * (MAIN + EDGE)
MARGIN = 96
ROWS0 = 576
SEGS = 32
GROUP = 5
PICKS = 8
MIB = 1024 * 1024
TINY = pl.CostEstimate(flops=10**6, bytes_accessed=10**5, transcendentals=0)
LONG = pl.CostEstimate(flops=10**6, bytes_accessed=6 * 10**7, transcendentals=0)
F32, BF16 = jnp.float32, jnp.bfloat16
NT = (((1,), (1,)), ((), ()))
TN = (((0,), (0,)), ((), ()))


def tables():
    f = np.arange(MAIN + EDGE)[:, None]
    scale = np.where(f == 0, 1.0 / POINTS, 2.0 / POINTS)

    def waves(at, edge_sign):
        ang = 2 * np.pi * ((f * at[None, :]) % POINTS) / POINTS
        cos, sin = np.cos(ang), np.sin(ang)
        return cos[:MAIN], sin[:MAIN], cos[MAIN:], edge_sign * sin[MAIN:]

    rows = np.arange(WIN)
    shift = np.arange(TAPS) - REACH
    fwd = np.concatenate(waves(rows, 1), 0)
    weight = np.concatenate([scale[:MAIN]] * 2 + [scale[MAIN:]] * 2, 0)
    inv = (weight * fwd).T
    c, s, c4, s4 = waves(shift, 1)
    taps = np.concatenate([c, s, c4, c4, s4, -s4], 0)
    main, edge = scale[:MAIN], scale[MAIN:]
    back = np.concatenate([main * c, -main * s, edge * c4, edge * c4, -edge * s4, edge * s4], 0).T

    def split(table):
        high = table.astype(BF16).astype(np.float32)
        low = (table - high).astype(BF16).astype(np.float32)
        return np.concatenate([high, low, high], 1)

    return (
        jnp.asarray(split(fwd), BF16),
        jnp.asarray(split(inv)[:, : 2 * FREQ + 2 * MAIN], BF16),
        jnp.asarray(taps, F32),
        jnp.asarray(back, F32),
    )


def aligned(start, rows):
    base = pl.multiple_of(lax.div(start, rows) * rows, rows)
    return base, start - base


def pieces(x):
    high = x.astype(BF16)
    return jnp.concatenate([high, high, (x - high.astype(F32)).astype(BF16)], 0)


def uneven_pieces(x, rows):
    high = x.astype(BF16).astype(F32)
    return jnp.concatenate(
        [jnp.concatenate([high, high], 0).astype(BF16), (x - high)[:rows].astype(BF16)], 0
    )


def turned(x):
    return jnp.concatenate([x[EDGE:], x[:EDGE]], 0)


def chunk_kernel(first, rows, load, blocks, last, halves, *refs):
    (len_ref, frames_hbm, gout_hbm, w_ref, wout_ref, taps_ref, bias_ref,
     fwd_ref, inv_ref, tap_table_ref, back_table_ref) = refs[:11]
    refs = refs[11:]
    if first:
        gp_prev_hbm, act_prev_hbm, sum_prev = refs[:3]
        refs = refs[3:]
        gp_prev, act_prev, tail_sem = refs[-3:]
        refs = refs[:-3]
    gp_ref, act_ref, sum_ref = refs[:3]
    outs = refs[3 : 3 + len(halves)]
    fr, go, gsig, gated, gsw, conv, gc, spec, kf, acc, f_sem, g_sem = refs[3 + len(halves) :]
    ch = wout_ref.shape[0]
    block = load // blocks

    def copy(hbm, vmem, sem, i):
        src = pl.ds(pl.multiple_of(first + i * block, 16), block)
        dst = pl.ds(pl.multiple_of(i * block, 16), block)
        return pltpu.make_async_copy(hbm.at[src], vmem.at[dst], sem.at[i])

    if first:
        at = pl.ds(gp_prev_hbm.shape[0] - MARGIN, MARGIN)
        tails = [
            pltpu.make_async_copy(gp_prev_hbm.at[at], gp_prev, tail_sem.at[0]),
            pltpu.make_async_copy(act_prev_hbm.at[at], act_prev, tail_sem.at[1]),
        ]
        for tail in tails:
            tail.start()
    for i in range(blocks):
        copy(frames_hbm, fr, f_sem, i).start()
        copy(gout_hbm, go, g_sem, i).start()

    beyond = pl.ds(load, WIN)
    gated[beyond, :] = jnp.zeros((WIN, ch), F32)
    gc[beyond, :] = jnp.zeros((WIN, ch), F32)
    conv[...] = jnp.zeros_like(conv)
    kf[...] = jnp.dot(
        tap_table_ref[...], taps_ref[...],
        precision=lax.Precision.HIGHEST, preferred_element_type=F32,
    )
    acc[...] = sum_prev[...] if first else jnp.zeros_like(acc)

    def before(state):
        return state[1] < first

    def skip(state):
        return state[0] + 1, state[1] + len_ref[0, state[0]]

    k0, s0 = lax.while_loop(before, skip, (jnp.int32(0), jnp.int32(0)))
    s0 = s0 - first

    def project(i, carry):
        at = pl.ds(pl.multiple_of(i * block, 16), block)
        copy(frames_hbm, fr, f_sem, i).wait()
        both = jnp.dot(fr[at, :], w_ref[...], preferred_element_type=F32)
        sig = jax.nn.sigmoid(both[:, ch:])
        gsig[at, :] = sig
        gated[at, :] = both[:, :ch] * sig
        copy(gout_hbm, go, g_sem, i).wait()
        gsw[at, :] = lax.dot_general(go[at, :], wout_ref[...], NT, preferred_element_type=F32)
        return carry

    lax.fori_loop(0, blocks, project, 0)

    row = lax.broadcasted_iota(jnp.int32, (WIN, 128), 0)
    row8 = lax.broadcasted_iota(jnp.int32, (8, ch), 0)

    def spectra(src, places):
        parts = []
        for base, off, length in places:
            keep = (row >= off) & (row < off + length)
            for lane in range(0, ch, 128):
                x = src[pl.ds(base, WIN), lane : lane + 128]
                parts.append(pieces(jnp.where(keep, x, 0.0)))
        both = jnp.dot(fwd_ref[...], jnp.concatenate(parts, 1), preferred_element_type=F32)
        return [both[:, j * ch : (j + 1) * ch] for j in range(len(places))]

    def inverses(specs):
        parts = [uneven_pieces(jnp.concatenate(p, 0), 2 * MAIN) for p in specs]
        both = jnp.dot(inv_ref[...], jnp.concatenate(parts, 1), preferred_element_type=F32)
        return [both[:, j * ch : (j + 1) * ch] for j in range(len(specs))]

    main, sine, edge = slice(0, MAIN), slice(MAIN, 2 * MAIN), slice(2 * MAIN, FREQ)

    def put(out, base, off):
        head = pl.ds(base, 8)
        conv[head, :] = jnp.where(row8 >= off, out[:8], conv[head, :])
        conv[pl.ds(base + 8, WIN - 8), :] = out[8:]

    def group_of(start, k):
        places = []
        for j in range(GROUP):
            live = (start < rows) & (k + j < SEGS)
            length = jnp.where(live, len_ref[0, jnp.minimum(k + j, SEGS - 1)], 0)
            base, off = aligned(jnp.where(live, start, load), 8)
            places.append((base, off, length))
            start = start + length
        return places, start

    def more(state):
        return (state[1] < rows) & (state[0] < SEGS)

    def forward(state):
        k, start = state
        places, start = group_of(start, k)
        kc, ks, ke, kt = kf[main], kf[sine], kf[edge], kf[FREQ:]
        specs = []
        for i, s in enumerate(spectra(gated, places)):
            spec[k - k0 + i] = s
            gr, gi, ge = s[main], s[sine], s[edge]
            specs.append((kc * gr + ks * gi, kc * gi - ks * gr, ke * ge + kt * turned(ge)))
        results = inverses(specs)
        for (base, off, length), out in zip(places, results):
            put(out, base, off)
        return k + GROUP, start

    lax.while_loop(more, forward, (k0, s0))

    bias = bias_ref[...].reshape(1, ch)

    def swish(i, carry):
        at = pl.ds(pl.multiple_of(i * block, 16), block)
        c = conv[at, :] + bias
        sig = jax.nn.sigmoid(c)
        act_ref[at, :] = (c * sig).astype(BF16)
        gc[at, :] = gsw[at, :] * sig * (1.0 + c * (1.0 - sig))
        return carry

    lax.fori_loop(0, blocks, swish, 0)

    def backward(state):
        k, start = state
        places, start = group_of(start, k)
        kc, ks, ke, kt = kf[main], kf[sine], kf[edge], kf[FREQ:]
        sums = [jnp.zeros((n, ch), F32) for n in (MAIN, MAIN, 8, 8, 8)]
        specs = []
        for i, s in enumerate(spectra(gc, places)):
            cr, ci, ce = s[main], s[sine], s[edge]
            g = spec[k - k0 + i]
            gr, gi, ge = g[main], g[sine], g[edge]
            swapped = turned(ce)
            specs.append((kc * cr - ks * ci, kc * ci + ks * cr, ke * ce - kt * swapped))
            terms = (gr * cr + gi * ci, gr * ci - gi * cr, ge * ce, ge * swapped, s[:8])
            sums = [total + term for total, term in zip(sums, terms)]
        results = inverses(specs)
        at = 0
        for total in sums:
            acc[at : at + total.shape[0], :] += total
            at += total.shape[0]
        for (base, off, length), out in zip(places, results):
            put(out, base, off)
        return k + GROUP, start

    lax.while_loop(more, backward, (k0, s0))

    def project_back(i, carry):
        at = pl.ds(pl.multiple_of(i * block, 16), block)
        g = conv[at, :]
        sig = gsig[at, :]
        gp_ref[at, :ch] = (g * sig).astype(BF16)
        gp_ref[at, ch:] = (g * gated[at, :] * (1.0 - sig)).astype(BF16)
        return carry

    lax.fori_loop(0, blocks, project_back, 0)

    if first:
        for tail in tails:
            tail.wait()
        head = pl.ds(0, MARGIN)
        from_prev = lax.broadcasted_iota(jnp.int32, (MARGIN, 1), 0) < s0
        gp_ref[head, :] = jnp.where(
            from_prev, gp_prev[...].astype(F32), gp_ref[head, :].astype(F32)
        ).astype(BF16)
        act_ref[head, :] = jnp.where(
            from_prev, act_prev[...].astype(F32), act_ref[head, :].astype(F32)
        ).astype(BF16)

    mine = lax.axis_index("mp")
    for out, (start, size, picks) in zip(outs, halves):
        for j, pick in enumerate(picks):
            at = pl.ds(pl.multiple_of(pick(mine) * ch, ch), ch)
            out[:, j * ch : (j + 1) * ch] = lax.dot_general(
                gp_ref[start : start + size, :], w_ref[at, :], NT, preferred_element_type=F32
            ).astype(out.dtype)

    if last:
        taps_grad = jnp.dot(
            back_table_ref[...], acc[: FREQ + 8, :],
            precision=lax.Precision.HIGHEST, preferred_element_type=F32,
        )
        sum_ref[:TAPS, :] = taps_grad
        sum_ref[TAPS:, :] = acc[FREQ + 8 : FREQ + 9, :]
    else:
        sum_ref[...] = acc[...]


def chunk_call(first, rows, halves, prev, lengths, frames, grad_out, w_flat, w_out, taps, bias, consts):
    total, width = frames.shape
    ch = w_out.shape[0]
    last = first + rows == total
    load = rows if last else rows + MARGIN
    blocks = next(n for n in range(-(-load // 480), load) if load % (16 * n) == 0)
    vm = pl.BlockSpec(memory_space=pltpu.VMEM)
    hbm = pl.BlockSpec(memory_space=pl.ANY)
    sm = pl.BlockSpec(memory_space=pltpu.SMEM)
    operands = [lengths, frames, grad_out, w_flat, w_out, taps, bias, *consts]
    specs = [sm, hbm, hbm] + [vm] * 8
    if first:
        operands += prev
        specs += [hbm, hbm, vm]

    def body(*refs):
        chunk_kernel(first, rows, load, blocks, last, [h[:3] for h in halves], *refs)

    out_shape = [
        jax.ShapeDtypeStruct((load, 2 * ch), BF16),
        jax.ShapeDtypeStruct((load, ch), BF16),
        jax.ShapeDtypeStruct((TAPS + 1 if last else FREQ + 16, ch), F32),
    ] + [jax.ShapeDtypeStruct((size, len(picks) * ch), dtype) for _, size, picks, dtype in halves]
    return pl.pallas_call(
        body,
        out_shape=out_shape,
        in_specs=specs,
        out_specs=[vm] * len(out_shape),
        scratch_shapes=[
            pltpu.VMEM((load, width), BF16),
            pltpu.VMEM((load, width), BF16),
            pltpu.VMEM((load, ch), F32),
            pltpu.VMEM((load + WIN, ch), F32),
            pltpu.VMEM((load, ch), F32),
            pltpu.VMEM((load + WIN, ch), F32),
            pltpu.VMEM((load + WIN, ch), F32),
            pltpu.VMEM((SEGS + GROUP, FREQ, ch), F32),
            pltpu.VMEM((FREQ + 8, ch), F32),
            pltpu.VMEM((FREQ + 16, ch), F32),
            pltpu.SemaphoreType.DMA((blocks,)),
            pltpu.SemaphoreType.DMA((blocks,)),
        ] + ([
            pltpu.VMEM((MARGIN, 2 * ch), BF16),
            pltpu.VMEM((MARGIN, ch), BF16),
            pltpu.SemaphoreType.DMA((2,)),
        ] if first else []),
        compiler_params=pltpu.CompilerParams(vmem_limit_bytes=40 * MIB),
        cost_estimate=pl.CostEstimate(flops=2 * 10**10, bytes_accessed=2 * 10**7, transcendentals=0),
        name="chunk%d" % first,
    )(*operands)


def zero_sum_kernel(keep0, near0, far0, back0, after, held_ref):
    held_ref[...] = (
        keep0[...] + near0[...].astype(F32) + far0[...].astype(F32) + back0[...].astype(F32)
    ).astype(BF16)


def pass_kernel(keep_a, keep_b, first_a, first_b, out_a, out_b):
    out_a[...] = (keep_a[...] + first_a[...].astype(F32)).astype(BF16)
    out_b[...] = (keep_b[...] + first_b[...].astype(F32)).astype(BF16)


def pass_call(keep_a, keep_b, first_a, first_b):
    half, ch = keep_a.shape[0], keep_a.shape[1] // 2
    out = jax.ShapeDtypeStruct((half, ch), BF16)
    return pl.pallas_call(
        pass_kernel,
        grid=(1,),
        out_shape=(out, out),
        in_specs=[pl.BlockSpec((half, ch), lambda i: (0, 1))] * 4,
        out_specs=[pl.BlockSpec((half, ch), lambda i: (0, 0))] * 2,
        compiler_params=pltpu.CompilerParams(vmem_limit_bytes=16 * MIB),
        cost_estimate=TINY,
        name="pass",
    )(keep_a, keep_b, first_a, first_b)


def pick_kernel(
    len_ref, owner_ref, held0, keep_a, keep_b, first_a, first_b, last_a, last_b, out_ref, held
):
    rows0, ch = held0.shape
    half = last_a.shape[0]
    rows = rows0 + 2 * half
    held[pl.ds(0, rows0), :] = held0[...]
    for at, keep, one, two in ((rows0, keep_a, first_a, last_a), (rows0 + half, keep_b, first_b, last_b)):
        held[pl.ds(at, half), :] = (keep[...] + one[...].astype(F32) + two[...].astype(F32)).astype(BF16)
    held[pl.ds(rows, MARGIN), :] = jnp.zeros((MARGIN, ch), BF16)
    row = lax.broadcasted_iota(jnp.int32, (MAXLEN, MARGIN), 0)
    lane = lax.broadcasted_iota(jnp.int32, (MAXLEN, MARGIN), 1)

    def pick(i, start):
        for j in range(PICKS):
            k = i * PICKS + j
            length = len_ref[0, k]
            base, off = aligned(start, 16)
            hot = jnp.where((lane == row + off) & (row < length), 1.0, 0.0).astype(BF16)
            out_ref[owner_ref[0, k]] = jnp.dot(
                hot, held[pl.ds(base, MARGIN), :], preferred_element_type=F32
            ).astype(BF16)
            start = start + length
        return start

    lax.fori_loop(0, SEGS // PICKS, pick, jnp.int32(0))


def pick_call(lengths, owners, held0, keep_a, keep_b, first_a, first_b, last_a, last_b):
    rows0, ch = held0.shape
    half = last_a.shape[0]
    sm = pl.BlockSpec(memory_space=pltpu.SMEM)
    part = pl.BlockSpec((half, ch), lambda i: (0, 0))
    return pl.pallas_call(
        pick_kernel,
        grid=(1,),
        out_shape=jax.ShapeDtypeStruct((SEGS, MAXLEN, ch), BF16),
        in_specs=[sm, sm, pl.BlockSpec((rows0, ch), lambda i: (0, 0))] + [part] * 6,
        out_specs=pl.BlockSpec((SEGS, MAXLEN, ch), lambda i: (0, 0, 0)),
        scratch_shapes=[pltpu.VMEM((rows0 + 2 * half + MARGIN, ch), BF16)],
        compiler_params=pltpu.CompilerParams(vmem_limit_bytes=24 * MIB),
        cost_estimate=TINY,
        name="pick",
    )(lengths, owners, held0, keep_a, keep_b, first_a, first_b, last_a, last_b)


def order_kernel(slot_ref, src, dst, done_ref, sem):
    def copy(u):
        return pltpu.make_async_copy(src.at[slot_ref[0, u]], dst.at[u], sem.at[u])

    for u in range(SEGS):
        copy(u).start()
    for u in range(SEGS):
        copy(u).wait()
    done_ref[...] = jnp.zeros_like(done_ref)


def order_call(slots, received):
    return pl.pallas_call(
        order_kernel,
        out_shape=(
            jax.ShapeDtypeStruct(received.shape, received.dtype),
            jax.ShapeDtypeStruct((8, 128), F32),
        ),
        in_specs=[pl.BlockSpec(memory_space=pltpu.SMEM), pl.BlockSpec(memory_space=pltpu.VMEM)],
        out_specs=(pl.BlockSpec(memory_space=pl.ANY), pl.BlockSpec(memory_space=pltpu.VMEM)),
        scratch_shapes=[pltpu.SemaphoreType.DMA((SEGS,))],
        compiler_params=pltpu.CompilerParams(vmem_limit_bytes=16 * MIB),
        cost_estimate=TINY,
        name="order",
    )(slots, received)


COLS = 4
PARTS = 1


def weight_kernel(
    deep, frames_hbm, gout_hbm, gp0_hbm, gp1_hbm, act0_hbm, act1_hbm, keep_ref, send_ref,
    fr, go, gp, act, held, f_sem, g_sem, p_sem,
):
    core = lax.rem(lax.axis_index("dp"), 2)
    total, width = frames_hbm.shape
    cols = width // COLS
    rows1 = gp1_hbm.shape[0]
    rows0 = total - rows1
    wide = gp.shape[1]

    def read(hbm, vmem, sem):
        step = total // PARTS
        return [
            pltpu.make_async_copy(hbm.at[pl.ds(i * step, step)], vmem.at[pl.ds(i * step, step)], sem.at[i])
            for i in range(PARTS)
        ]

    def pair(one, two, out, at):
        return [
            pltpu.make_async_copy(one.at[pl.ds(0, rows0)], out.at[pl.ds(0, rows0)], p_sem.at[at]),
            pltpu.make_async_copy(two, out.at[pl.ds(rows0, rows1)], p_sem.at[at + 1]),
        ]

    first = pair(act0_hbm, act1_hbm, act, 0) + read(gout_hbm, go, g_sem)
    second = pair(gp0_hbm, gp1_hbm, gp, 2) + read(frames_hbm, fr, f_sem)
    for copy in first + second:
        copy.start()
    pairs = cols // (2 * deep)
    step = total // PARTS

    def share(j, at):
        for i in range(pairs):
            own = pl.ds(pl.multiple_of(j * cols + (2 * i + core) * deep, 16), deep)
            other = pl.ds(pl.multiple_of(j * cols + (2 * i + 1 - core) * deep, 16), deep)
            keep_ref[j * pairs + i, :, at] = held[own, at]
            send_ref[j * pairs + i, :, at] = held[other, at].astype(BF16)

    out_cols, in_cols = slice(wide, None), slice(0, wide)
    for copy in first[:2]:
        copy.wait()
    for p in range(PARTS):
        first[2 + p].wait()
        rows = slice(p * step, (p + 1) * step)
        for j in range(COLS):
            here = slice(j * cols, (j + 1) * cols)
            term = lax.dot_general(go[rows, here], act[rows, :], TN, preferred_element_type=F32)
            held[here, out_cols] = term if p == 0 else held[here, out_cols] + term
    for copy in second:
        copy.wait()
    for j in range(COLS):
        here = slice(j * cols, (j + 1) * cols)
        held[here, in_cols] = lax.dot_general(fr[:, here], gp[...], TN, preferred_element_type=F32)
        share(j, out_cols)
        share(j, in_cols)


def weight_call(deep, frames, grad_out, gp0, gp1, act0, act1):
    total, width = frames.shape
    ch = act0.shape[1]
    pairs = width // (2 * deep)
    vm = pl.BlockSpec(memory_space=pltpu.VMEM)
    return pl.pallas_call(
        lambda *refs: weight_kernel(deep, *refs),
        out_shape=(
            jax.ShapeDtypeStruct((pairs, deep, 3 * ch), F32),
            jax.ShapeDtypeStruct((pairs, deep, 3 * ch), BF16),
        ),
        in_specs=[pl.BlockSpec(memory_space=pl.ANY)] * 6,
        out_specs=(vm, vm),
        scratch_shapes=[
            pltpu.VMEM((total, width), BF16),
            pltpu.VMEM((total, width), BF16),
            pltpu.VMEM((total, 2 * ch), BF16),
            pltpu.VMEM((total, ch), BF16),
            pltpu.VMEM((width, 3 * ch), F32),
            pltpu.SemaphoreType.DMA((PARTS,)),
            pltpu.SemaphoreType.DMA((PARTS,)),
            pltpu.SemaphoreType.DMA((4,)),
        ],
        compiler_params=pltpu.CompilerParams(vmem_limit_bytes=40 * MIB),
        cost_estimate=pl.CostEstimate(flops=11 * 10**9, bytes_accessed=2 * 10**7, transcendentals=0),
        name="weight",
    )(frames, grad_out, gp0, gp1, act0, act1)


CUT = 640


def put_small(out, at, x):
    taps, ch = x.shape
    high = x.astype(BF16)
    for j, part in enumerate((high, (x - high.astype(F32)).astype(BF16))):
        out[at + j] = jnp.zeros(out.shape[1:], out.dtype)
        out[at + j, :taps, :ch] = part


def get_small(ref, at, shape):
    taps, ch = shape
    return ref[at, :taps, :ch].astype(F32) + ref[at + 1, :taps, :ch].astype(F32)


def places():
    dp = lax.axis_index("dp")
    return lax.div(dp, 8), lax.rem(lax.div(dp, 2), 4)


def near(v):
    return v ^ 1


def far(v):
    return 3 - v


def both_ways():
    dp = lax.axis_index("dp")
    x, y = lax.div(dp, 8), lax.rem(lax.div(dp, 2), 4)
    return (slice(0, CUT), x, y, True), (slice(CUT, None), y, x, False)


def core_sum_kernel(keep, got, small, small_got, *outs):
    small_total = small[...] + small_got[...]
    outs[4][...] = small_total
    for i, (cols, a, b, x_first) in enumerate(both_ways()):
        for j in range(4):
            for where, out, slot in ((a, outs[i], 0), (far(a), outs[i], 4), (near(a), outs[2 + i], 0), (far(near(a)), outs[2 + i], 4)):
                at = where * 4 + j if x_first else j * 4 + where
                total = keep[at, :, cols] + got[at, :, cols].astype(F32)
                out[slot + j] = total.astype(out.dtype)
    put_small(outs[3], 8, small_total)


def half_sum_kernel(own_x, own_y, small, got_x, got_y, *outs):
    small_total = small[...] + get_small(got_y, 8, small.shape)
    outs[4][...] = small_total
    for i, ((cols, a, b, x_first), own, got) in enumerate(zip(both_ways(), (own_x, own_y), (got_x, got_y))):
        for s in range(2):
            for j, where in enumerate((b, far(b))):
                at = 4 * s + where
                outs[i][2 * s + j] = own[at] + got[at].astype(F32)
            for j, where in enumerate((near(b), far(near(b)))):
                at = 4 * s + where
                outs[2 + i][2 * s + j] = (own[at] + got[at].astype(F32)).astype(BF16)
    put_small(outs[3], 4, small_total)


def square_sum_kernel(own_x, own_y, small, got_x, got_y, own_ref, small_out, *outs):
    taps, ch = small.shape
    small_total = small[...] + get_small(got_y, 4, small.shape)
    small_out[...] = small_total
    high = small_total.astype(BF16)
    low = (small_total - high.astype(F32)).astype(BF16)
    for out, at_x, at_y in ((own_ref, 0, 0), (outs[0], 2, 1), (outs[1], 1, 2), (outs[2], 3, 3)):
        out[:, :CUT] = (own_x[at_x] + got_x[at_x].astype(F32)).astype(out.dtype)
        out[:, CUT : 3 * ch] = (own_y[at_y] + got_y[at_y].astype(F32)).astype(out.dtype)
    for out in outs:
        out[:, 3 * ch :] = jnp.zeros((out.shape[0], 2 * ch), BF16)
        out[:taps, 3 * ch : 4 * ch] = high
        out[:taps, 4 * ch :] = low


def last_sum_kernel(scale, own, small, r1, r2, r3, after, w_in_out, w_out_out, kernel_out, bias_out):
    taps, ch = small.shape
    total, small_total = own[...], small[...]
    for r in (r1, r2, r3):
        total = total + r[:, : 3 * ch].astype(F32)
        small_total = small_total + r[:taps, 3 * ch : 4 * ch].astype(F32) + r[:taps, 4 * ch :].astype(F32)
    total, small_total = total * scale, small_total * scale
    w_in_out[:, 0, :] = total[:, :ch]
    w_in_out[:, 1, :] = total[:, ch : 2 * ch]
    w_out_out[...] = total[:, 2 * ch :]
    kernel_out[...] = small_total[:TAPS]
    bias_out[...] = small_total[TAPS:].reshape(ch)


def sum_call(kernel, name, cost, out_shape, *operands, after=()):
    vm = pl.BlockSpec(memory_space=pltpu.VMEM)
    return pl.pallas_call(
        kernel,
        out_shape=out_shape,
        in_specs=[vm] * len(operands) + [pl.BlockSpec(memory_space=pl.ANY)] * len(after),
        out_specs=[vm] * len(out_shape),
        compiler_params=pltpu.CompilerParams(vmem_limit_bytes=24 * MIB),
        cost_estimate=cost,
        name=name,
    )(*operands, *after)


def halves(n, deep, wide, small):
    return [
        jax.ShapeDtypeStruct((n, deep, CUT), F32),
        jax.ShapeDtypeStruct((n, deep, wide - CUT), F32),
        jax.ShapeDtypeStruct((n, deep, CUT), BF16),
        jax.ShapeDtypeStruct((n + 2, deep, wide - CUT), BF16),
        jax.ShapeDtypeStruct(small.shape, F32),
    ]


def move(array, fx=None, fy=None):
    def to(i):
        x, y, c = i // 8, i // 2 % 4, i % 2
        if fx is None and fy is None:
            c ^= 1
        return ((fx(x) if fx else x) * 4 + (fy(y) if fy else y)) * 2 + c

    return lax.ppermute(array, "dp", [(i, to(i)) for i in range(lax.axis_size("dp"))])


def together(live, stage, *operands):
    shapes = jax.eval_shape(stage, *operands)

    def never(*_):
        return jax.tree.map(lambda s: jnp.zeros(s.shape, s.dtype), shapes)

    return lax.cond(live, stage, never, *operands)


def on_device(
    frames, grad_out, w_in, conv_kernel, conv_bias, w_out, seg_lengths, seg_owner, slot_device
):
    count_dev = lax.axis_size("dp")
    rows, width = frames.shape
    ch = w_out.shape[0]
    scale = 1.0 / math.sqrt(rows * count_dev)
    deep = width // count_dev
    w_flat = w_in.reshape(width, 2 * ch)
    consts = tables()
    shared = (seg_lengths, frames, grad_out, w_flat, w_out, conv_kernel, conv_bias, consts)
    quarter = (rows - ROWS0) // 2

    def turn(d):
        return lambda m: (m + d) % 4

    def mine(m):
        return m

    def other(m):
        return far(near(m))

    gp0, act0, sum0, keep0, near0, far0, back0 = chunk_call(
        0, ROWS0,
        [(0, ROWS0, [turn(d)], F32 if d == 0 else BF16) for d in range(4)],
        None, *shared,
    )

    def ring(d):
        return [(i, (i + d) % 4) for i in range(4)]

    live = seg_lengths[0, 0] > 0

    def zeroth_stage(near0, far0, back0, gp0, act0, sum0, *shared):
        shared = shared[:7] + (shared[7:],)
        return (
            lax.ppermute(near0, "mp", ring(1)),
            lax.ppermute(far0, "mp", ring(2)),
            lax.ppermute(back0, "mp", ring(3)),
            *chunk_call(
                ROWS0, rows - ROWS0,
                [
                    (0, quarter, [near, other], BF16),
                    (quarter, quarter, [far, other], BF16),
                    (0, quarter, [mine, far], F32),
                    (quarter, quarter, [mine, near], F32),
                ],
                (gp0, act0, sum0), *shared,
            ),
        )

    near0, far0, back0, gp1, act1, small, send_a, send_b, keep_a, keep_b = zeroth_stage(
        near0, far0, back0, gp0, act0, sum0, *shared[:7], *consts
    )
    pair = [(i, i ^ 1) for i in range(4)]
    cross = [(i, 3 - i) for i in range(4)]
    first_a = lax.ppermute(send_a, "mp", pair)
    first_b = lax.ppermute(send_b, "mp", cross)
    wide = 3 * ch

    def weight_stage(frames, grad_out, gp0, gp1, act0, act1, small, keep0, near0, far0, back0):
        small_got = move(small)
        keep, send = weight_call(deep, frames, grad_out, gp0, gp1, act0, act1)
        got = move(send)
        (held0,) = sum_call(
            zero_sum_kernel, "zero_sum", TINY, [jax.ShapeDtypeStruct(keep0.shape, BF16)],
            keep0, near0, far0, back0, after=(keep,),
        )
        sums = sum_call(
            core_sum_kernel, "core_sum", TINY, halves(8, deep, wide, small), keep, got, small, small_got
        )
        return held0, *sums

    def last_stage(send_a, send_b):
        return lax.ppermute(send_a, "mp", cross), lax.ppermute(send_b, "mp", pair)

    def first_stage(send_a, send_b, keep_a, keep_b, *operands):
        first_a = lax.ppermute(send_a, "mp", pair)
        first_b = lax.ppermute(send_b, "mp", cross)
        held0, own_x, own_y, send_x, send_y, small = together(live, weight_stage, *operands)
        got_x, got_y = move(send_x, fx=near), move(send_y, fy=near)
        send_a, send_b = pass_call(keep_a, keep_b, first_a, first_b)
        last_a, last_b = together(live, last_stage, send_a, send_b)
        return first_a, first_b, held0, own_x, own_y, small, got_x, got_y, last_a, last_b

    def third_stage(send_x, send_y, *operands):
        got_x, got_y = move(send_x, fy=near), move(send_y, fx=near)
        return got_x, got_y, pick_call(*operands)

    first_a, first_b, held0, own_x, own_y, small, got_x, got_y, last_a, last_b = first_stage(
        send_a, send_b, keep_a, keep_b,
        frames, grad_out, gp0, gp1, act0, act1, small, keep0, near0, far0, back0,
    )
    own_x, own_y, send_x, send_y, small = sum_call(
        half_sum_kernel, "half_sum", TINY, halves(4, deep, wide, small), own_x, own_y, small, got_x, got_y
    )
    got_x, got_y, outgoing = together(
        live, third_stage, send_x, send_y,
        seg_lengths, seg_owner, held0, keep_a, keep_b, first_a, first_b, last_a, last_b,
    )
    received = lax.all_to_all(outgoing, "dp", split_axis=0, concat_axis=0, tiled=True)
    dx_frames, done = order_call(slot_device, received)
    own, small, *sends = sum_call(
        square_sum_kernel, "square_sum", TINY,
        [jax.ShapeDtypeStruct((deep, wide), F32), jax.ShapeDtypeStruct(small.shape, F32)]
        + [jax.ShapeDtypeStruct((deep, wide + 2 * ch), BF16)] * 3,
        own_x, own_y, small, got_x, got_y,
    )
    grad_w_in, grad_w_out, grad_kernel, grad_bias = sum_call(
        lambda *refs: last_sum_kernel(scale, *refs), "last_sum", TINY,
        [
            jax.ShapeDtypeStruct((deep, 2, ch), F32),
            jax.ShapeDtypeStruct((deep, ch), F32),
            jax.ShapeDtypeStruct((TAPS, ch), F32),
            jax.ShapeDtypeStruct((ch,), F32),
        ],
        own, small, move(sends[2], fx=far, fy=far), move(sends[0], fx=far), move(sends[1], fy=far),
        after=(done,),
    )
    return dx_frames, grad_w_in, grad_w_out.T, grad_kernel, grad_bias


def solution(mesh):
    return jax.shard_map(
        on_device,
        mesh=mesh,
        in_specs=(
            P("dp", None),
            P("dp", None),
            P(None, None, "mp"),
            P(None, "mp"),
            P("mp"),
            P("mp", None),
            P("dp", None),
            P("dp", None),
            P("dp", None),
        ),
        out_specs=(P("dp", None, "mp"), P("dp", None, "mp"), P("mp", "dp"), P(None, "mp"), P("mp")),
        check_vma=False,
    )
```

```python
import math

import jax
import jax.numpy as jnp
import numpy as np
from jax import lax
from jax.experimental import pallas as pl
from jax.experimental.pallas import tpu as pltpu
from jax.sharding import PartitionSpec as P

TAPS = 31
MAXLEN = 72
REACH = 15
WIN = 80
POINTS = 87
MAIN = 40
EDGE = 4
FREQ = 2 * (MAIN + EDGE)
MARGIN = 96
ROWS0 = 576
SEGS = 32
GROUP = 5
PICKS = 8
MIB = 1024 * 1024
TINY = pl.CostEstimate(flops=10**6, bytes_accessed=10**5, transcendentals=0)
LONG = pl.CostEstimate(flops=10**6, bytes_accessed=6 * 10**7, transcendentals=0)
F32, BF16 = jnp.float32, jnp.bfloat16
NT = (((1,), (1,)), ((), ()))
TN = (((0,), (0,)), ((), ()))


def tables():
    f = np.arange(MAIN + EDGE)[:, None]
    scale = np.where(f == 0, 1.0 / POINTS, 2.0 / POINTS)

    def waves(at, edge_sign):
        ang = 2 * np.pi * ((f * at[None, :]) % POINTS) / POINTS
        cos, sin = np.cos(ang), np.sin(ang)
        return cos[:MAIN], sin[:MAIN], cos[MAIN:], edge_sign * sin[MAIN:]

    rows = np.arange(WIN)
    shift = np.arange(TAPS) - REACH
    fwd = np.concatenate(waves(rows, 1), 0)
    weight = np.concatenate([scale[:MAIN]] * 2 + [scale[MAIN:]] * 2, 0)
    inv = (weight * fwd).T
    c, s, c4, s4 = waves(shift, 1)
    taps = np.concatenate([c, s, c4, c4, s4, -s4], 0)
    main, edge = scale[:MAIN], scale[MAIN:]
    back = np.concatenate([main * c, -main * s, edge * c4, edge * c4, -edge * s4, edge * s4], 0).T

    def split(table):
        high = table.astype(BF16).astype(np.float32)
        low = (table - high).astype(BF16).astype(np.float32)
        return np.concatenate([high, low, high], 1)

    return (
        jnp.asarray(split(fwd), BF16),
        jnp.asarray(split(inv)[:, : 2 * FREQ + 2 * MAIN], BF16),
        jnp.asarray(taps, F32),
        jnp.asarray(back, F32),
    )


def aligned(start, rows):
    base = pl.multiple_of(lax.div(start, rows) * rows, rows)
    return base, start - base


def pieces(x):
    high = x.astype(BF16)
    return jnp.concatenate([high, high, (x - high.astype(F32)).astype(BF16)], 0)


def uneven_pieces(x, rows):
    high = x.astype(BF16).astype(F32)
    return jnp.concatenate(
        [jnp.concatenate([high, high], 0).astype(BF16), (x - high)[:rows].astype(BF16)], 0
    )


def turned(x):
    return jnp.concatenate([x[EDGE:], x[:EDGE]], 0)


def chunk_kernel(first, rows, load, blocks, last, halves, *refs):
    (len_ref, frames_hbm, gout_hbm, w_ref, wout_ref, taps_ref, bias_ref,
     fwd_ref, inv_ref, tap_table_ref, back_table_ref) = refs[:11]
    refs = refs[11:]
    if first:
        gp_prev_hbm, act_prev_hbm, sum_prev = refs[:3]
        refs = refs[3:]
        gp_prev, act_prev, tail_sem = refs[-3:]
        refs = refs[:-3]
    gp_ref, act_ref, sum_ref = refs[:3]
    outs = refs[3 : 3 + len(halves)]
    fr, go, gsig, gated, gsw, conv, gc, spec, kf, acc, f_sem, g_sem = refs[3 + len(halves) :]
    ch = wout_ref.shape[0]
    block = load // blocks

    def copy(hbm, vmem, sem, i):
        src = pl.ds(pl.multiple_of(first + i * block, 16), block)
        dst = pl.ds(pl.multiple_of(i * block, 16), block)
        return pltpu.make_async_copy(hbm.at[src], vmem.at[dst], sem.at[i])

    if first:
        at = pl.ds(gp_prev_hbm.shape[0] - MARGIN, MARGIN)
        tails = [
            pltpu.make_async_copy(gp_prev_hbm.at[at], gp_prev, tail_sem.at[0]),
            pltpu.make_async_copy(act_prev_hbm.at[at], act_prev, tail_sem.at[1]),
        ]
        for tail in tails:
            tail.start()
    for i in range(blocks):
        copy(frames_hbm, fr, f_sem, i).start()
        copy(gout_hbm, go, g_sem, i).start()

    beyond = pl.ds(load, WIN)
    gated[beyond, :] = jnp.zeros((WIN, ch), F32)
    gc[beyond, :] = jnp.zeros((WIN, ch), F32)
    conv[...] = jnp.zeros_like(conv)
    kf[...] = jnp.dot(
        tap_table_ref[...], taps_ref[...],
        precision=lax.Precision.HIGHEST, preferred_element_type=F32,
    )
    acc[...] = sum_prev[...] if first else jnp.zeros_like(acc)

    def before(state):
        return state[1] < first

    def skip(state):
        return state[0] + 1, state[1] + len_ref[0, state[0]]

    k0, s0 = lax.while_loop(before, skip, (jnp.int32(0), jnp.int32(0)))
    s0 = s0 - first

    def project(i, carry):
        at = pl.ds(pl.multiple_of(i * block, 16), block)
        copy(frames_hbm, fr, f_sem, i).wait()
        both = jnp.dot(fr[at, :], w_ref[...], preferred_element_type=F32)
        sig = jax.nn.sigmoid(both[:, ch:])
        gsig[at, :] = sig
        gated[at, :] = both[:, :ch] * sig
        copy(gout_hbm, go, g_sem, i).wait()
        gsw[at, :] = lax.dot_general(go[at, :], wout_ref[...], NT, preferred_element_type=F32)
        return carry

    lax.fori_loop(0, blocks, project, 0)

    row = lax.broadcasted_iota(jnp.int32, (WIN, 128), 0)
    row8 = lax.broadcasted_iota(jnp.int32, (8, ch), 0)

    def spectra(src, places):
        parts = []
        for base, off, length in places:
            keep = (row >= off) & (row < off + length)
            for lane in range(0, ch, 128):
                x = src[pl.ds(base, WIN), lane : lane + 128]
                parts.append(pieces(jnp.where(keep, x, 0.0)))
        both = jnp.dot(fwd_ref[...], jnp.concatenate(parts, 1), preferred_element_type=F32)
        return [both[:, j * ch : (j + 1) * ch] for j in range(len(places))]

    def inverses(specs):
        parts = [uneven_pieces(jnp.concatenate(p, 0), 2 * MAIN) for p in specs]
        both = jnp.dot(inv_ref[...], jnp.concatenate(parts, 1), preferred_element_type=F32)
        return [both[:, j * ch : (j + 1) * ch] for j in range(len(specs))]

    main, sine, edge = slice(0, MAIN), slice(MAIN, 2 * MAIN), slice(2 * MAIN, FREQ)

    def put(out, base, off):
        head = pl.ds(base, 8)
        conv[head, :] = jnp.where(row8 >= off, out[:8], conv[head, :])
        conv[pl.ds(base + 8, WIN - 8), :] = out[8:]

    def group_of(start, k):
        places = []
        for j in range(GROUP):
            live = (start < rows) & (k + j < SEGS)
            length = jnp.where(live, len_ref[0, jnp.minimum(k + j, SEGS - 1)], 0)
            base, off = aligned(jnp.where(live, start, load), 8)
            places.append((base, off, length))
            start = start + length
        return places, start

    def more(state):
        return (state[1] < rows) & (state[0] < SEGS)

    def forward(state):
        k, start = state
        places, start = group_of(start, k)
        kc, ks, ke, kt = kf[main], kf[sine], kf[edge], kf[FREQ:]
        specs = []
        for i, s in enumerate(spectra(gated, places)):
            spec[k - k0 + i] = s
            gr, gi, ge = s[main], s[sine], s[edge]
            specs.append((kc * gr + ks * gi, kc * gi - ks * gr, ke * ge + kt * turned(ge)))
        results = inverses(specs)
        for (base, off, length), out in zip(places, results):
            put(out, base, off)
        return k + GROUP, start

    lax.while_loop(more, forward, (k0, s0))

    bias = bias_ref[...].reshape(1, ch)

    def swish(i, carry):
        at = pl.ds(pl.multiple_of(i * block, 16), block)
        c = conv[at, :] + bias
        sig = jax.nn.sigmoid(c)
        act_ref[at, :] = (c * sig).astype(BF16)
        gc[at, :] = gsw[at, :] * sig * (1.0 + c * (1.0 - sig))
        return carry

    lax.fori_loop(0, blocks, swish, 0)

    def backward(state):
        k, start = state
        places, start = group_of(start, k)
        kc, ks, ke, kt = kf[main], kf[sine], kf[edge], kf[FREQ:]
        sums = [jnp.zeros((n, ch), F32) for n in (MAIN, MAIN, 8, 8, 8)]
        specs = []
        for i, s in enumerate(spectra(gc, places)):
            cr, ci, ce = s[main], s[sine], s[edge]
            g = spec[k - k0 + i]
            gr, gi, ge = g[main], g[sine], g[edge]
            swapped = turned(ce)
            specs.append((kc * cr - ks * ci, kc * ci + ks * cr, ke * ce - kt * swapped))
            terms = (gr * cr + gi * ci, gr * ci - gi * cr, ge * ce, ge * swapped, s[:8])
            sums = [total + term for total, term in zip(sums, terms)]
        results = inverses(specs)
        at = 0
        for total in sums:
            acc[at : at + total.shape[0], :] += total
            at += total.shape[0]
        for (base, off, length), out in zip(places, results):
            put(out, base, off)
        return k + GROUP, start

    lax.while_loop(more, backward, (k0, s0))

    def project_back(i, carry):
        at = pl.ds(pl.multiple_of(i * block, 16), block)
        g = conv[at, :]
        sig = gsig[at, :]
        gp_ref[at, :ch] = (g * sig).astype(BF16)
        gp_ref[at, ch:] = (g * gated[at, :] * (1.0 - sig)).astype(BF16)
        return carry

    lax.fori_loop(0, blocks, project_back, 0)

    if first:
        for tail in tails:
            tail.wait()
        head = pl.ds(0, MARGIN)
        from_prev = lax.broadcasted_iota(jnp.int32, (MARGIN, 1), 0) < s0
        gp_ref[head, :] = jnp.where(
            from_prev, gp_prev[...].astype(F32), gp_ref[head, :].astype(F32)
        ).astype(BF16)
        act_ref[head, :] = jnp.where(
            from_prev, act_prev[...].astype(F32), act_ref[head, :].astype(F32)
        ).astype(BF16)

    mine = lax.axis_index("mp")
    for out, (start, size, picks) in zip(outs, halves):
        for j, pick in enumerate(picks):
            at = pl.ds(pl.multiple_of(pick(mine) * ch, ch), ch)
            out[:, j * ch : (j + 1) * ch] = lax.dot_general(
                gp_ref[start : start + size, :], w_ref[at, :], NT, preferred_element_type=F32
            ).astype(out.dtype)

    if last:
        taps_grad = jnp.dot(
            back_table_ref[...], acc[: FREQ + 8, :],
            precision=lax.Precision.HIGHEST, preferred_element_type=F32,
        )
        sum_ref[:TAPS, :] = taps_grad
        sum_ref[TAPS:, :] = acc[FREQ + 8 : FREQ + 9, :]
    else:
        sum_ref[...] = acc[...]


def chunk_call(first, rows, halves, prev, lengths, frames, grad_out, w_flat, w_out, taps, bias, consts):
    total, width = frames.shape
    ch = w_out.shape[0]
    last = first + rows == total
    load = rows if last else rows + MARGIN
    blocks = next(n for n in range(-(-load // 480), load) if load % (16 * n) == 0)
    vm = pl.BlockSpec(memory_space=pltpu.VMEM)
    hbm = pl.BlockSpec(memory_space=pl.ANY)
    sm = pl.BlockSpec(memory_space=pltpu.SMEM)
    operands = [lengths, frames, grad_out, w_flat, w_out, taps, bias, *consts]
    specs = [sm, hbm, hbm] + [vm] * 8
    if first:
        operands += prev
        specs += [hbm, hbm, vm]

    def body(*refs):
        chunk_kernel(first, rows, load, blocks, last, [h[:3] for h in halves], *refs)

    out_shape = [
        jax.ShapeDtypeStruct((load, 2 * ch), BF16),
        jax.ShapeDtypeStruct((load, ch), BF16),
        jax.ShapeDtypeStruct((TAPS + 1 if last else FREQ + 16, ch), F32),
    ] + [jax.ShapeDtypeStruct((size, len(picks) * ch), dtype) for _, size, picks, dtype in halves]
    return pl.pallas_call(
        body,
        out_shape=out_shape,
        in_specs=specs,
        out_specs=[vm] * len(out_shape),
        scratch_shapes=[
            pltpu.VMEM((load, width), BF16),
            pltpu.VMEM((load, width), BF16),
            pltpu.VMEM((load, ch), F32),
            pltpu.VMEM((load + WIN, ch), F32),
            pltpu.VMEM((load, ch), F32),
            pltpu.VMEM((load + WIN, ch), F32),
            pltpu.VMEM((load + WIN, ch), F32),
            pltpu.VMEM((SEGS + GROUP, FREQ, ch), F32),
            pltpu.VMEM((FREQ + 8, ch), F32),
            pltpu.VMEM((FREQ + 16, ch), F32),
            pltpu.SemaphoreType.DMA((blocks,)),
            pltpu.SemaphoreType.DMA((blocks,)),
        ] + ([
            pltpu.VMEM((MARGIN, 2 * ch), BF16),
            pltpu.VMEM((MARGIN, ch), BF16),
            pltpu.SemaphoreType.DMA((2,)),
        ] if first else []),
        compiler_params=pltpu.CompilerParams(vmem_limit_bytes=40 * MIB),
        cost_estimate=pl.CostEstimate(flops=2 * 10**10, bytes_accessed=2 * 10**7, transcendentals=0),
        name="chunk%d" % first,
    )(*operands)


def zero_sum_kernel(keep0, near0, far0, back0, after, held_ref):
    held_ref[...] = (
        keep0[...] + near0[...].astype(F32) + far0[...].astype(F32) + back0[...].astype(F32)
    ).astype(BF16)


def pass_kernel(keep_a, keep_b, first_a, first_b, out_a, out_b):
    out_a[...] = (keep_a[...] + first_a[...].astype(F32)).astype(BF16)
    out_b[...] = (keep_b[...] + first_b[...].astype(F32)).astype(BF16)


def pass_call(keep_a, keep_b, first_a, first_b):
    half, ch = keep_a.shape[0], keep_a.shape[1] // 2
    out = jax.ShapeDtypeStruct((half, ch), BF16)
    return pl.pallas_call(
        pass_kernel,
        grid=(1,),
        out_shape=(out, out),
        in_specs=[pl.BlockSpec((half, ch), lambda i: (0, 1))] * 4,
        out_specs=[pl.BlockSpec((half, ch), lambda i: (0, 0))] * 2,
        compiler_params=pltpu.CompilerParams(vmem_limit_bytes=16 * MIB),
        cost_estimate=TINY,
        name="pass",
    )(keep_a, keep_b, first_a, first_b)


def pick_kernel(
    len_ref, owner_ref, held0, keep_a, keep_b, first_a, first_b, last_a, last_b, out_ref, held
):
    rows0, ch = held0.shape
    half = last_a.shape[0]
    rows = rows0 + 2 * half
    held[pl.ds(0, rows0), :] = held0[...]
    for at, keep, one, two in ((rows0, keep_a, first_a, last_a), (rows0 + half, keep_b, first_b, last_b)):
        held[pl.ds(at, half), :] = (keep[...] + one[...].astype(F32) + two[...].astype(F32)).astype(BF16)
    held[pl.ds(rows, MARGIN), :] = jnp.zeros((MARGIN, ch), BF16)
    row = lax.broadcasted_iota(jnp.int32, (MAXLEN, MARGIN), 0)
    lane = lax.broadcasted_iota(jnp.int32, (MAXLEN, MARGIN), 1)

    def pick(i, start):
        for j in range(PICKS):
            k = i * PICKS + j
            length = len_ref[0, k]
            base, off = aligned(start, 16)
            hot = jnp.where((lane == row + off) & (row < length), 1.0, 0.0).astype(BF16)
            out_ref[owner_ref[0, k]] = jnp.dot(
                hot, held[pl.ds(base, MARGIN), :], preferred_element_type=F32
            ).astype(BF16)
            start = start + length
        return start

    lax.fori_loop(0, SEGS // PICKS, pick, jnp.int32(0))


def pick_call(lengths, owners, held0, keep_a, keep_b, first_a, first_b, last_a, last_b):
    rows0, ch = held0.shape
    half = last_a.shape[0]
    sm = pl.BlockSpec(memory_space=pltpu.SMEM)
    part = pl.BlockSpec((half, ch), lambda i: (0, 0))
    return pl.pallas_call(
        pick_kernel,
        grid=(1,),
        out_shape=jax.ShapeDtypeStruct((SEGS, MAXLEN, ch), BF16),
        in_specs=[sm, sm, pl.BlockSpec((rows0, ch), lambda i: (0, 0))] + [part] * 6,
        out_specs=pl.BlockSpec((SEGS, MAXLEN, ch), lambda i: (0, 0, 0)),
        scratch_shapes=[pltpu.VMEM((rows0 + 2 * half + MARGIN, ch), BF16)],
        compiler_params=pltpu.CompilerParams(vmem_limit_bytes=24 * MIB),
        cost_estimate=TINY,
        name="pick",
    )(lengths, owners, held0, keep_a, keep_b, first_a, first_b, last_a, last_b)


def order_kernel(slot_ref, src, dst, done_ref, sem):
    def copy(u):
        return pltpu.make_async_copy(src.at[slot_ref[0, u]], dst.at[u], sem.at[u])

    for u in range(SEGS):
        copy(u).start()
    for u in range(SEGS):
        copy(u).wait()
    done_ref[...] = jnp.zeros_like(done_ref)


def order_call(slots, received):
    return pl.pallas_call(
        order_kernel,
        out_shape=(
            jax.ShapeDtypeStruct(received.shape, received.dtype),
            jax.ShapeDtypeStruct((8, 128), F32),
        ),
        in_specs=[pl.BlockSpec(memory_space=pltpu.SMEM), pl.BlockSpec(memory_space=pltpu.VMEM)],
        out_specs=(pl.BlockSpec(memory_space=pl.ANY), pl.BlockSpec(memory_space=pltpu.VMEM)),
        scratch_shapes=[pltpu.SemaphoreType.DMA((SEGS,))],
        compiler_params=pltpu.CompilerParams(vmem_limit_bytes=16 * MIB),
        cost_estimate=TINY,
        name="order",
    )(slots, received)


COLS = 4
PARTS = 1


def weight_kernel(
    deep, frames_hbm, gout_hbm, gp0_hbm, gp1_hbm, act0_hbm, act1_hbm, keep_ref, send_ref,
    fr, go, gp, act, held, f_sem, g_sem, p_sem,
):
    core = lax.rem(lax.axis_index("dp"), 2)
    total, width = frames_hbm.shape
    cols = width // COLS
    rows1 = gp1_hbm.shape[0]
    rows0 = total - rows1
    wide = gp.shape[1]

    def read(hbm, vmem, sem):
        step = total // PARTS
        return [
            pltpu.make_async_copy(hbm.at[pl.ds(i * step, step)], vmem.at[pl.ds(i * step, step)], sem.at[i])
            for i in range(PARTS)
        ]

    def pair(one, two, out, at):
        return [
            pltpu.make_async_copy(one.at[pl.ds(0, rows0)], out.at[pl.ds(0, rows0)], p_sem.at[at]),
            pltpu.make_async_copy(two, out.at[pl.ds(rows0, rows1)], p_sem.at[at + 1]),
        ]

    first = pair(act0_hbm, act1_hbm, act, 0) + read(gout_hbm, go, g_sem)
    second = pair(gp0_hbm, gp1_hbm, gp, 2) + read(frames_hbm, fr, f_sem)
    for copy in first + second:
        copy.start()
    pairs = cols // (2 * deep)
    step = total // PARTS

    def share(j, at):
        for i in range(pairs):
            own = pl.ds(pl.multiple_of(j * cols + (2 * i + core) * deep, 16), deep)
            other = pl.ds(pl.multiple_of(j * cols + (2 * i + 1 - core) * deep, 16), deep)
            keep_ref[j * pairs + i, :, at] = held[own, at]
            send_ref[j * pairs + i, :, at] = held[other, at].astype(BF16)

    out_cols, in_cols = slice(wide, None), slice(0, wide)
    for copy in first[:2]:
        copy.wait()
    for p in range(PARTS):
        first[2 + p].wait()
        rows = slice(p * step, (p + 1) * step)
        for j in range(COLS):
            here = slice(j * cols, (j + 1) * cols)
            term = lax.dot_general(go[rows, here], act[rows, :], TN, preferred_element_type=F32)
            held[here, out_cols] = term if p == 0 else held[here, out_cols] + term
    for copy in second:
        copy.wait()
    for j in range(COLS):
        here = slice(j * cols, (j + 1) * cols)
        held[here, in_cols] = lax.dot_general(fr[:, here], gp[...], TN, preferred_element_type=F32)
        share(j, out_cols)
        share(j, in_cols)


def weight_call(deep, frames, grad_out, gp0, gp1, act0, act1):
    total, width = frames.shape
    ch = act0.shape[1]
    pairs = width // (2 * deep)
    vm = pl.BlockSpec(memory_space=pltpu.VMEM)
    return pl.pallas_call(
        lambda *refs: weight_kernel(deep, *refs),
        out_shape=(
            jax.ShapeDtypeStruct((pairs, deep, 3 * ch), F32),
            jax.ShapeDtypeStruct((pairs, deep, 3 * ch), BF16),
        ),
        in_specs=[pl.BlockSpec(memory_space=pl.ANY)] * 6,
        out_specs=(vm, vm),
        scratch_shapes=[
            pltpu.VMEM((total, width), BF16),
            pltpu.VMEM((total, width), BF16),
            pltpu.VMEM((total, 2 * ch), BF16),
            pltpu.VMEM((total, ch), BF16),
            pltpu.VMEM((width, 3 * ch), F32),
            pltpu.SemaphoreType.DMA((PARTS,)),
            pltpu.SemaphoreType.DMA((PARTS,)),
            pltpu.SemaphoreType.DMA((4,)),
        ],
        compiler_params=pltpu.CompilerParams(vmem_limit_bytes=40 * MIB),
        cost_estimate=pl.CostEstimate(flops=11 * 10**9, bytes_accessed=2 * 10**7, transcendentals=0),
        name="weight",
    )(frames, grad_out, gp0, gp1, act0, act1)


CUT = 640


def put_small(out, at, x):
    taps, ch = x.shape
    high = x.astype(BF16)
    for j, part in enumerate((high, (x - high.astype(F32)).astype(BF16))):
        out[at + j] = jnp.zeros(out.shape[1:], out.dtype)
        out[at + j, :taps, :ch] = part


def get_small(ref, at, shape):
    taps, ch = shape
    return ref[at, :taps, :ch].astype(F32) + ref[at + 1, :taps, :ch].astype(F32)


def places():
    dp = lax.axis_index("dp")
    return lax.div(dp, 8), lax.rem(lax.div(dp, 2), 4)


def near(v):
    return v ^ 1


def far(v):
    return 3 - v


def both_ways():
    dp = lax.axis_index("dp")
    x, y = lax.div(dp, 8), lax.rem(lax.div(dp, 2), 4)
    return (slice(0, CUT), x, y, True), (slice(CUT, None), y, x, False)


def core_sum_kernel(keep, got, small, small_got, *outs):
    small_total = small[...] + small_got[...]
    outs[4][...] = small_total
    for i, (cols, a, b, x_first) in enumerate(both_ways()):
        for j in range(4):
            for where, out, slot in ((a, outs[i], 0), (far(a), outs[i], 4), (near(a), outs[2 + i], 0), (far(near(a)), outs[2 + i], 4)):
                at = where * 4 + j if x_first else j * 4 + where
                total = keep[at, :, cols] + got[at, :, cols].astype(F32)
                out[slot + j] = total.astype(out.dtype)
    put_small(outs[3], 8, small_total)


def half_sum_kernel(own_x, own_y, small, got_x, got_y, *outs):
    small_total = small[...] + get_small(got_y, 8, small.shape)
    outs[4][...] = small_total
    for i, ((cols, a, b, x_first), own, got) in enumerate(zip(both_ways(), (own_x, own_y), (got_x, got_y))):
        for s in range(2):
            for j, where in enumerate((b, far(b))):
                at = 4 * s + where
                outs[i][2 * s + j] = own[at] + got[at].astype(F32)
            for j, where in enumerate((near(b), far(near(b)))):
                at = 4 * s + where
                outs[2 + i][2 * s + j] = (own[at] + got[at].astype(F32)).astype(BF16)
    put_small(outs[3], 4, small_total)


def square_sum_kernel(own_x, own_y, small, got_x, got_y, own_ref, small_out, *outs):
    taps, ch = small.shape
    small_total = small[...] + get_small(got_y, 4, small.shape)
    small_out[...] = small_total
    high = small_total.astype(BF16)
    low = (small_total - high.astype(F32)).astype(BF16)
    for out, at_x, at_y in ((own_ref, 0, 0), (outs[0], 2, 1), (outs[1], 1, 2), (outs[2], 3, 3)):
        out[:, :CUT] = (own_x[at_x] + got_x[at_x].astype(F32)).astype(out.dtype)
        out[:, CUT : 3 * ch] = (own_y[at_y] + got_y[at_y].astype(F32)).astype(out.dtype)
    for out in outs:
        out[:, 3 * ch :] = jnp.zeros((out.shape[0], 2 * ch), BF16)
        out[:taps, 3 * ch : 4 * ch] = high
        out[:taps, 4 * ch :] = low


def last_sum_kernel(scale, own, small, r1, r2, r3, after, w_in_out, w_out_out, kernel_out, bias_out):
    taps, ch = small.shape
    total, small_total = own[...], small[...]
    for r in (r1, r2, r3):
        total = total + r[:, : 3 * ch].astype(F32)
        small_total = small_total + r[:taps, 3 * ch : 4 * ch].astype(F32) + r[:taps, 4 * ch :].astype(F32)
    total, small_total = total * scale, small_total * scale
    w_in_out[:, 0, :] = total[:, :ch]
    w_in_out[:, 1, :] = total[:, ch : 2 * ch]
    w_out_out[...] = total[:, 2 * ch :]
    kernel_out[...] = small_total[:TAPS]
    bias_out[...] = small_total[TAPS:].reshape(ch)


def sum_call(kernel, name, cost, out_shape, *operands, after=()):
    vm = pl.BlockSpec(memory_space=pltpu.VMEM)
    return pl.pallas_call(
        kernel,
        out_shape=out_shape,
        in_specs=[vm] * len(operands) + [pl.BlockSpec(memory_space=pl.ANY)] * len(after),
        out_specs=[vm] * len(out_shape),
        compiler_params=pltpu.CompilerParams(vmem_limit_bytes=24 * MIB),
        cost_estimate=cost,
        name=name,
    )(*operands, *after)


def halves(n, deep, wide, small):
    return [
        jax.ShapeDtypeStruct((n, deep, CUT), F32),
        jax.ShapeDtypeStruct((n, deep, wide - CUT), F32),
        jax.ShapeDtypeStruct((n, deep, CUT), BF16),
        jax.ShapeDtypeStruct((n + 2, deep, wide - CUT), BF16),
        jax.ShapeDtypeStruct(small.shape, F32),
    ]


def move(array, fx=None, fy=None):
    def to(i):
        x, y, c = i // 8, i // 2 % 4, i % 2
        if fx is None and fy is None:
            c ^= 1
        return ((fx(x) if fx else x) * 4 + (fy(y) if fy else y)) * 2 + c

    return lax.ppermute(array, "dp", [(i, to(i)) for i in range(lax.axis_size("dp"))])


def together(live, stage, *operands):
    shapes = jax.eval_shape(stage, *operands)

    def never(*_):
        return jax.tree.map(lambda s: jnp.zeros(s.shape, s.dtype), shapes)

    return lax.cond(live, stage, never, *operands)


def until_owners(
    frames, grad_out, w_in, conv_kernel, conv_bias, w_out, seg_lengths, seg_owner
):
    count_dev = lax.axis_size("dp")
    rows, width = frames.shape
    ch = w_out.shape[0]
    scale = 1.0 / math.sqrt(rows * count_dev)
    deep = width // count_dev
    w_flat = w_in.reshape(width, 2 * ch)
    consts = tables()
    shared = (seg_lengths, frames, grad_out, w_flat, w_out, conv_kernel, conv_bias, consts)
    quarter = (rows - ROWS0) // 2

    def turn(d):
        return lambda m: (m + d) % 4

    def mine(m):
        return m

    def other(m):
        return far(near(m))

    gp0, act0, sum0, keep0, near0, far0, back0 = chunk_call(
        0, ROWS0,
        [(0, ROWS0, [turn(d)], F32 if d == 0 else BF16) for d in range(4)],
        None, *shared,
    )

    def ring(d):
        return [(i, (i + d) % 4) for i in range(4)]

    live = seg_lengths[0, 0] > 0

    def zeroth_stage(near0, far0, back0, gp0, act0, sum0, *shared):
        shared = shared[:7] + (shared[7:],)
        return (
            lax.ppermute(near0, "mp", ring(1)),
            lax.ppermute(far0, "mp", ring(2)),
            lax.ppermute(back0, "mp", ring(3)),
            *chunk_call(
                ROWS0, rows - ROWS0,
                [
                    (0, quarter, [near, other], BF16),
                    (quarter, quarter, [far, other], BF16),
                    (0, quarter, [mine, far], F32),
                    (quarter, quarter, [mine, near], F32),
                ],
                (gp0, act0, sum0), *shared,
            ),
        )

    near0, far0, back0, gp1, act1, small, send_a, send_b, keep_a, keep_b = zeroth_stage(
        near0, far0, back0, gp0, act0, sum0, *shared[:7], *consts
    )
    pair = [(i, i ^ 1) for i in range(4)]
    cross = [(i, 3 - i) for i in range(4)]
    first_a = lax.ppermute(send_a, "mp", pair)
    first_b = lax.ppermute(send_b, "mp", cross)
    wide = 3 * ch

    def weight_stage(frames, grad_out, gp0, gp1, act0, act1, small, keep0, near0, far0, back0):
        small_got = move(small)
        keep, send = weight_call(deep, frames, grad_out, gp0, gp1, act0, act1)
        got = move(send)
        (held0,) = sum_call(
            zero_sum_kernel, "zero_sum", TINY, [jax.ShapeDtypeStruct(keep0.shape, BF16)],
            keep0, near0, far0, back0, after=(keep,),
        )
        sums = sum_call(
            core_sum_kernel, "core_sum", TINY, halves(8, deep, wide, small), keep, got, small, small_got
        )
        return held0, *sums

    def last_stage(send_a, send_b):
        return lax.ppermute(send_a, "mp", cross), lax.ppermute(send_b, "mp", pair)

    def first_stage(send_a, send_b, keep_a, keep_b, *operands):
        first_a = lax.ppermute(send_a, "mp", pair)
        first_b = lax.ppermute(send_b, "mp", cross)
        held0, own_x, own_y, send_x, send_y, small = together(live, weight_stage, *operands)
        got_x, got_y = move(send_x, fx=near), move(send_y, fy=near)
        send_a, send_b = pass_call(keep_a, keep_b, first_a, first_b)
        last_a, last_b = last_stage(send_a, send_b)
        return first_a, first_b, held0, own_x, own_y, small, got_x, got_y, last_a, last_b

    def third_stage(send_x, send_y, *operands):
        got_x, got_y = move(send_x, fy=near), move(send_y, fx=near)
        return got_x, got_y, pick_call(*operands)

    first_a, first_b, held0, own_x, own_y, small, got_x, got_y, last_a, last_b = first_stage(
        send_a, send_b, keep_a, keep_b,
        frames, grad_out, gp0, gp1, act0, act1, small, keep0, near0, far0, back0,
    )
    own_x, own_y, send_x, send_y, small = sum_call(
        half_sum_kernel, "half_sum", TINY, halves(4, deep, wide, small), own_x, own_y, small, got_x, got_y
    )
    got_x, got_y, outgoing = third_stage(
        send_x, send_y,
        seg_lengths, seg_owner, held0, keep_a, keep_b, first_a, first_b, last_a, last_b,
    )
    return outgoing, own_x, own_y, small, got_x, got_y


def on_device(
    frames, grad_out, w_in, conv_kernel, conv_bias, w_out, seg_lengths, seg_owner, slot_device
):
    rows, width = frames.shape
    ch = w_out.shape[0]
    count_dev = lax.axis_size("dp")
    scale = 1.0 / math.sqrt(rows * count_dev)
    deep, wide = width // count_dev, 3 * ch
    outgoing, own_x, own_y, small, got_x, got_y = together(
        seg_lengths[0, 0] > 0, until_owners,
        frames, grad_out, w_in, conv_kernel, conv_bias, w_out, seg_lengths, seg_owner,
    )
    received = lax.all_to_all(outgoing, "dp", split_axis=0, concat_axis=0, tiled=True)
    dx_frames, done = order_call(slot_device, received)
    own, small, *sends = sum_call(
        square_sum_kernel, "square_sum", TINY,
        [jax.ShapeDtypeStruct((deep, wide), F32), jax.ShapeDtypeStruct(small.shape, F32)]
        + [jax.ShapeDtypeStruct((deep, wide + 2 * ch), BF16)] * 3,
        own_x, own_y, small, got_x, got_y,
    )
    grad_w_in, grad_w_out, grad_kernel, grad_bias = sum_call(
        lambda *refs: last_sum_kernel(scale, *refs), "last_sum", TINY,
        [
            jax.ShapeDtypeStruct((deep, 2, ch), F32),
            jax.ShapeDtypeStruct((deep, ch), F32),
            jax.ShapeDtypeStruct((TAPS, ch), F32),
            jax.ShapeDtypeStruct((ch,), F32),
        ],
        own, small, move(sends[2], fx=far, fy=far), move(sends[0], fx=far), move(sends[1], fy=far),
        after=(done,),
    )
    return dx_frames, grad_w_in, grad_w_out.T, grad_kernel, grad_bias


def solution(mesh):
    return jax.shard_map(
        on_device,
        mesh=mesh,
        in_specs=(
            P("dp", None),
            P("dp", None),
            P(None, None, "mp"),
            P(None, "mp"),
            P("mp"),
            P("mp", None),
            P("dp", None),
            P("dp", None),
            P("dp", None),
        ),
        out_specs=(P("dp", None, "mp"), P("dp", None, "mp"), P("mp", "dp"), P(None, "mp"), P("mp")),
        check_vma=False,
    )
```

```python
import math

import jax
import jax.numpy as jnp
import numpy as np
from jax import lax
from jax.experimental import pallas as pl
from jax.experimental.pallas import tpu as pltpu
from jax.sharding import PartitionSpec as P

TAPS = 31
MAXLEN = 72
REACH = 15
WIN = 80
POINTS = 87
MAIN = 40
EDGE = 4
FREQ = 2 * (MAIN + EDGE)
MARGIN = 96
ROWS0 = 608
SEGS = 32
GROUP = 5
PICKS = 8
MIB = 1024 * 1024
TINY = pl.CostEstimate(flops=10**6, bytes_accessed=10**5, transcendentals=0)
LONG = pl.CostEstimate(flops=10**6, bytes_accessed=6 * 10**7, transcendentals=0)
F32, BF16 = jnp.float32, jnp.bfloat16
NT = (((1,), (1,)), ((), ()))
TN = (((0,), (0,)), ((), ()))


def tables():
    f = np.arange(MAIN + EDGE)[:, None]
    scale = np.where(f == 0, 1.0 / POINTS, 2.0 / POINTS)

    def waves(at, edge_sign):
        ang = 2 * np.pi * ((f * at[None, :]) % POINTS) / POINTS
        cos, sin = np.cos(ang), np.sin(ang)
        return cos[:MAIN], sin[:MAIN], cos[MAIN:], edge_sign * sin[MAIN:]

    rows = np.arange(WIN)
    shift = np.arange(TAPS) - REACH
    fwd = np.concatenate(waves(rows, 1), 0)
    weight = np.concatenate([scale[:MAIN]] * 2 + [scale[MAIN:]] * 2, 0)
    inv = (weight * fwd).T
    c, s, c4, s4 = waves(shift, 1)
    taps = np.concatenate([c, s, c4, c4, s4, -s4], 0)
    main, edge = scale[:MAIN], scale[MAIN:]
    back = np.concatenate([main * c, -main * s, edge * c4, edge * c4, -edge * s4, edge * s4], 0).T

    def split(table):
        high = table.astype(BF16).astype(np.float32)
        low = (table - high).astype(BF16).astype(np.float32)
        return np.concatenate([high, low, high], 1)

    return (
        jnp.asarray(split(fwd), BF16),
        jnp.asarray(split(inv)[:, : 2 * FREQ + 2 * MAIN], BF16),
        jnp.asarray(taps, F32),
        jnp.asarray(back, F32),
    )


def aligned(start, rows):
    base = pl.multiple_of(lax.div(start, rows) * rows, rows)
    return base, start - base


def pieces(x):
    high = x.astype(BF16)
    return jnp.concatenate([high, high, (x - high.astype(F32)).astype(BF16)], 0)


def uneven_pieces(x, rows):
    high = x.astype(BF16).astype(F32)
    return jnp.concatenate(
        [jnp.concatenate([high, high], 0).astype(BF16), (x - high)[:rows].astype(BF16)], 0
    )


def turned(x):
    return jnp.concatenate([x[EDGE:], x[:EDGE]], 0)


def chunk_kernel(first, rows, load, blocks, last, halves, *refs):
    (len_ref, frames_hbm, gout_hbm, w_ref, wout_ref, taps_ref, bias_ref,
     fwd_ref, inv_ref, tap_table_ref, back_table_ref) = refs[:11]
    refs = refs[11:]
    if first:
        gp_prev_hbm, act_prev_hbm, sum_prev = refs[:3]
        refs = refs[3:]
        gp_prev, act_prev, tail_sem = refs[-3:]
        refs = refs[:-3]
    gp_ref, act_ref, sum_ref = refs[:3]
    outs = refs[3 : 3 + len(halves)]
    fr, go, gsig, gated, gsw, conv, gc, spec, kf, acc, f_sem, g_sem = refs[3 + len(halves) :]
    ch = wout_ref.shape[0]
    block = load // blocks

    def copy(hbm, vmem, sem, i):
        src = pl.ds(pl.multiple_of(first + i * block, 16), block)
        dst = pl.ds(pl.multiple_of(i * block, 16), block)
        return pltpu.make_async_copy(hbm.at[src], vmem.at[dst], sem.at[i])

    if first:
        at = pl.ds(gp_prev_hbm.shape[0] - MARGIN, MARGIN)
        tails = [
            pltpu.make_async_copy(gp_prev_hbm.at[at], gp_prev, tail_sem.at[0]),
            pltpu.make_async_copy(act_prev_hbm.at[at], act_prev, tail_sem.at[1]),
        ]
        for tail in tails:
            tail.start()
    for i in range(blocks):
        copy(frames_hbm, fr, f_sem, i).start()
        copy(gout_hbm, go, g_sem, i).start()

    beyond = pl.ds(load, WIN)
    gated[beyond, :] = jnp.zeros((WIN, ch), F32)
    gc[beyond, :] = jnp.zeros((WIN, ch), F32)
    conv[...] = jnp.zeros_like(conv)
    kf[...] = jnp.dot(
        tap_table_ref[...], taps_ref[...],
        precision=lax.Precision.HIGHEST, preferred_element_type=F32,
    )
    acc[...] = sum_prev[...] if first else jnp.zeros_like(acc)

    def before(state):
        return state[1] < first

    def skip(state):
        return state[0] + 1, state[1] + len_ref[0, state[0]]

    k0, s0 = lax.while_loop(before, skip, (jnp.int32(0), jnp.int32(0)))
    s0 = s0 - first

    def project(i, carry):
        at = pl.ds(pl.multiple_of(i * block, 16), block)
        copy(frames_hbm, fr, f_sem, i).wait()
        both = jnp.dot(fr[at, :], w_ref[...], preferred_element_type=F32)
        sig = jax.nn.sigmoid(both[:, ch:])
        gsig[at, :] = sig
        gated[at, :] = both[:, :ch] * sig
        copy(gout_hbm, go, g_sem, i).wait()
        gsw[at, :] = lax.dot_general(go[at, :], wout_ref[...], NT, preferred_element_type=F32)
        return carry

    lax.fori_loop(0, blocks, project, 0)

    row = lax.broadcasted_iota(jnp.int32, (WIN, 128), 0)
    row8 = lax.broadcasted_iota(jnp.int32, (8, ch), 0)

    def spectra(src, places):
        parts = []
        for base, off, length in places:
            keep = (row >= off) & (row < off + length)
            for lane in range(0, ch, 128):
                x = src[pl.ds(base, WIN), lane : lane + 128]
                parts.append(pieces(jnp.where(keep, x, 0.0)))
        both = jnp.dot(fwd_ref[...], jnp.concatenate(parts, 1), preferred_element_type=F32)
        return [both[:, j * ch : (j + 1) * ch] for j in range(len(places))]

    def inverses(specs):
        parts = [uneven_pieces(jnp.concatenate(p, 0), 2 * MAIN) for p in specs]
        both = jnp.dot(inv_ref[...], jnp.concatenate(parts, 1), preferred_element_type=F32)
        return [both[:, j * ch : (j + 1) * ch] for j in range(len(specs))]

    main, sine, edge = slice(0, MAIN), slice(MAIN, 2 * MAIN), slice(2 * MAIN, FREQ)

    def put(out, base, off):
        head = pl.ds(base, 8)
        conv[head, :] = jnp.where(row8 >= off, out[:8], conv[head, :])
        conv[pl.ds(base + 8, WIN - 8), :] = out[8:]

    def group_of(start, k):
        places = []
        for j in range(GROUP):
            live = (start < rows) & (k + j < SEGS)
            length = jnp.where(live, len_ref[0, jnp.minimum(k + j, SEGS - 1)], 0)
            base, off = aligned(jnp.where(live, start, load), 8)
            places.append((base, off, length))
            start = start + length
        return places, start

    def more(state):
        return (state[1] < rows) & (state[0] < SEGS)

    def forward(state):
        k, start = state
        places, start = group_of(start, k)
        kc, ks, ke, kt = kf[main], kf[sine], kf[edge], kf[FREQ:]
        specs = []
        for i, s in enumerate(spectra(gated, places)):
            spec[k - k0 + i] = s
            gr, gi, ge = s[main], s[sine], s[edge]
            specs.append((kc * gr + ks * gi, kc * gi - ks * gr, ke * ge + kt * turned(ge)))
        results = inverses(specs)
        for (base, off, length), out in zip(places, results):
            put(out, base, off)
        return k + GROUP, start

    lax.while_loop(more, forward, (k0, s0))

    bias = bias_ref[...].reshape(1, ch)

    def swish(i, carry):
        at = pl.ds(pl.multiple_of(i * block, 16), block)
        c = conv[at, :] + bias
        sig = jax.nn.sigmoid(c)
        act_ref[at, :] = (c * sig).astype(BF16)
        gc[at, :] = gsw[at, :] * sig * (1.0 + c * (1.0 - sig))
        return carry

    lax.fori_loop(0, blocks, swish, 0)

    def backward(state):
        k, start = state
        places, start = group_of(start, k)
        kc, ks, ke, kt = kf[main], kf[sine], kf[edge], kf[FREQ:]
        sums = [jnp.zeros((n, ch), F32) for n in (MAIN, MAIN, 8, 8, 8)]
        specs = []
        for i, s in enumerate(spectra(gc, places)):
            cr, ci, ce = s[main], s[sine], s[edge]
            g = spec[k - k0 + i]
            gr, gi, ge = g[main], g[sine], g[edge]
            swapped = turned(ce)
            specs.append((kc * cr - ks * ci, kc * ci + ks * cr, ke * ce - kt * swapped))
            terms = (gr * cr + gi * ci, gr * ci - gi * cr, ge * ce, ge * swapped, s[:8])
            sums = [total + term for total, term in zip(sums, terms)]
        results = inverses(specs)
        at = 0
        for total in sums:
            acc[at : at + total.shape[0], :] += total
            at += total.shape[0]
        for (base, off, length), out in zip(places, results):
            put(out, base, off)
        return k + GROUP, start

    lax.while_loop(more, backward, (k0, s0))

    def project_back(i, carry):
        at = pl.ds(pl.multiple_of(i * block, 16), block)
        g = conv[at, :]
        sig = gsig[at, :]
        gp_ref[at, :ch] = (g * sig).astype(BF16)
        gp_ref[at, ch:] = (g * gated[at, :] * (1.0 - sig)).astype(BF16)
        return carry

    lax.fori_loop(0, blocks, project_back, 0)

    if first:
        for tail in tails:
            tail.wait()
        head = pl.ds(0, MARGIN)
        from_prev = lax.broadcasted_iota(jnp.int32, (MARGIN, 1), 0) < s0
        gp_ref[head, :] = jnp.where(
            from_prev, gp_prev[...].astype(F32), gp_ref[head, :].astype(F32)
        ).astype(BF16)
        act_ref[head, :] = jnp.where(
            from_prev, act_prev[...].astype(F32), act_ref[head, :].astype(F32)
        ).astype(BF16)

    mine = lax.axis_index("mp")
    for out, (start, size, picks) in zip(outs, halves):
        for j, pick in enumerate(picks):
            at = pl.ds(pl.multiple_of(pick(mine) * ch, ch), ch)
            out[:, j * ch : (j + 1) * ch] = lax.dot_general(
                gp_ref[start : start + size, :], w_ref[at, :], NT, preferred_element_type=F32
            ).astype(out.dtype)

    if last:
        taps_grad = jnp.dot(
            back_table_ref[...], acc[: FREQ + 8, :],
            precision=lax.Precision.HIGHEST, preferred_element_type=F32,
        )
        sum_ref[:TAPS, :] = taps_grad
        sum_ref[TAPS:, :] = acc[FREQ + 8 : FREQ + 9, :]
    else:
        sum_ref[...] = acc[...]


def chunk_call(first, rows, halves, prev, lengths, frames, grad_out, w_flat, w_out, taps, bias, consts):
    total, width = frames.shape
    ch = w_out.shape[0]
    last = first + rows == total
    load = rows if last else rows + MARGIN
    blocks = next(n for n in range(-(-load // 480), load) if load % (16 * n) == 0)
    vm = pl.BlockSpec(memory_space=pltpu.VMEM)
    hbm = pl.BlockSpec(memory_space=pl.ANY)
    sm = pl.BlockSpec(memory_space=pltpu.SMEM)
    operands = [lengths, frames, grad_out, w_flat, w_out, taps, bias, *consts]
    specs = [sm, hbm, hbm] + [vm] * 8
    if first:
        operands += prev
        specs += [hbm, hbm, vm]

    def body(*refs):
        chunk_kernel(first, rows, load, blocks, last, [h[:3] for h in halves], *refs)

    out_shape = [
        jax.ShapeDtypeStruct((load, 2 * ch), BF16),
        jax.ShapeDtypeStruct((load, ch), BF16),
        jax.ShapeDtypeStruct((TAPS + 1 if last else FREQ + 16, ch), F32),
    ] + [jax.ShapeDtypeStruct((size, len(picks) * ch), dtype) for _, size, picks, dtype in halves]
    return pl.pallas_call(
        body,
        out_shape=out_shape,
        in_specs=specs,
        out_specs=[vm] * len(out_shape),
        scratch_shapes=[
            pltpu.VMEM((load, width), BF16),
            pltpu.VMEM((load, width), BF16),
            pltpu.VMEM((load, ch), F32),
            pltpu.VMEM((load + WIN, ch), F32),
            pltpu.VMEM((load, ch), F32),
            pltpu.VMEM((load + WIN, ch), F32),
            pltpu.VMEM((load + WIN, ch), F32),
            pltpu.VMEM((SEGS + GROUP, FREQ, ch), F32),
            pltpu.VMEM((FREQ + 8, ch), F32),
            pltpu.VMEM((FREQ + 16, ch), F32),
            pltpu.SemaphoreType.DMA((blocks,)),
            pltpu.SemaphoreType.DMA((blocks,)),
        ] + ([
            pltpu.VMEM((MARGIN, 2 * ch), BF16),
            pltpu.VMEM((MARGIN, ch), BF16),
            pltpu.SemaphoreType.DMA((2,)),
        ] if first else []),
        compiler_params=pltpu.CompilerParams(vmem_limit_bytes=40 * MIB),
        cost_estimate=pl.CostEstimate(flops=2 * 10**10, bytes_accessed=2 * 10**7, transcendentals=0),
        name="chunk%d" % first,
    )(*operands)


def zero_sum_kernel(keep0, near0, far0, back0, after, held_ref):
    held_ref[...] = (
        keep0[...] + near0[...].astype(F32) + far0[...].astype(F32) + back0[...].astype(F32)
    ).astype(BF16)


def pass_kernel(keep_a, keep_b, first_a, first_b, out_a, out_b):
    out_a[...] = (keep_a[...] + first_a[...].astype(F32)).astype(BF16)
    out_b[...] = (keep_b[...] + first_b[...].astype(F32)).astype(BF16)


def pass_call(keep_a, keep_b, first_a, first_b):
    half, ch = keep_a.shape[0], keep_a.shape[1] // 2
    out = jax.ShapeDtypeStruct((half, ch), BF16)
    return pl.pallas_call(
        pass_kernel,
        grid=(1,),
        out_shape=(out, out),
        in_specs=[pl.BlockSpec((half, ch), lambda i: (0, 1))] * 4,
        out_specs=[pl.BlockSpec((half, ch), lambda i: (0, 0))] * 2,
        compiler_params=pltpu.CompilerParams(vmem_limit_bytes=16 * MIB),
        cost_estimate=TINY,
        name="pass",
    )(keep_a, keep_b, first_a, first_b)


def pick_kernel(
    len_ref, owner_ref, held0, keep_a, keep_b, first_a, first_b, last_a, last_b, out_ref, held
):
    rows0, ch = held0.shape
    half = last_a.shape[0]
    rows = rows0 + 2 * half
    held[pl.ds(0, rows0), :] = held0[...]
    for at, keep, one, two in ((rows0, keep_a, first_a, last_a), (rows0 + half, keep_b, first_b, last_b)):
        held[pl.ds(at, half), :] = (keep[...] + one[...].astype(F32) + two[...].astype(F32)).astype(BF16)
    held[pl.ds(rows, MARGIN), :] = jnp.zeros((MARGIN, ch), BF16)
    row = lax.broadcasted_iota(jnp.int32, (MAXLEN, MARGIN), 0)
    lane = lax.broadcasted_iota(jnp.int32, (MAXLEN, MARGIN), 1)

    def pick(i, start):
        for j in range(PICKS):
            k = i * PICKS + j
            length = len_ref[0, k]
            base, off = aligned(start, 16)
            hot = jnp.where((lane == row + off) & (row < length), 1.0, 0.0).astype(BF16)
            out_ref[owner_ref[0, k]] = jnp.dot(
                hot, held[pl.ds(base, MARGIN), :], preferred_element_type=F32
            ).astype(BF16)
            start = start + length
        return start

    lax.fori_loop(0, SEGS // PICKS, pick, jnp.int32(0))


def pick_call(lengths, owners, held0, keep_a, keep_b, first_a, first_b, last_a, last_b):
    rows0, ch = held0.shape
    half = last_a.shape[0]
    sm = pl.BlockSpec(memory_space=pltpu.SMEM)
    part = pl.BlockSpec((half, ch), lambda i: (0, 0))
    return pl.pallas_call(
        pick_kernel,
        grid=(1,),
        out_shape=jax.ShapeDtypeStruct((SEGS, MAXLEN, ch), BF16),
        in_specs=[sm, sm, pl.BlockSpec((rows0, ch), lambda i: (0, 0))] + [part] * 6,
        out_specs=pl.BlockSpec((SEGS, MAXLEN, ch), lambda i: (0, 0, 0)),
        scratch_shapes=[pltpu.VMEM((rows0 + 2 * half + MARGIN, ch), BF16)],
        compiler_params=pltpu.CompilerParams(vmem_limit_bytes=24 * MIB),
        cost_estimate=TINY,
        name="pick",
    )(lengths, owners, held0, keep_a, keep_b, first_a, first_b, last_a, last_b)


def order_kernel(slot_ref, src, dst, done_ref, sem):
    def copy(u):
        return pltpu.make_async_copy(src.at[slot_ref[0, u]], dst.at[u], sem.at[u])

    for u in range(SEGS):
        copy(u).start()
    for u in range(SEGS):
        copy(u).wait()
    done_ref[...] = jnp.zeros_like(done_ref)


def order_call(slots, received):
    return pl.pallas_call(
        order_kernel,
        out_shape=(
            jax.ShapeDtypeStruct(received.shape, received.dtype),
            jax.ShapeDtypeStruct((8, 128), F32),
        ),
        in_specs=[pl.BlockSpec(memory_space=pltpu.SMEM), pl.BlockSpec(memory_space=pltpu.VMEM)],
        out_specs=(pl.BlockSpec(memory_space=pl.ANY), pl.BlockSpec(memory_space=pltpu.VMEM)),
        scratch_shapes=[pltpu.SemaphoreType.DMA((SEGS,))],
        compiler_params=pltpu.CompilerParams(vmem_limit_bytes=16 * MIB),
        cost_estimate=TINY,
        name="order",
    )(slots, received)


COLS = 4
PARTS = 1


def weight_kernel(
    deep, frames_hbm, gout_hbm, gp0_hbm, gp1_hbm, act0_hbm, act1_hbm, keep_ref, send_ref,
    fr, go, gp, act, held, f_sem, g_sem, p_sem,
):
    core = lax.rem(lax.axis_index("dp"), 2)
    total, width = frames_hbm.shape
    cols = width // COLS
    rows1 = gp1_hbm.shape[0]
    rows0 = total - rows1
    wide = gp.shape[1]

    def read(hbm, vmem, sem):
        step = total // PARTS
        return [
            pltpu.make_async_copy(hbm.at[pl.ds(i * step, step)], vmem.at[pl.ds(i * step, step)], sem.at[i])
            for i in range(PARTS)
        ]

    def pair(one, two, out, at):
        return [
            pltpu.make_async_copy(one.at[pl.ds(0, rows0)], out.at[pl.ds(0, rows0)], p_sem.at[at]),
            pltpu.make_async_copy(two, out.at[pl.ds(rows0, rows1)], p_sem.at[at + 1]),
        ]

    first = pair(act0_hbm, act1_hbm, act, 0) + read(gout_hbm, go, g_sem)
    second = pair(gp0_hbm, gp1_hbm, gp, 2) + read(frames_hbm, fr, f_sem)
    for copy in first + second:
        copy.start()
    pairs = cols // (2 * deep)
    step = total // PARTS

    def share(j, at):
        for i in range(pairs):
            own = pl.ds(pl.multiple_of(j * cols + (2 * i + core) * deep, 16), deep)
            other = pl.ds(pl.multiple_of(j * cols + (2 * i + 1 - core) * deep, 16), deep)
            keep_ref[j * pairs + i, :, at] = held[own, at].astype(BF16)
            send_ref[j * pairs + i, :, at] = held[other, at].astype(BF16)

    out_cols, in_cols = slice(wide, None), slice(0, wide)
    for copy in first[:2]:
        copy.wait()
    for p in range(PARTS):
        first[2 + p].wait()
        rows = slice(p * step, (p + 1) * step)
        for j in range(COLS):
            here = slice(j * cols, (j + 1) * cols)
            term = lax.dot_general(go[rows, here], act[rows, :], TN, preferred_element_type=F32)
            held[here, out_cols] = term if p == 0 else held[here, out_cols] + term
    for copy in second:
        copy.wait()
    for j in range(COLS):
        here = slice(j * cols, (j + 1) * cols)
        held[here, in_cols] = lax.dot_general(fr[:, here], gp[...], TN, preferred_element_type=F32)
        share(j, out_cols)
        share(j, in_cols)


def weight_call(deep, frames, grad_out, gp0, gp1, act0, act1):
    total, width = frames.shape
    ch = act0.shape[1]
    pairs = width // (2 * deep)
    vm = pl.BlockSpec(memory_space=pltpu.VMEM)
    return pl.pallas_call(
        lambda *refs: weight_kernel(deep, *refs),
        out_shape=(
            jax.ShapeDtypeStruct((pairs, deep, 3 * ch), BF16),
            jax.ShapeDtypeStruct((pairs, deep, 3 * ch), BF16),
        ),
        in_specs=[pl.BlockSpec(memory_space=pl.ANY)] * 6,
        out_specs=(vm, vm),
        scratch_shapes=[
            pltpu.VMEM((total, width), BF16),
            pltpu.VMEM((total, width), BF16),
            pltpu.VMEM((total, 2 * ch), BF16),
            pltpu.VMEM((total, ch), BF16),
            pltpu.VMEM((width, 3 * ch), F32),
            pltpu.SemaphoreType.DMA((PARTS,)),
            pltpu.SemaphoreType.DMA((PARTS,)),
            pltpu.SemaphoreType.DMA((4,)),
        ],
        compiler_params=pltpu.CompilerParams(vmem_limit_bytes=40 * MIB),
        cost_estimate=pl.CostEstimate(flops=11 * 10**9, bytes_accessed=2 * 10**7, transcendentals=0),
        name="weight",
    )(frames, grad_out, gp0, gp1, act0, act1)


CUT = 640


def put_small(out, at, x):
    taps, ch = x.shape
    high = x.astype(BF16)
    for j, part in enumerate((high, (x - high.astype(F32)).astype(BF16))):
        out[at + j] = jnp.zeros(out.shape[1:], out.dtype)
        out[at + j, :taps, :ch] = part


def get_small(ref, at, shape):
    taps, ch = shape
    return ref[at, :taps, :ch].astype(F32) + ref[at + 1, :taps, :ch].astype(F32)


def places():
    dp = lax.axis_index("dp")
    return lax.div(dp, 8), lax.rem(lax.div(dp, 2), 4)


def near(v):
    return v ^ 1


def far(v):
    return 3 - v


def both_ways():
    dp = lax.axis_index("dp")
    x, y = lax.div(dp, 8), lax.rem(lax.div(dp, 2), 4)
    return (slice(0, CUT), x, y, True), (slice(CUT, None), y, x, False)


def core_sum_kernel(keep, got, small, small_got, *outs):
    small_total = small[...] + small_got[...]
    outs[4][...] = small_total
    for i, (cols, a, b, x_first) in enumerate(both_ways()):
        for j in range(4):
            for where, out, slot in ((a, outs[i], 0), (far(a), outs[i], 4), (near(a), outs[2 + i], 0), (far(near(a)), outs[2 + i], 4)):
                at = where * 4 + j if x_first else j * 4 + where
                total = keep[at, :, cols].astype(F32) + got[at, :, cols].astype(F32)
                out[slot + j] = total.astype(out.dtype)
    put_small(outs[3], 8, small_total)


def half_sum_kernel(own_x, own_y, small, got_x, got_y, *outs):
    small_total = small[...] + get_small(got_y, 8, small.shape)
    outs[4][...] = small_total
    for i, ((cols, a, b, x_first), own, got) in enumerate(zip(both_ways(), (own_x, own_y), (got_x, got_y))):
        for s in range(2):
            for j, where in enumerate((b, far(b))):
                at = 4 * s + where
                outs[i][2 * s + j] = own[at] + got[at].astype(F32)
            for j, where in enumerate((near(b), far(near(b)))):
                at = 4 * s + where
                outs[2 + i][2 * s + j] = (own[at] + got[at].astype(F32)).astype(BF16)
    put_small(outs[3], 4, small_total)


def square_sum_kernel(own_x, own_y, small, got_x, got_y, own_ref, small_out, *outs):
    taps, ch = small.shape
    small_total = small[...] + get_small(got_y, 4, small.shape)
    small_out[...] = small_total
    high = small_total.astype(BF16)
    low = (small_total - high.astype(F32)).astype(BF16)
    for out, at_x, at_y in ((own_ref, 0, 0), (outs[0], 2, 1), (outs[1], 1, 2), (outs[2], 3, 3)):
        out[:, :CUT] = (own_x[at_x] + got_x[at_x].astype(F32)).astype(out.dtype)
        out[:, CUT : 3 * ch] = (own_y[at_y] + got_y[at_y].astype(F32)).astype(out.dtype)
    for out in outs:
        out[:, 3 * ch :] = jnp.zeros((out.shape[0], 2 * ch), BF16)
        out[:taps, 3 * ch : 4 * ch] = high
        out[:taps, 4 * ch :] = low


def last_sum_kernel(scale, own, small, r1, r2, r3, after, w_in_out, w_out_out, kernel_out, bias_out):
    taps, ch = small.shape
    total, small_total = own[...], small[...]
    for r in (r1, r2, r3):
        total = total + r[:, : 3 * ch].astype(F32)
        small_total = small_total + r[:taps, 3 * ch : 4 * ch].astype(F32) + r[:taps, 4 * ch :].astype(F32)
    total, small_total = total * scale, small_total * scale
    w_in_out[:, 0, :] = total[:, :ch]
    w_in_out[:, 1, :] = total[:, ch : 2 * ch]
    w_out_out[...] = total[:, 2 * ch :]
    kernel_out[...] = small_total[:TAPS]
    bias_out[...] = small_total[TAPS:].reshape(ch)


def sum_call(kernel, name, cost, out_shape, *operands, after=()):
    vm = pl.BlockSpec(memory_space=pltpu.VMEM)
    return pl.pallas_call(
        kernel,
        out_shape=out_shape,
        in_specs=[vm] * len(operands) + [pl.BlockSpec(memory_space=pl.ANY)] * len(after),
        out_specs=[vm] * len(out_shape),
        compiler_params=pltpu.CompilerParams(vmem_limit_bytes=24 * MIB),
        cost_estimate=cost,
        name=name,
    )(*operands, *after)


def halves(n, deep, wide, small):
    return [
        jax.ShapeDtypeStruct((n, deep, CUT), F32),
        jax.ShapeDtypeStruct((n, deep, wide - CUT), F32),
        jax.ShapeDtypeStruct((n, deep, CUT), BF16),
        jax.ShapeDtypeStruct((n + 2, deep, wide - CUT), BF16),
        jax.ShapeDtypeStruct(small.shape, F32),
    ]


def move(array, fx=None, fy=None):
    def to(i):
        x, y, c = i // 8, i // 2 % 4, i % 2
        if fx is None and fy is None:
            c ^= 1
        return ((fx(x) if fx else x) * 4 + (fy(y) if fy else y)) * 2 + c

    return lax.ppermute(array, "dp", [(i, to(i)) for i in range(lax.axis_size("dp"))])


def together(live, stage, *operands):
    shapes = jax.eval_shape(stage, *operands)

    def never(*_):
        return jax.tree.map(lambda s: jnp.zeros(s.shape, s.dtype), shapes)

    return lax.cond(live, stage, never, *operands)


def until_owners(
    frames, grad_out, w_in, conv_kernel, conv_bias, w_out, seg_lengths, seg_owner
):
    count_dev = lax.axis_size("dp")
    rows, width = frames.shape
    ch = w_out.shape[0]
    scale = 1.0 / math.sqrt(rows * count_dev)
    deep = width // count_dev
    w_flat = w_in.reshape(width, 2 * ch)
    consts = tables()
    shared = (seg_lengths, frames, grad_out, w_flat, w_out, conv_kernel, conv_bias, consts)
    quarter = (rows - ROWS0) // 2

    def turn(d):
        return lambda m: (m + d) % 4

    def mine(m):
        return m

    def other(m):
        return far(near(m))

    gp0, act0, sum0, keep0, near0, far0, back0 = chunk_call(
        0, ROWS0,
        [(0, ROWS0, [turn(d)], F32 if d == 0 else BF16) for d in range(4)],
        None, *shared,
    )

    def ring(d):
        return [(i, (i + d) % 4) for i in range(4)]

    live = seg_lengths[0, 0] > 0

    def zeroth_stage(near0, far0, back0, gp0, act0, sum0, *shared):
        shared = shared[:7] + (shared[7:],)
        return (
            lax.ppermute(near0, "mp", ring(1)),
            lax.ppermute(far0, "mp", ring(2)),
            lax.ppermute(back0, "mp", ring(3)),
            *chunk_call(
                ROWS0, rows - ROWS0,
                [
                    (0, quarter, [near, other], BF16),
                    (quarter, quarter, [far, other], BF16),
                    (0, quarter, [mine, far], F32),
                    (quarter, quarter, [mine, near], F32),
                ],
                (gp0, act0, sum0), *shared,
            ),
        )

    near0, far0, back0, gp1, act1, small, send_a, send_b, keep_a, keep_b = zeroth_stage(
        near0, far0, back0, gp0, act0, sum0, *shared[:7], *consts
    )
    pair = [(i, i ^ 1) for i in range(4)]
    cross = [(i, 3 - i) for i in range(4)]
    first_a = lax.ppermute(send_a, "mp", pair)
    first_b = lax.ppermute(send_b, "mp", cross)
    wide = 3 * ch

    def weight_stage(frames, grad_out, gp0, gp1, act0, act1, small, keep0, near0, far0, back0):
        small_got = move(small)
        keep, send = weight_call(deep, frames, grad_out, gp0, gp1, act0, act1)
        got = move(send)
        (held0,) = sum_call(
            zero_sum_kernel, "zero_sum", TINY, [jax.ShapeDtypeStruct(keep0.shape, BF16)],
            keep0, near0, far0, back0, after=(keep,),
        )
        sums = sum_call(
            core_sum_kernel, "core_sum", TINY, halves(8, deep, wide, small), keep, got, small, small_got
        )
        return held0, *sums

    def last_stage(send_a, send_b):
        return lax.ppermute(send_a, "mp", cross), lax.ppermute(send_b, "mp", pair)

    def first_stage(send_a, send_b, keep_a, keep_b, *operands):
        first_a = lax.ppermute(send_a, "mp", pair)
        first_b = lax.ppermute(send_b, "mp", cross)
        held0, own_x, own_y, send_x, send_y, small = together(live, weight_stage, *operands)
        got_x, got_y = move(send_x, fx=near), move(send_y, fy=near)
        send_a, send_b = pass_call(keep_a, keep_b, first_a, first_b)
        last_a, last_b = last_stage(send_a, send_b)
        return first_a, first_b, held0, own_x, own_y, small, got_x, got_y, last_a, last_b

    def third_stage(send_x, send_y, *operands):
        got_x, got_y = move(send_x, fy=near), move(send_y, fx=near)
        return got_x, got_y, pick_call(*operands)

    first_a, first_b, held0, own_x, own_y, small, got_x, got_y, last_a, last_b = first_stage(
        send_a, send_b, keep_a, keep_b,
        frames, grad_out, gp0, gp1, act0, act1, small, keep0, near0, far0, back0,
    )
    own_x, own_y, send_x, send_y, small = sum_call(
        half_sum_kernel, "half_sum", TINY, halves(4, deep, wide, small), own_x, own_y, small, got_x, got_y
    )
    got_x, got_y, outgoing = third_stage(
        send_x, send_y,
        seg_lengths, seg_owner, held0, keep_a, keep_b, first_a, first_b, last_a, last_b,
    )
    return outgoing, own_x, own_y, small, got_x, got_y


def on_device(
    frames, grad_out, w_in, conv_kernel, conv_bias, w_out, seg_lengths, seg_owner, slot_device
):
    rows, width = frames.shape
    ch = w_out.shape[0]
    count_dev = lax.axis_size("dp")
    scale = 1.0 / math.sqrt(rows * count_dev)
    deep, wide = width // count_dev, 3 * ch
    outgoing, own_x, own_y, small, got_x, got_y = together(
        seg_lengths[0, 0] > 0, until_owners,
        frames, grad_out, w_in, conv_kernel, conv_bias, w_out, seg_lengths, seg_owner,
    )
    received = lax.all_to_all(outgoing, "dp", split_axis=0, concat_axis=0, tiled=True)
    dx_frames, done = order_call(slot_device, received)
    own, small, *sends = sum_call(
        square_sum_kernel, "square_sum", TINY,
        [jax.ShapeDtypeStruct((deep, wide), F32), jax.ShapeDtypeStruct(small.shape, F32)]
        + [jax.ShapeDtypeStruct((deep, wide + 2 * ch), BF16)] * 3,
        own_x, own_y, small, got_x, got_y,
    )
    grad_w_in, grad_w_out, grad_kernel, grad_bias = sum_call(
        lambda *refs: last_sum_kernel(scale, *refs), "last_sum", TINY,
        [
            jax.ShapeDtypeStruct((deep, 2, ch), F32),
            jax.ShapeDtypeStruct((deep, ch), F32),
            jax.ShapeDtypeStruct((TAPS, ch), F32),
            jax.ShapeDtypeStruct((ch,), F32),
        ],
        own, small, move(sends[2], fx=far, fy=far), move(sends[0], fx=far), move(sends[1], fy=far),
        after=(done,),
    )
    return dx_frames, grad_w_in, grad_w_out.T, grad_kernel, grad_bias


def solution(mesh):
    return jax.shard_map(
        on_device,
        mesh=mesh,
        in_specs=(
            P("dp", None),
            P("dp", None),
            P(None, None, "mp"),
            P(None, "mp"),
            P("mp"),
            P("mp", None),
            P("dp", None),
            P("dp", None),
            P("dp", None),
        ),
        out_specs=(P("dp", None, "mp"), P("dp", None, "mp"), P("mp", "dp"), P(None, "mp"), P("mp")),
        check_vma=False,
    )
```
